32 devices in a mesh: head: 4 (over y, core), tok: 8 (over z, x).
Axes of the slice: x: 2, y: 2, z: 4, core: 2. Of those that a mesh axis runs over, the one named last changes fastest.
Arguments:
- hires_tokens: bfloat16 [32768, 1024], P('tok'), may hold values from -6 to 6
- lowres_tokens: bfloat16 [2048, 1024], P('tok'), may hold values from -6 to 6
- norm_gain: float32 [1024], replicated, may hold values from 0.1 to 1.9
- w_cross_q: bfloat16 [1024, 1024], P(None, 'head'), may hold values from -0.1875 to 0.1875
- w_low_kv: bfloat16 [1024, 2, 1024], P(None, None, 'head'), may hold values from -0.1875 to 0.1875
- w_view_qkv: bfloat16 [1024, 3, 1024], P(None, None, 'head'), may hold values from -0.1875 to 0.1875
- w_out: bfloat16 [2, 1024, 1024], P(None, 'head'), may hold values from -0.125 to 0.125
- block_lists: int32 [256, 8], P('tok'), may hold values from 0 to 15, as said below
- block_counts: int32 [256], P('tok'), may hold values from 1 to 8, as said below
Outputs:
- layer_out: bfloat16 [32768, 1024], P('tok', 'head')
The draws below stay inside these ranges and needn't reach their ends.
Inputs may be any that keep to these rules, and one draw needn't show every extreme that they name: `block_lists`: each row names 8 distinct low-resolution blocks; only the first block_counts entries of a row are used. `block_counts`: in every draw there is at least one index of tok all of whose query blocks use all 8 entries; query blocks of the other indices may use any count from 1 to 8.
All inputs are finite; a program needn't handle non-finite values.
Results may differ from the reference program's by a relative error of at most 0.009.
Values may be sent and summed in bfloat16 or wider, within the bound.
No kernel may reach another device: no remote copies, remote signals or barrier semaphores. Data moves between devices by JAX's collectives and lax.ppermute only.
A program may use at most 128 MiB of HBM per device.

```python
import math
import jax
import jax.numpy as jnp
from jax import lax

D = 1024
HEADS = 8
HD = 128
VIEWS = 8
BLOCK = 128
MAXB = 8
TOK_DEV = 4096
TOKENS = 32768
PIX = 4096
LOWTOK = 2048
LOWBLK = 16
QBLK = 256
N_HEAD = 4


def draw_block_lists(key, part):
    row_keys = jax.random.split(jax.random.fold_in(key, 11), QBLK)

    def one_row(row_key):
        return jax.random.permutation(row_key, LOWBLK)[:MAXB]
    return jax.vmap(one_row)(row_keys).astype(jnp.int32)


def draw_block_counts(key, part):
    per_dev = TOK_DEV // BLOCK
    devices = QBLK // per_dev
    key_level, key_draw, key_full = jax.random.split(jax.random.fold_in(key, 23), 3)
    dev_level = jax.random.randint(key_level, (devices, 1), 1, MAXB + 1)
    raw_draw = jax.random.randint(key_draw, (devices, per_dev), 0, 1 << 20)
    counts = 1 + raw_draw % dev_level
    full_dev = jax.random.randint(key_full, (), 0, devices)
    counts = jnp.where(jnp.arange(devices)[:, None] == full_dev, MAXB, counts)
    return counts.reshape(QBLK).astype(jnp.int32)


def block_scale(rng, extent, shards, low, top_value):
    factor_of = 1.0
    for position, parts in shards:
        draws = jax.random.uniform(jax.random.fold_in(jax.random.fold_in(rng, 6), position), (parts,), jnp.float32, low / len(shards), top_value / len(shards))
        factor_of = factor_of * jnp.repeat(jnp.exp(draws), extent[position] // parts).reshape((-1,) + (1,) * (len(extent) - 1 - position))
    return factor_of


def normal_values(stream_key, extent, width, reach, shards=(), held_as=jnp.bfloat16):
    entries = jax.random.normal(stream_key, extent, jnp.float32) * width
    if len(shards) > 0:
        entries = block_scale(stream_key, extent, shards, -0.22, 0.18) * entries
    return jnp.clip(entries, min=-reach, max=reach).astype(held_as)


def setup_inputs(seed: int = 0) -> dict:
    key_of = jax.random.split(jax.random.key(seed), 10)
    hires_tokens = normal_values(key_of[0], (TOKENS, D), 1.0, 6.0, ((0, 8),))
    lowres_tokens = normal_values(key_of[1], (LOWTOK, D), 1.0, 6.0, ((0, 8),))
    norm_gain = jnp.clip(1.0 + 0.18 * jax.random.normal(key_of[2], (D,), jnp.float32), 0.1, 1.9)
    w_cross_q = normal_values(key_of[3], (D, D), D ** -0.5, 0.1875, ((1, 4),))
    w_low_kv = normal_values(key_of[4], (D, 2, D), D ** -0.5, 0.1875, ((2, 4),))
    w_view_qkv = normal_values(key_of[5], (D, 3, D), D ** -0.5, 0.1875, ((2, 4),))
    w_out = normal_values(key_of[6], (2, D, D), (2 * D) ** -0.5, 0.125, ((1, 4),))
    block_lists = draw_block_lists(jax.random.fold_in(key_of[9], 71), 0)
    block_counts = draw_block_counts(jax.random.fold_in(key_of[9], 71), 0)
    return dict(hires_tokens=hires_tokens, lowres_tokens=lowres_tokens, norm_gain=norm_gain, w_cross_q=w_cross_q, w_low_kv=w_low_kv, w_view_qkv=w_view_qkv, w_out=w_out, block_lists=block_lists, block_counts=block_counts)


def rms_rows(row_block, norm_gain):
    values = row_block.astype(jnp.float32)
    factor = lax.rsqrt(lax.optimization_barrier(jnp.mean(values * values, axis=-1, keepdims=True)) + 1e-06)
    return (values * factor * norm_gain.astype(jnp.float32)).astype(jnp.bfloat16)

def masked_softmax(scores, is_valid):
    exponent = jnp.where(is_valid, jnp.exp(scores), jnp.zeros_like(scores))
    return (exponent / lax.optimization_barrier(jnp.sum(exponent, axis=-1, keepdims=True))).astype(jnp.bfloat16)

def reference(hires_tokens, lowres_tokens, norm_gain, w_cross_q, w_low_kv, w_view_qkv, w_out, block_lists, block_counts):
    normed = rms_rows(hires_tokens, norm_gain)
    low_normed = rms_rows(lowres_tokens, norm_gain)
    cross_query = jnp.dot(normed, w_cross_q, preferred_element_type=jnp.float32).astype(jnp.bfloat16)
    low_kv = jnp.dot(low_normed, w_low_kv.reshape(D, 2 * D), preferred_element_type=jnp.float32).astype(jnp.bfloat16)
    low_blocks = low_kv.reshape(LOWBLK, BLOCK, 2, HEADS, HD)
    q_blocks = cross_query.reshape(QBLK, BLOCK, HEADS, HD)
    slot_of_key = jnp.arange(MAXB * BLOCK, dtype=jnp.int32) // BLOCK

    def attend(inputs):
        queries, block_ids, live_count = inputs
        picked = low_blocks[block_ids].reshape(MAXB * BLOCK, 2, HEADS, HD).astype(jnp.float32)
        scores = jnp.einsum('qhe,khe->hqk', queries.astype(jnp.float32), picked[:, 0]) / math.sqrt(HD)
        weights = masked_softmax(scores, (slot_of_key < live_count)[None, None, :])
        mixed_out = jnp.einsum('hqk,khe->qhe', weights.astype(jnp.float32), picked[:, 1])
        return mixed_out.astype(jnp.bfloat16)
    cross_out = lax.map(attend, (q_blocks, block_lists, block_counts)).reshape(TOKENS, D)
    view_qkv = jnp.dot(normed, w_view_qkv.reshape(D, 3 * D), preferred_element_type=jnp.float32).astype(jnp.bfloat16)
    view_qkv = view_qkv.reshape(VIEWS, PIX, 3, HEADS, HD).astype(jnp.float32)
    scores = jnp.einsum('vphe,uphe->phvu', view_qkv[:, :, 0], view_qkv[:, :, 1]) / math.sqrt(HD)
    weights = masked_softmax(scores, True)
    view_out = jnp.einsum('phvu,uphe->vphe', weights.astype(jnp.float32), view_qkv[:, :, 2])
    view_out = view_out.astype(jnp.bfloat16).reshape(TOKENS, D)
    group_cols = D // N_HEAD
    total_sum = jnp.zeros((TOKENS, D), jnp.float32)
    for group_index in range(N_HEAD):
        lower = group_index * group_cols
        upper = lower + group_cols
        group_term = jnp.dot(cross_out[:, lower:upper], w_out[0, lower:upper], preferred_element_type=jnp.float32)
        group_term = group_term + jnp.dot(view_out[:, lower:upper], w_out[1, lower:upper], preferred_element_type=jnp.float32)
        rounded = lax.optimization_barrier(group_term.astype(jnp.bfloat16))
        total_sum = total_sum + rounded.astype(jnp.float32)
    return (hires_tokens.astype(jnp.float32) + total_sum).astype(jnp.bfloat16)
```

```python
import functools
import math

import jax
import jax.numpy as jnp
from jax import lax
from jax.experimental import pallas as pl
from jax.experimental.pallas import tpu as pltpu
from jax.sharding import PartitionSpec as P

HD = 128
VIEWS = 8
BLOCK = 128
LOG2_SCALE = math.log2(math.e) / math.sqrt(HD)
VMEM_BYTES = 48 * 1024 * 1024
CONTRACT_LAST = (((1,), (1,)), ((), ()))


def rms_rows(row_block, norm_gain):
    values = row_block.astype(jnp.float32)
    factor = lax.rsqrt(jnp.mean(values * values, axis=-1, keepdims=True) + 1e-06)
    return (values * factor * norm_gain).astype(jnp.bfloat16)


def f32_dot(left, right):
    return jnp.dot(left, right, preferred_element_type=jnp.float32)


def block_diagonal(tiles):
    rows = []
    for index, tile in enumerate(tiles):
        zero = jnp.zeros_like(tile)
        rows.append(
            jnp.concatenate([tile if k == index else zero for k in range(len(tiles))], axis=1)
        )
    return jnp.concatenate(rows, axis=0)


def cross_kernel(
    lists_ref, counts_ref, tokens_ref, gain_ref, wq_ref, kv_ref, out_ref, vt_ref, q_ref
):
    step = pl.program_id(0)
    rows, cols = out_ref.shape
    heads = cols // HD
    low_rows = kv_ref.shape[0]
    per_step = rows // BLOCK
    listed = lists_ref.shape[1]

    @pl.when(step == 0)
    def _():
        def one_block(block, carry):
            start = pl.multiple_of(block * BLOCK, BLOCK)
            values = kv_ref[pl.ds(start, BLOCK), cols:]
            vt_ref[:, pl.ds(start, BLOCK)] = values.T
            return carry

        lax.fori_loop(0, low_rows // BLOCK, one_block, 0)

    normed = rms_rows(tokens_ref[...], gain_ref[...])
    q_ref[...] = (f32_dot(normed, wq_ref[...]) * LOG2_SCALE).astype(jnp.bfloat16)

    def one_block(local, carry):
        block = step * per_step + local
        row_start = pl.multiple_of(local * BLOCK, BLOCK)
        count = counts_ref[block]
        first = lists_ref[block, 0]
        starts = [
            pl.multiple_of(jnp.where(j < count, lists_ref[block, j], first) * BLOCK, BLOCK)
            for j in range(listed)
        ]
        query = block_diagonal(
            [q_ref[pl.ds(row_start, BLOCK), h * HD : (h + 1) * HD] for h in range(heads)]
        )
        keys = jnp.concatenate([kv_ref[pl.ds(s, BLOCK), :cols] for s in starts], axis=0)
        scores = lax.dot_general(keys, query, CONTRACT_LAST, preferred_element_type=jnp.float32)
        top = jnp.max(scores, axis=0, keepdims=True)
        weights = []
        total = jnp.zeros_like(top)
        for j in range(listed):
            shift = top + jnp.where(j < count, 0.0, 1e30)
            weight = jnp.exp2(scores[j * BLOCK : (j + 1) * BLOCK] - shift)
            total = total + jnp.sum(weight, axis=0, keepdims=True)
            weights.append(weight.astype(jnp.bfloat16))
        values_t = jnp.concatenate([vt_ref[:, pl.ds(s, BLOCK)] for s in starts], axis=1)
        mixed_t = f32_dot(values_t, jnp.concatenate(weights, axis=0)) / total
        for h in range(heads):
            part = slice(h * HD, (h + 1) * HD)
            out_ref[pl.ds(row_start, BLOCK), part] = mixed_t[part, part].T.astype(jnp.bfloat16)
        return carry

    lax.fori_loop(0, per_step, one_block, 0)


def cross_attention(hires_tokens, gain, w_cross_q, all_kv, block_lists, block_counts):
    tok_rows, width = hires_tokens.shape
    cols = w_cross_q.shape[1]
    low_rows = all_kv.shape[0]
    rows = math.gcd(tok_rows, 4 * BLOCK)
    return pl.pallas_call(
        cross_kernel,
        out_shape=jax.ShapeDtypeStruct((tok_rows, cols), jnp.bfloat16),
        grid_spec=pltpu.PrefetchScalarGridSpec(
            num_scalar_prefetch=2,
            grid=(tok_rows // rows,),
            in_specs=[
                pl.BlockSpec((rows, width), lambda i, *_: (i, 0)),
                pl.BlockSpec((1, width), lambda i, *_: (0, 0)),
                pl.BlockSpec((width, cols), lambda i, *_: (0, 0)),
                pl.BlockSpec((low_rows, 2 * cols), lambda i, *_: (0, 0)),
            ],
            out_specs=pl.BlockSpec((rows, cols), lambda i, *_: (i, 0)),
            scratch_shapes=[
                pltpu.VMEM((cols, low_rows), jnp.bfloat16),
                pltpu.VMEM((rows, cols), jnp.bfloat16),
            ],
        ),
        compiler_params=pltpu.CompilerParams(vmem_limit_bytes=VMEM_BYTES),
        cost_estimate=pl.CostEstimate(
            flops=2 * tok_rows * cols * (width + 2 * block_lists.shape[1] * BLOCK * 2),
            bytes_accessed=2 * tok_rows * (width + cols),
            transcendentals=tok_rows * block_lists.shape[1] * BLOCK * (cols // HD),
        ),
        name="cross",
    )(block_lists, block_counts, hires_tokens, gain, w_cross_q, all_kv)


def view_kernel(tokens_ref, gain_ref, w_ref, out_ref, qkv_ref, mixed_ref):
    _, sources, run, width = tokens_ref.shape
    cols = out_ref.shape[-1]
    heads = cols // HD
    rows = sources * run
    pixels = rows // VIEWS
    group = math.gcd(pixels, 32)
    gain = gain_ref[...]
    source_step = max(1, 256 // run)
    for s in range(0, sources, source_step):
        tokens = tokens_ref[0, s : s + source_step].reshape(source_step * run, width)
        projected = f32_dot(rms_rows(tokens, gain), w_ref[...])
        start = s * run
        stop = start + source_step * run
        qkv_ref[start:stop, :cols] = (projected[:, :cols] * LOG2_SCALE).astype(jnp.bfloat16)
        qkv_ref[start:stop, cols:] = projected[:, cols:].astype(jnp.bfloat16)
    size = VIEWS * group
    row_pixel = lax.broadcasted_iota(jnp.int32, (size, size), 0) % group
    col_pixel = lax.broadcasted_iota(jnp.int32, (size, size), 1) % group
    same = row_pixel == col_pixel

    def gathered(first, column):
        part = slice(column, column + HD)
        return jnp.concatenate(
            [qkv_ref[v * pixels + first : v * pixels + first + group, part] for v in range(VIEWS)],
            axis=0,
        )

    for first in range(0, pixels, group):
        for h in range(heads):
            query = gathered(first, h * HD)
            key = gathered(first, cols + h * HD)
            value = gathered(first, 2 * cols + h * HD)
            scores = lax.dot_general(query, key, CONTRACT_LAST, preferred_element_type=jnp.float32)
            scores = jnp.where(same, scores, -1e30)
            weight = jnp.exp2(scores - jnp.max(scores, axis=1, keepdims=True))
            total = jnp.sum(weight, axis=1, keepdims=True)
            mixed = (f32_dot(weight.astype(jnp.bfloat16), value) / total).astype(jnp.bfloat16)
            for v in range(VIEWS):
                mixed_ref[v * pixels + first : v * pixels + first + group, h * HD : (h + 1) * HD] = (
                    mixed[v * group : (v + 1) * group]
                )
    out_ref[:, 0] = mixed_ref[...].reshape(sources, run, cols)


def view_attention(tokens, gain, w_view):
    parts, sources, run, width = tokens.shape
    cols = w_view.shape[1] // 3
    rows = sources * run
    return pl.pallas_call(
        view_kernel,
        out_shape=jax.ShapeDtypeStruct((sources, parts, run, cols), jnp.bfloat16),
        grid=(parts,),
        in_specs=[
            pl.BlockSpec((1, sources, run, width), lambda i: (i, 0, 0, 0)),
            pl.BlockSpec((1, width), lambda i: (0, 0)),
            pl.BlockSpec((width, 3 * cols), lambda i: (0, 0)),
        ],
        out_specs=pl.BlockSpec((sources, 1, run, cols), lambda i: (0, i, 0, 0)),
        scratch_shapes=[
            pltpu.VMEM((rows, 3 * cols), jnp.bfloat16),
            pltpu.VMEM((rows, cols), jnp.bfloat16),
        ],
        compiler_params=pltpu.CompilerParams(vmem_limit_bytes=VMEM_BYTES),
        cost_estimate=pl.CostEstimate(
            flops=2 * parts * rows * cols * (3 * width + 512),
            bytes_accessed=2 * parts * rows * (width + cols),
            transcendentals=parts * rows * 512,
        ),
        name="view",
    )(tokens, gain, w_view)


def out_kernel(cross_ref, view_ref, w_ref, out_ref):
    total = f32_dot(cross_ref[...], w_ref[0]) + f32_dot(view_ref[...], w_ref[1])
    out_ref[...] = total.astype(jnp.bfloat16)


def out_projection(cross_out, view_out, w_out):
    tok_rows, cols = cross_out.shape
    width = w_out.shape[2]
    rows = math.gcd(tok_rows, 512)
    return pl.pallas_call(
        out_kernel,
        out_shape=jax.ShapeDtypeStruct((tok_rows, width), jnp.bfloat16),
        grid=(tok_rows // rows,),
        in_specs=[
            pl.BlockSpec((rows, cols), lambda i: (i, 0)),
            pl.BlockSpec((rows, cols), lambda i: (i, 0)),
            pl.BlockSpec((2, cols, width), lambda i: (0, 0, 0)),
        ],
        out_specs=pl.BlockSpec((rows, width), lambda i: (i, 0)),
        compiler_params=pltpu.CompilerParams(vmem_limit_bytes=VMEM_BYTES),
        cost_estimate=pl.CostEstimate(
            flops=4 * tok_rows * cols * width,
            bytes_accessed=2 * tok_rows * (2 * cols + width),
            transcendentals=0,
        ),
        name="project",
    )(cross_out, view_out, w_out)


def shards(
    n_head,
    n_tok,
    hires_tokens,
    lowres_tokens,
    norm_gain,
    w_cross_q,
    w_low_kv,
    w_view_qkv,
    w_out,
    block_lists,
    block_counts,
):
    tok_rows, width = hires_tokens.shape
    cols = w_cross_q.shape[1]
    run = tok_rows // (n_tok * n_head)
    head_index = lax.axis_index("head")
    gain = norm_gain.reshape(1, width)

    low_kv = f32_dot(
        rms_rows(lowres_tokens, norm_gain), w_low_kv.reshape(width, 2 * cols)
    ).astype(jnp.bfloat16)
    all_kv = lax.all_gather(low_kv, "tok", axis=0, tiled=True)

    to_send = lax.dynamic_index_in_dim(
        hires_tokens.reshape(n_tok, n_head, run, width), head_index, 1, keepdims=False
    )
    arrived = lax.all_to_all(to_send, "tok", split_axis=0, concat_axis=0, tiled=True)
    view_tokens = lax.all_gather(arrived, "head", axis=0, tiled=False)

    cross_out = cross_attention(hires_tokens, gain, w_cross_q, all_kv, block_lists, block_counts)
    mixed = view_attention(view_tokens, gain, w_view_qkv.reshape(width, 3 * cols))
    view_out = lax.all_to_all(
        mixed.reshape(tok_rows, cols), "tok", split_axis=0, concat_axis=0, tiled=True
    )
    partial_value = out_projection(cross_out, view_out, w_out)
    summed = lax.psum_scatter(
        partial_value, "head", scatter_dimension=1, tiled=True
    ).astype(jnp.float32)
    out_cols = summed.shape[1]
    residual = lax.dynamic_slice_in_dim(hires_tokens, head_index * out_cols, out_cols, 1)
    return (residual.astype(jnp.float32) + summed).astype(jnp.bfloat16)


def solution(mesh):
    in_specs = (
        P("tok", None),
        P("tok", None),
        P(),
        P(None, "head"),
        P(None, None, "head"),
        P(None, None, "head"),
        P(None, "head", None),
        P("tok", None),
        P("tok"),
    )
    out_specs = P("tok", "head")
    body = functools.partial(shards, mesh.shape["head"], mesh.shape["tok"])
    return jax.shard_map(body, mesh=mesh, in_specs=in_specs, out_specs=out_specs, check_vma=False)
```

```python
import functools
import math

import jax
import jax.numpy as jnp
from jax import lax
from jax.experimental import pallas as pl
from jax.experimental.pallas import tpu as pltpu
from jax.sharding import PartitionSpec as P

HD = 128
VIEWS = 8
BLOCK = 128
LOG2_SCALE = math.log2(math.e) / math.sqrt(HD)
VMEM_BYTES = 48 * 1024 * 1024
CONTRACT_LAST = (((1,), (1,)), ((), ()))


def rms_rows(row_block, norm_gain):
    values = row_block.astype(jnp.float32)
    factor = lax.rsqrt(jnp.mean(values * values, axis=-1, keepdims=True) + 1e-06)
    return (values * factor * norm_gain).astype(jnp.bfloat16)


def f32_dot(left, right):
    return jnp.dot(left, right, preferred_element_type=jnp.float32)


def block_diagonal(tiles):
    rows = []
    for index, tile in enumerate(tiles):
        zero = jnp.zeros_like(tile)
        rows.append(
            jnp.concatenate([tile if k == index else zero for k in range(len(tiles))], axis=1)
        )
    return jnp.concatenate(rows, axis=0)


def cross_kernel(
    lists_ref, counts_ref, tokens_ref, gain_ref, wq_ref, kv_ref, out_ref, vt_ref, q_ref
):
    step = pl.program_id(0)
    rows, cols = out_ref.shape
    heads = cols // HD
    low_rows = kv_ref.shape[0]
    per_step = rows // BLOCK
    listed = lists_ref.shape[1]

    @pl.when(step == 0)
    def _():
        def one_block(block, carry):
            start = pl.multiple_of(block * BLOCK, BLOCK)
            values = kv_ref[pl.ds(start, BLOCK), cols:]
            vt_ref[:, pl.ds(start, BLOCK)] = values.T
            return carry

        lax.fori_loop(0, low_rows // BLOCK, one_block, 0)

    normed = rms_rows(tokens_ref[...], gain_ref[...])
    q_ref[...] = (f32_dot(normed, wq_ref[...]) * LOG2_SCALE).astype(jnp.bfloat16)

    def one_block(local, carry):
        block = step * per_step + local
        row_start = pl.multiple_of(local * BLOCK, BLOCK)
        count = counts_ref[block]
        first = lists_ref[block, 0]
        starts = [
            pl.multiple_of(jnp.where(j < count, lists_ref[block, j], first) * BLOCK, BLOCK)
            for j in range(listed)
        ]
        query = block_diagonal(
            [q_ref[pl.ds(row_start, BLOCK), h * HD : (h + 1) * HD] for h in range(heads)]
        )
        keys = jnp.concatenate([kv_ref[pl.ds(s, BLOCK), :cols] for s in starts], axis=0)
        scores = lax.dot_general(keys, query, CONTRACT_LAST, preferred_element_type=jnp.float32)
        top = jnp.max(scores, axis=0, keepdims=True)
        weights = []
        total = jnp.zeros_like(top)
        for j in range(listed):
            shift = top + jnp.where(j < count, 0.0, 1e30)
            weight = jnp.exp2(scores[j * BLOCK : (j + 1) * BLOCK] - shift)
            total = total + jnp.sum(weight, axis=0, keepdims=True)
            weights.append(weight.astype(jnp.bfloat16))
        values_t = jnp.concatenate([vt_ref[:, pl.ds(s, BLOCK)] for s in starts], axis=1)
        mixed_t = f32_dot(values_t, jnp.concatenate(weights, axis=0)) / total
        for h in range(heads):
            part = slice(h * HD, (h + 1) * HD)
            out_ref[pl.ds(row_start, BLOCK), part] = mixed_t[part, part].T.astype(jnp.bfloat16)
        return carry

    lax.fori_loop(0, per_step, one_block, 0, unroll=True)


def cross_attention(hires_tokens, gain, w_cross_q, all_kv, block_lists, block_counts):
    tok_rows, width = hires_tokens.shape
    cols = w_cross_q.shape[1]
    low_rows = all_kv.shape[0]
    rows = math.gcd(tok_rows, 4 * BLOCK)
    return pl.pallas_call(
        cross_kernel,
        out_shape=jax.ShapeDtypeStruct((tok_rows, cols), jnp.bfloat16),
        grid_spec=pltpu.PrefetchScalarGridSpec(
            num_scalar_prefetch=2,
            grid=(tok_rows // rows,),
            in_specs=[
                pl.BlockSpec((rows, width), lambda i, *_: (i, 0)),
                pl.BlockSpec((1, width), lambda i, *_: (0, 0)),
                pl.BlockSpec((width, cols), lambda i, *_: (0, 0)),
                pl.BlockSpec((low_rows, 2 * cols), lambda i, *_: (0, 0)),
            ],
            out_specs=pl.BlockSpec((rows, cols), lambda i, *_: (i, 0)),
            scratch_shapes=[
                pltpu.VMEM((cols, low_rows), jnp.bfloat16),
                pltpu.VMEM((rows, cols), jnp.bfloat16),
            ],
        ),
        compiler_params=pltpu.CompilerParams(vmem_limit_bytes=VMEM_BYTES),
        cost_estimate=pl.CostEstimate(
            flops=2 * tok_rows * cols * (width + 2 * block_lists.shape[1] * BLOCK * 2),
            bytes_accessed=2 * tok_rows * (width + cols),
            transcendentals=tok_rows * block_lists.shape[1] * BLOCK * (cols // HD),
        ),
        name="cross",
    )(block_lists, block_counts, hires_tokens, gain, w_cross_q, all_kv)


def view_kernel(tokens_ref, gain_ref, w_ref, out_ref, normed_ref, qkv_ref, mixed_ref):
    sources, run, width = tokens_ref.shape
    cols = out_ref.shape[-1]
    heads = cols // HD
    rows = sources * run
    pixels = rows // VIEWS
    group = math.gcd(pixels, 32)
    tile = math.gcd(rows, 256)

    @pl.when(pl.program_id(0) == 0)
    def _():
        gain = gain_ref[...]
        step = max(1, tile // run)
        for s in range(0, sources, step):
            tokens = tokens_ref[s : s + step].reshape(step * run, width)
            normed_ref[s * run : (s + step) * run] = rms_rows(tokens, gain)

    for start in range(0, rows, tile):
        stop = start + tile
        projected = f32_dot(normed_ref[start:stop], w_ref[0])
        qkv_ref[start:stop, :cols] = (projected[:, :cols] * LOG2_SCALE).astype(jnp.bfloat16)
        qkv_ref[start:stop, cols:] = projected[:, cols:].astype(jnp.bfloat16)
    size = VIEWS * group
    row_pixel = lax.broadcasted_iota(jnp.int32, (size, size), 0) % group
    col_pixel = lax.broadcasted_iota(jnp.int32, (size, size), 1) % group
    same = row_pixel == col_pixel

    def gathered(first, column):
        part = slice(column, column + HD)
        return jnp.concatenate(
            [qkv_ref[v * pixels + first : v * pixels + first + group, part] for v in range(VIEWS)],
            axis=0,
        )

    for first in range(0, pixels, group):
        for h in range(heads):
            query = gathered(first, h * HD)
            key = gathered(first, cols + h * HD)
            value = gathered(first, 2 * cols + h * HD)
            scores = lax.dot_general(query, key, CONTRACT_LAST, preferred_element_type=jnp.float32)
            scores = jnp.where(same, scores, -1e30)
            weight = jnp.exp2(scores - jnp.max(scores, axis=1, keepdims=True))
            total = jnp.sum(weight, axis=1, keepdims=True)
            mixed = (f32_dot(weight.astype(jnp.bfloat16), value) / total).astype(jnp.bfloat16)
            for v in range(VIEWS):
                mixed_ref[v * pixels + first : v * pixels + first + group, h * HD : (h + 1) * HD] = (
                    mixed[v * group : (v + 1) * group]
                )
    out_ref[...] = mixed_ref[...].reshape(sources, run, cols)


def view_attention(tokens, gain, w_view):
    sources, run, width = tokens.shape
    parts = w_view.shape[0]
    cols = w_view.shape[2] // 3
    rows = sources * run
    return pl.pallas_call(
        view_kernel,
        out_shape=jax.ShapeDtypeStruct((sources, run, parts * cols), jnp.bfloat16),
        grid=(parts,),
        in_specs=[
            pl.BlockSpec((sources, run, width), lambda i: (0, 0, 0)),
            pl.BlockSpec((1, width), lambda i: (0, 0)),
            pl.BlockSpec((1, width, 3 * cols), lambda i: (i, 0, 0)),
        ],
        out_specs=pl.BlockSpec((sources, run, cols), lambda i: (0, 0, i)),
        scratch_shapes=[
            pltpu.VMEM((rows, width), jnp.bfloat16),
            pltpu.VMEM((rows, 3 * cols), jnp.bfloat16),
            pltpu.VMEM((rows, cols), jnp.bfloat16),
        ],
        compiler_params=pltpu.CompilerParams(vmem_limit_bytes=VMEM_BYTES),
        cost_estimate=pl.CostEstimate(
            flops=2 * parts * rows * cols * (3 * width + 512),
            bytes_accessed=2 * (2 * rows * width + 3 * parts * width * cols),
            transcendentals=parts * rows * 512,
        ),
        name="view",
    )(tokens, gain, w_view)


def out_kernel(cross_ref, view_ref, tokens_ref, w_ref, out_ref):
    parts, _, cols = cross_ref.shape
    total = tokens_ref[...].astype(jnp.float32)
    for g in range(parts):
        total = total + f32_dot(cross_ref[g], w_ref[g, 0])
        total = total + f32_dot(view_ref[:, g * cols : (g + 1) * cols], w_ref[g, 1])
    for g in range(parts):
        out_ref[g] = total[:, g * cols : (g + 1) * cols].astype(jnp.bfloat16)


def out_projection(cross_out, view_out, tokens, w_out):
    parts, quarter, cols = cross_out.shape
    width = w_out.shape[3]
    rows = math.gcd(quarter, 256)
    return pl.pallas_call(
        out_kernel,
        out_shape=jax.ShapeDtypeStruct((parts, quarter, cols), jnp.bfloat16),
        grid=(quarter // rows,),
        in_specs=[
            pl.BlockSpec((parts, rows, cols), lambda i: (0, i, 0)),
            pl.BlockSpec((rows, width), lambda i: (i, 0)),
            pl.BlockSpec((rows, width), lambda i: (i, 0)),
            pl.BlockSpec((parts, 2, cols, width), lambda i: (0, 0, 0, 0)),
        ],
        out_specs=pl.BlockSpec((parts, rows, cols), lambda i: (0, i, 0)),
        compiler_params=pltpu.CompilerParams(vmem_limit_bytes=VMEM_BYTES),
        cost_estimate=pl.CostEstimate(
            flops=4 * quarter * width * width,
            bytes_accessed=2 * (4 * quarter * width + 2 * width * width),
            transcendentals=0,
        ),
        name="project",
    )(cross_out, view_out, tokens, w_out)


def shards(
    n_head,
    n_tok,
    hires_tokens,
    lowres_tokens,
    norm_gain,
    w_cross_q,
    w_low_kv,
    w_view_qkv,
    w_out,
    block_lists,
    block_counts,
):
    tok_rows, width = hires_tokens.shape
    cols = w_cross_q.shape[1]
    quarter = tok_rows // n_head
    head_index = lax.axis_index("head")
    gain = norm_gain.reshape(1, width)

    own_rows = lax.dynamic_slice_in_dim(hires_tokens, head_index * quarter, quarter, 0)
    low_kv = f32_dot(
        rms_rows(lowres_tokens, norm_gain), w_low_kv.reshape(width, 2 * cols)
    ).astype(jnp.bfloat16)
    w_view = w_view_qkv.reshape(width, 3 * cols)
    own_rows, low_kv, w_view = lax.optimization_barrier((own_rows, low_kv, w_view))

    w_view = lax.all_gather(w_view, "head", axis=0, tiled=False)
    arrived = lax.all_to_all(
        own_rows.reshape(n_tok, quarter // n_tok, width),
        "tok", split_axis=0, concat_axis=0, tiled=True,
    )
    all_kv = lax.all_gather(low_kv, "tok", axis=0, tiled=True)
    w_out = lax.all_gather(w_out, "head", axis=0, tiled=False)

    mixed = view_attention(arrived, gain, w_view)
    view_out = lax.all_to_all(mixed, "tok", split_axis=0, concat_axis=0, tiled=True)

    cross_out = cross_attention(hires_tokens, gain, w_cross_q, all_kv, block_lists, block_counts)
    cross_out = lax.all_to_all(
        cross_out.reshape(n_head, quarter, cols), "head", split_axis=0, concat_axis=0, tiled=True
    )
    layer_out = out_projection(cross_out, view_out.reshape(quarter, width), own_rows, w_out)
    layer_out = lax.all_to_all(layer_out, "head", split_axis=0, concat_axis=0, tiled=True)
    return layer_out.reshape(tok_rows, cols)


def solution(mesh):
    in_specs = (
        P("tok", None),
        P("tok", None),
        P(),
        P(None, "head"),
        P(None, None, "head"),
        P(None, None, "head"),
        P(None, "head", None),
        P("tok", None),
        P("tok"),
    )
    out_specs = P("tok", "head")
    body = functools.partial(shards, mesh.shape["head"], mesh.shape["tok"])
    return jax.shard_map(body, mesh=mesh, in_specs=in_specs, out_specs=out_specs, check_vma=False)
```

```python
import functools
import math

import jax
import jax.numpy as jnp
from jax import lax
from jax.experimental import pallas as pl
from jax.experimental.pallas import tpu as pltpu
from jax.sharding import PartitionSpec as P

HD = 128
VIEWS = 8
BLOCK = 128
LOG2_SCALE = math.log2(math.e) / math.sqrt(HD)
VMEM_BYTES = 60 * 1024 * 1024
CONTRACT_LAST = (((1,), (1,)), ((), ()))


def rms_rows(row_block, norm_gain):
    values = row_block.astype(jnp.float32)
    factor = lax.rsqrt(jnp.mean(values * values, axis=-1, keepdims=True) + 1e-06)
    return (values * factor * norm_gain).astype(jnp.bfloat16)


def f32_dot(left, right):
    return jnp.dot(left, right, preferred_element_type=jnp.float32)


def block_diagonal(tiles):
    rows = []
    for index, tile in enumerate(tiles):
        zero = jnp.zeros_like(tile)
        rows.append(
            jnp.concatenate([tile if k == index else zero for k in range(len(tiles))], axis=1)
        )
    return jnp.concatenate(rows, axis=0)


def ring_place(tok, n_tok):
    half = lax.div(tok, 2)
    return jnp.where(lax.rem(tok, 2) == 0, half, n_tok - 1 - half)


def cross_kernel(lists_ref, counts_ref, tok_ref, tokens_ref, gain_ref, wq_ref, *refs):
    kv_refs = refs[:-4]
    out_ref, k_ref, vt_ref, q_ref = refs[-4:]
    step = pl.program_id(0)
    rows, cols = out_ref.shape
    heads = cols // HD
    per_step = rows // BLOCK
    listed = lists_ref.shape[1]

    @pl.when(step == 0)
    def _():
        n_tok = len(kv_refs)
        for offset, kv_ref in enumerate(kv_refs):
            chunk = kv_ref.shape[0]
            place = lax.rem(ring_place(tok_ref[0], n_tok) + offset, n_tok)
            home = jnp.where(place < (n_tok + 1) // 2, 2 * place, 2 * (n_tok - 1 - place) + 1)
            start = pl.multiple_of(home * chunk, BLOCK)
            k_ref[pl.ds(start, chunk), :] = kv_ref[:, :cols]
            vt_ref[:, pl.ds(start, chunk)] = kv_ref[:, cols:].T

    normed = rms_rows(tokens_ref[...], gain_ref[...])
    q_ref[...] = (f32_dot(normed, wq_ref[...]) * LOG2_SCALE).astype(jnp.bfloat16)

    def one_block(local, carry):
        block = step * per_step + local
        row_start = pl.multiple_of(local * BLOCK, BLOCK)
        count = counts_ref[block]
        first = lists_ref[block, 0]
        starts = [
            pl.multiple_of(jnp.where(j < count, lists_ref[block, j], first) * BLOCK, BLOCK)
            for j in range(listed)
        ]
        query = block_diagonal(
            [q_ref[pl.ds(row_start, BLOCK), h * HD : (h + 1) * HD] for h in range(heads)]
        )
        keys = jnp.concatenate([k_ref[pl.ds(s, BLOCK), :] for s in starts], axis=0)
        scores = lax.dot_general(keys, query, CONTRACT_LAST, preferred_element_type=jnp.float32)
        top = jnp.max(scores, axis=0, keepdims=True)
        weights = []
        total = jnp.zeros_like(top)
        for j in range(listed):
            shift = top + jnp.where(j < count, 0.0, 1e30)
            weight = jnp.exp2(scores[j * BLOCK : (j + 1) * BLOCK] - shift)
            total = total + jnp.sum(weight, axis=0, keepdims=True)
            weights.append(weight.astype(jnp.bfloat16))
        values_t = jnp.concatenate([vt_ref[:, pl.ds(s, BLOCK)] for s in starts], axis=1)
        mixed_t = f32_dot(values_t, jnp.concatenate(weights, axis=0)) / total
        for h in range(heads):
            part = slice(h * HD, (h + 1) * HD)
            out_ref[pl.ds(row_start, BLOCK), part] = mixed_t[part, part].T.astype(jnp.bfloat16)
        return carry

    lax.fori_loop(0, per_step, one_block, 0, unroll=True)


def cross_attention(hires_tokens, gain, w_cross_q, kv_chunks, block_lists, block_counts):
    tok_index = lax.axis_index("tok").reshape(1)
    tok_rows, width = hires_tokens.shape
    cols = w_cross_q.shape[1]
    chunk = kv_chunks[0].shape[0]
    low_rows = chunk * len(kv_chunks)
    rows = math.gcd(tok_rows, 4 * BLOCK)
    return pl.pallas_call(
        cross_kernel,
        out_shape=jax.ShapeDtypeStruct((tok_rows, cols), jnp.bfloat16),
        grid_spec=pltpu.PrefetchScalarGridSpec(
            num_scalar_prefetch=3,
            grid=(tok_rows // rows,),
            in_specs=[
                pl.BlockSpec((rows, width), lambda i, *_: (i, 0)),
                pl.BlockSpec((1, width), lambda i, *_: (0, 0)),
                pl.BlockSpec((width, cols), lambda i, *_: (0, 0)),
            ]
            + [pl.BlockSpec((chunk, 2 * cols), lambda i, *_: (0, 0)) for _ in kv_chunks],
            out_specs=pl.BlockSpec((rows, cols), lambda i, *_: (i, 0)),
            scratch_shapes=[
                pltpu.VMEM((low_rows, cols), jnp.bfloat16),
                pltpu.VMEM((cols, low_rows), jnp.bfloat16),
                pltpu.VMEM((rows, cols), jnp.bfloat16),
            ],
        ),
        compiler_params=pltpu.CompilerParams(vmem_limit_bytes=VMEM_BYTES),
        cost_estimate=pl.CostEstimate(
            flops=2 * tok_rows * cols * (width + 2 * block_lists.shape[1] * BLOCK * 2),
            bytes_accessed=2 * tok_rows * (width + cols),
            transcendentals=tok_rows * block_lists.shape[1] * BLOCK * (cols // HD),
        ),
        name="cross",
    )(block_lists, block_counts, tok_index, hires_tokens, gain, w_cross_q, *kv_chunks)


def view_kernel(tokens_ref, gain_ref, w_ref, wo_ref, out_ref, normed_ref, qkv_ref, mixed_ref):
    sources, run, width = tokens_ref.shape
    parts, _, cols, _ = wo_ref.shape
    part_index = pl.program_id(0)
    heads = cols // HD
    rows = sources * run
    pixels = rows // VIEWS
    group = math.gcd(pixels, 32)
    tile = math.gcd(rows, 256)

    @pl.when(pl.program_id(0) == 0)
    def _():
        gain = gain_ref[...]
        step = max(1, tile // run)
        for s in range(0, sources, step):
            tokens = tokens_ref[s : s + step].reshape(step * run, width)
            normed_ref[s * run : (s + step) * run] = rms_rows(tokens, gain)

    for start in range(0, rows, tile):
        stop = start + tile
        tokens = normed_ref[start:stop]
        for k in range(3):
            projected = f32_dot(tokens, w_ref[0, k])
            if k == 0:
                projected = projected * LOG2_SCALE
            qkv_ref[start:stop, k * cols : (k + 1) * cols] = projected.astype(jnp.bfloat16)
    size = VIEWS * group
    row_pixel = lax.broadcasted_iota(jnp.int32, (size, size), 0) % group
    col_pixel = lax.broadcasted_iota(jnp.int32, (size, size), 1) % group
    same = row_pixel == col_pixel

    def gathered(first, column):
        part = slice(column, column + HD)
        return jnp.concatenate(
            [qkv_ref[v * pixels + first : v * pixels + first + group, part] for v in range(VIEWS)],
            axis=0,
        )

    for first in range(0, pixels, group):
        for h in range(heads):
            query = gathered(first, h * HD)
            key = gathered(first, cols + h * HD)
            value = gathered(first, 2 * cols + h * HD)
            scores = lax.dot_general(query, key, CONTRACT_LAST, preferred_element_type=jnp.float32)
            scores = jnp.where(same, scores, -1e30)
            weight = jnp.exp2(scores - jnp.max(scores, axis=1, keepdims=True))
            total = jnp.sum(weight, axis=1, keepdims=True)
            mixed = (f32_dot(weight.astype(jnp.bfloat16), value) / total).astype(jnp.bfloat16)
            for v in range(VIEWS):
                rows_of = slice(v * pixels + first, v * pixels + first + group)
                mixed_ref[part_index, rows_of, h * HD : (h + 1) * HD] = (
                    mixed[v * group : (v + 1) * group]
                )

    @pl.when(part_index == parts - 1)
    def _():
        step = max(1, tile // run)
        for s in range(0, sources, step):
            rows_of = slice(s * run, (s + step) * run)
            term = f32_dot(mixed_ref[0, rows_of], wo_ref[0, 0])
            for g in range(1, parts):
                term = term + f32_dot(mixed_ref[g, rows_of], wo_ref[g, 0])
            term = term.astype(jnp.bfloat16)
            for g in range(parts):
                out_ref[g, s : s + step] = term[:, g * cols : (g + 1) * cols].reshape(
                    step, run, cols
                )


def view_attention(tokens, gain, w_view, w_out):
    sources, run, width = tokens.shape
    parts = w_view.shape[0]
    cols = w_view.shape[3]
    rows = sources * run
    return pl.pallas_call(
        view_kernel,
        out_shape=jax.ShapeDtypeStruct((parts, sources, run, cols), jnp.bfloat16),
        grid=(parts,),
        in_specs=[
            pl.BlockSpec((sources, run, width), lambda i: (0, 0, 0)),
            pl.BlockSpec((1, width), lambda i: (0, 0)),
            pl.BlockSpec((1, 3, width, cols), lambda i: (i, 0, 0, 0)),
            pl.BlockSpec((parts, 1, cols, width), lambda i: (0, 1, 0, 0)),
        ],
        out_specs=pl.BlockSpec((parts, sources, run, cols), lambda i: (0, 0, 0, 0)),
        scratch_shapes=[
            pltpu.VMEM((rows, width), jnp.bfloat16),
            pltpu.VMEM((rows, 3 * cols), jnp.bfloat16),
            pltpu.VMEM((parts, rows, cols), jnp.bfloat16),
        ],
        compiler_params=pltpu.CompilerParams(vmem_limit_bytes=VMEM_BYTES),
        cost_estimate=pl.CostEstimate(
            flops=2 * rows * (parts * cols * (3 * width + 512) + width * width),
            bytes_accessed=2 * (2 * rows * width + 4 * parts * width * cols),
            transcendentals=parts * rows * 512,
        ),
        name="view",
    )(tokens, gain, w_view, w_out)


def project_kernel(cross_ref, w_ref, out_ref):
    parts, _, cols = cross_ref.shape
    total = f32_dot(cross_ref[0], w_ref[0, 0])
    for g in range(1, parts):
        total = total + f32_dot(cross_ref[g], w_ref[g, 0])
    for g in range(parts):
        out_ref[g] = total[:, g * cols : (g + 1) * cols].astype(jnp.bfloat16)


def cross_projection(cross_out, w_out):
    parts, quarter, cols = cross_out.shape
    width = w_out.shape[3]
    rows = math.gcd(quarter, 256)
    return pl.pallas_call(
        project_kernel,
        out_shape=jax.ShapeDtypeStruct((parts, quarter, cols), jnp.bfloat16),
        grid=(quarter // rows,),
        in_specs=[
            pl.BlockSpec((parts, rows, cols), lambda i: (0, i, 0)),
            pl.BlockSpec((parts, 1, cols, width), lambda i: (0, 0, 0, 0)),
        ],
        out_specs=pl.BlockSpec((parts, rows, cols), lambda i: (0, i, 0)),
        compiler_params=pltpu.CompilerParams(vmem_limit_bytes=VMEM_BYTES),
        cost_estimate=pl.CostEstimate(
            flops=2 * quarter * width * width,
            bytes_accessed=2 * (2 * quarter * width + width * width),
            transcendentals=0,
        ),
        name="project",
    )(cross_out, w_out)


def add_kernel(index_ref, tokens_ref, cross_ref, view_ref, out_ref):
    terms = cross_ref[...].astype(jnp.float32) + view_ref[...].astype(jnp.float32)
    out_ref[...] = (tokens_ref[...].astype(jnp.float32) + terms).astype(jnp.bfloat16)


def add_terms(head_index, hires_tokens, cross_term, view_term):
    tok_rows, cols = cross_term.shape
    rows = math.gcd(tok_rows, 1024)
    own = pl.BlockSpec((rows, cols), lambda i, index: (i, 0))
    return pl.pallas_call(
        add_kernel,
        out_shape=jax.ShapeDtypeStruct((tok_rows, cols), jnp.bfloat16),
        grid_spec=pltpu.PrefetchScalarGridSpec(
            num_scalar_prefetch=1,
            grid=(tok_rows // rows,),
            in_specs=[pl.BlockSpec((rows, cols), lambda i, index: (i, index[0])), own, own],
            out_specs=own,
        ),
        compiler_params=pltpu.CompilerParams(vmem_limit_bytes=VMEM_BYTES),
        cost_estimate=pl.CostEstimate(
            flops=2 * tok_rows * cols, bytes_accessed=8 * tok_rows * cols, transcendentals=0
        ),
        name="add",
    )(head_index.reshape(1), hires_tokens, cross_term, view_term)


def ring_chunks(own, n_tok):
    order = list(range(0, n_tok, 2)) + list(range(1, n_tok, 2))[::-1]
    upward = [(order[p], order[(p + 1) % n_tok]) for p in range(n_tok)]
    downward = [(order[p], order[p - 1]) for p in range(n_tok)]
    behind, ahead = [own], [own]
    for step in range(n_tok // 2):
        behind.append(lax.ppermute(behind[-1], "tok", upward))
        if step < (n_tok - 1) // 2:
            ahead.append(lax.ppermute(ahead[-1], "tok", downward))
    return ahead + behind[:0:-1]


def shards(
    n_head,
    n_tok,
    hires_tokens,
    lowres_tokens,
    norm_gain,
    w_cross_q,
    w_low_kv,
    w_view_qkv,
    w_out,
    block_lists,
    block_counts,
):
    tok_rows, width = hires_tokens.shape
    cols = w_cross_q.shape[1]
    quarter = tok_rows // n_head
    head_index = lax.axis_index("head")
    gain = norm_gain.reshape(1, width)

    w_view = lax.all_gather(w_view_qkv.transpose(1, 0, 2), "head", axis=0, tiled=False)
    low_kv = f32_dot(
        rms_rows(lowres_tokens, norm_gain), w_low_kv.reshape(width, 2 * cols)
    ).astype(jnp.bfloat16)
    kv_chunks = ring_chunks(low_kv, n_tok)
    own_rows = lax.dynamic_slice_in_dim(hires_tokens, head_index * quarter, quarter, 0)
    arrived = lax.all_to_all(
        own_rows.reshape(n_tok, quarter // n_tok, width),
        "tok", split_axis=0, concat_axis=0, tiled=True,
    )
    w_view, w_out = lax.optimization_barrier((w_view, w_out))
    w_out = lax.all_gather(w_out, "head", axis=0, tiled=False)

    cross_out = cross_attention(
        hires_tokens, gain, w_cross_q, kv_chunks, block_lists, block_counts
    )
    cross_out = lax.all_to_all(
        cross_out.reshape(n_head, quarter, cols), "head", split_axis=0, concat_axis=0, tiled=True
    )
    view_term = view_attention(arrived, gain, w_view, w_out)
    view_term, cross_out = lax.optimization_barrier((view_term, cross_out))
    view_term = lax.all_to_all(
        view_term.reshape(n_head * n_tok, quarter // n_tok, cols),
        ("head", "tok"), split_axis=0, concat_axis=0, tiled=True,
    )
    cross_term = cross_projection(cross_out, w_out)
    cross_term = lax.all_to_all(cross_term, "head", split_axis=0, concat_axis=0, tiled=True)
    return add_terms(
        head_index, hires_tokens, cross_term.reshape(tok_rows, cols),
        view_term.reshape(tok_rows, cols),
    )


def solution(mesh):
    in_specs = (
        P("tok", None),
        P("tok", None),
        P(),
        P(None, "head"),
        P(None, None, "head"),
        P(None, None, "head"),
        P(None, "head", None),
        P("tok", None),
        P("tok"),
    )
    out_specs = P("tok", "head")
    body = functools.partial(shards, mesh.shape["head"], mesh.shape["tok"])
    return jax.shard_map(body, mesh=mesh, in_specs=in_specs, out_specs=out_specs, check_vma=False)
```

```python
import functools
import math

import jax
import jax.numpy as jnp
from jax import lax
from jax.experimental import pallas as pl
from jax.experimental.pallas import tpu as pltpu
from jax.sharding import PartitionSpec as P

HD = 128
VIEWS = 8
BLOCK = 128
LOG2_SCALE = math.log2(math.e) / math.sqrt(HD)
VMEM_BYTES = 60 * 1024 * 1024
SMALL_VMEM_BYTES = 24 * 1024 * 1024
CONTRACT_LAST = (((1,), (1,)), ((), ()))


def rms_rows(row_block, norm_gain):
    values = row_block.astype(jnp.float32)
    factor = lax.rsqrt(jnp.mean(values * values, axis=-1, keepdims=True) + 1e-06)
    return (values * factor * norm_gain).astype(jnp.bfloat16)


def f32_dot(left, right):
    return jnp.dot(left, right, preferred_element_type=jnp.float32)


def block_diagonal(tiles):
    rows = []
    for index, tile in enumerate(tiles):
        zero = jnp.zeros_like(tile)
        rows.append(
            jnp.concatenate([tile if k == index else zero for k in range(len(tiles))], axis=1)
        )
    return jnp.concatenate(rows, axis=0)


def ring_place(tok, n_tok):
    half = lax.div(tok, 2)
    return jnp.where(lax.rem(tok, 2) == 0, half, n_tok - 1 - half)


def cross_kernel(lists_ref, counts_ref, tok_ref, tokens_ref, gain_ref, wq_ref, *refs):
    kv_refs = refs[:-4]
    out_ref, k_ref, vt_ref, q_ref = refs[-4:]
    step = pl.program_id(0)
    rows, cols = out_ref.shape
    heads = cols // HD
    per_step = rows // BLOCK
    listed = lists_ref.shape[1]

    @pl.when(step == 0)
    def _():
        n_tok = len(kv_refs)
        for offset, kv_ref in enumerate(kv_refs):
            chunk = kv_ref.shape[0]
            place = lax.rem(ring_place(tok_ref[0], n_tok) + offset, n_tok)
            home = jnp.where(place < (n_tok + 1) // 2, 2 * place, 2 * (n_tok - 1 - place) + 1)
            start = pl.multiple_of(home * chunk, BLOCK)
            k_ref[pl.ds(start, chunk), :] = kv_ref[:, :cols]
            vt_ref[:, pl.ds(start, chunk)] = kv_ref[:, cols:].T

    normed = rms_rows(tokens_ref[...], gain_ref[...])
    q_ref[...] = (f32_dot(normed, wq_ref[...]) * LOG2_SCALE).astype(jnp.bfloat16)

    def one_block(local, carry):
        block = step * per_step + local
        row_start = pl.multiple_of(local * BLOCK, BLOCK)
        count = counts_ref[block]
        first = lists_ref[block, 0]
        starts = [
            pl.multiple_of(jnp.where(j < count, lists_ref[block, j], first) * BLOCK, BLOCK)
            for j in range(listed)
        ]
        query = block_diagonal(
            [q_ref[pl.ds(row_start, BLOCK), h * HD : (h + 1) * HD] for h in range(heads)]
        )
        keys = jnp.concatenate([k_ref[pl.ds(s, BLOCK), :] for s in starts], axis=0)
        scores = lax.dot_general(keys, query, CONTRACT_LAST, preferred_element_type=jnp.float32)
        top = jnp.max(scores, axis=0, keepdims=True)
        weights = []
        total = jnp.zeros_like(top)
        for j in range(listed):
            shift = top + jnp.where(j < count, 0.0, 1e30)
            weight = jnp.exp2(scores[j * BLOCK : (j + 1) * BLOCK] - shift)
            total = total + jnp.sum(weight, axis=0, keepdims=True)
            weights.append(weight.astype(jnp.bfloat16))
        values_t = jnp.concatenate([vt_ref[:, pl.ds(s, BLOCK)] for s in starts], axis=1)
        mixed_t = f32_dot(values_t, jnp.concatenate(weights, axis=0)) / total
        for h in range(heads):
            part = slice(h * HD, (h + 1) * HD)
            out_ref[pl.ds(row_start, BLOCK), part] = mixed_t[part, part].T.astype(jnp.bfloat16)
        return carry

    lax.fori_loop(0, per_step, one_block, 0, unroll=True)


def cross_attention(hires_tokens, gain, w_cross_q, kv_chunks, block_lists, block_counts):
    tok_index = lax.axis_index("tok").reshape(1)
    tok_rows, width = hires_tokens.shape
    cols = w_cross_q.shape[1]
    chunk = kv_chunks[0].shape[0]
    low_rows = chunk * len(kv_chunks)
    rows = math.gcd(tok_rows, 4 * BLOCK)
    return pl.pallas_call(
        cross_kernel,
        out_shape=jax.ShapeDtypeStruct((tok_rows, cols), jnp.bfloat16),
        grid_spec=pltpu.PrefetchScalarGridSpec(
            num_scalar_prefetch=3,
            grid=(tok_rows // rows,),
            in_specs=[
                pl.BlockSpec((rows, width), lambda i, *_: (i, 0)),
                pl.BlockSpec((1, width), lambda i, *_: (0, 0)),
                pl.BlockSpec((width, cols), lambda i, *_: (0, 0)),
            ]
            + [pl.BlockSpec((chunk, 2 * cols), lambda i, *_: (0, 0)) for _ in kv_chunks],
            out_specs=pl.BlockSpec((rows, cols), lambda i, *_: (i, 0)),
            scratch_shapes=[
                pltpu.VMEM((low_rows, cols), jnp.bfloat16),
                pltpu.VMEM((cols, low_rows), jnp.bfloat16),
                pltpu.VMEM((rows, cols), jnp.bfloat16),
            ],
        ),
        compiler_params=pltpu.CompilerParams(vmem_limit_bytes=VMEM_BYTES),
        cost_estimate=pl.CostEstimate(
            flops=2 * tok_rows * cols * (width + 2 * block_lists.shape[1] * BLOCK * 2),
            bytes_accessed=2 * tok_rows * (width + cols),
            transcendentals=tok_rows * block_lists.shape[1] * BLOCK * (cols // HD),
        ),
        name="cross",
    )(block_lists, block_counts, tok_index, hires_tokens, gain, w_cross_q, *kv_chunks)


def view_kernel(tokens_ref, gain_ref, w_ref, wo_ref, out_ref, normed_ref, qkv_ref, mixed_ref):
    sources, run, width = tokens_ref.shape
    parts, cols, _ = wo_ref.shape
    part_index = pl.program_id(0)
    heads = cols // HD
    rows = sources * run
    pixels = rows // VIEWS
    group = math.gcd(pixels, 32)
    tile = math.gcd(rows, 256)

    @pl.when(pl.program_id(0) == 0)
    def _():
        gain = gain_ref[...]
        step = max(1, tile // run)
        for s in range(0, sources, step):
            tokens = tokens_ref[s : s + step].reshape(step * run, width)
            normed_ref[s * run : (s + step) * run] = rms_rows(tokens, gain)

    for start in range(0, rows, tile):
        stop = start + tile
        tokens = normed_ref[start:stop]
        for k in range(3):
            projected = f32_dot(tokens, w_ref[0, k])
            if k == 0:
                projected = projected * LOG2_SCALE
            qkv_ref[start:stop, k * cols : (k + 1) * cols] = projected.astype(jnp.bfloat16)
    size = VIEWS * group
    row_pixel = lax.broadcasted_iota(jnp.int32, (size, size), 0) % group
    col_pixel = lax.broadcasted_iota(jnp.int32, (size, size), 1) % group
    same = row_pixel == col_pixel

    def gathered(first, column):
        part = slice(column, column + HD)
        return jnp.concatenate(
            [qkv_ref[v * pixels + first : v * pixels + first + group, part] for v in range(VIEWS)],
            axis=0,
        )

    for first in range(0, pixels, group):
        for h in range(heads):
            query = gathered(first, h * HD)
            key = gathered(first, cols + h * HD)
            value = gathered(first, 2 * cols + h * HD)
            scores = lax.dot_general(query, key, CONTRACT_LAST, preferred_element_type=jnp.float32)
            scores = jnp.where(same, scores, -1e30)
            weight = jnp.exp2(scores - jnp.max(scores, axis=1, keepdims=True))
            total = jnp.sum(weight, axis=1, keepdims=True)
            mixed = (f32_dot(weight.astype(jnp.bfloat16), value) / total).astype(jnp.bfloat16)
            for v in range(VIEWS):
                rows_of = slice(v * pixels + first, v * pixels + first + group)
                mixed_ref[part_index, rows_of, h * HD : (h + 1) * HD] = (
                    mixed[v * group : (v + 1) * group]
                )

    @pl.when(part_index == parts - 1)
    def _():
        step = max(1, tile // run)
        for s in range(0, sources, step):
            rows_of = slice(s * run, (s + step) * run)
            term = f32_dot(mixed_ref[0, rows_of], wo_ref[0])
            for g in range(1, parts):
                term = term + f32_dot(mixed_ref[g, rows_of], wo_ref[g])
            term = term.astype(jnp.bfloat16)
            for g in range(parts):
                out_ref[g, s : s + step] = term[:, g * cols : (g + 1) * cols].reshape(
                    step, run, cols
                )


def view_attention(tokens, gain, w_view, w_out):
    sources, run, width = tokens.shape
    parts = w_view.shape[0]
    cols = w_view.shape[3]
    rows = sources * run
    return pl.pallas_call(
        view_kernel,
        out_shape=jax.ShapeDtypeStruct((parts, sources, run, cols), jnp.bfloat16),
        grid=(parts,),
        in_specs=[
            pl.BlockSpec((sources, run, width), lambda i: (0, 0, 0)),
            pl.BlockSpec((1, width), lambda i: (0, 0)),
            pl.BlockSpec((1, 3, width, cols), lambda i: (i, 0, 0, 0)),
            pl.BlockSpec((parts, cols, width), lambda i: (0, 0, 0)),
        ],
        out_specs=pl.BlockSpec((parts, sources, run, cols), lambda i: (0, 0, 0, 0)),
        scratch_shapes=[
            pltpu.VMEM((rows, width), jnp.bfloat16),
            pltpu.VMEM((rows, 3 * cols), jnp.bfloat16),
            pltpu.VMEM((parts, rows, cols), jnp.bfloat16),
        ],
        compiler_params=pltpu.CompilerParams(vmem_limit_bytes=VMEM_BYTES),
        cost_estimate=pl.CostEstimate(
            flops=2 * rows * (parts * cols * (3 * width + 512) + width * width),
            bytes_accessed=2 * (2 * rows * width + 4 * parts * width * cols),
            transcendentals=parts * rows * 512,
        ),
        name="view",
    )(tokens, gain, w_view, w_out)


def base_kernel(index_ref, tokens_ref, cross_ref, w_ref, out_ref):
    total = tokens_ref[...].astype(jnp.float32)
    for g in range(cross_ref.shape[0]):
        total = total + f32_dot(cross_ref[g], w_ref[g])
    out_ref[...] = total


def residual_and_cross(hires_tokens, cross_all, w_columns):
    parts, tok_rows, cols = cross_all.shape
    rows = math.gcd(tok_rows, 512)
    head_index = lax.axis_index("head").reshape(1)
    return pl.pallas_call(
        base_kernel,
        out_shape=jax.ShapeDtypeStruct((tok_rows, cols), jnp.float32),
        grid_spec=pltpu.PrefetchScalarGridSpec(
            num_scalar_prefetch=1,
            grid=(tok_rows // rows,),
            in_specs=[
                pl.BlockSpec((rows, cols), lambda i, index: (i, index[0])),
                pl.BlockSpec((parts, rows, cols), lambda i, index: (0, i, 0)),
                pl.BlockSpec((parts, cols, cols), lambda i, index: (0, 0, 0)),
            ],
            out_specs=pl.BlockSpec((rows, cols), lambda i, index: (i, 0)),
        ),
        compiler_params=pltpu.CompilerParams(vmem_limit_bytes=SMALL_VMEM_BYTES),
        cost_estimate=pl.CostEstimate(
            flops=2 * parts * tok_rows * cols * cols,
            bytes_accessed=2 * tok_rows * cols * (parts + 3),
            transcendentals=0,
        ),
        name="base",
    )(head_index, hires_tokens, cross_all, w_columns)


def add_kernel(base_ref, *refs):
    view_refs, out_ref = refs[:-1], refs[-1]
    for chunk, view_ref in enumerate(view_refs):
        @pl.when(pl.program_id(1) == chunk)
        def _():
            out_ref[...] = (base_ref[...] + view_ref[0].astype(jnp.float32)).astype(jnp.bfloat16)


def add_view(base, view_terms):
    tok_rows, cols = base.shape
    n_head, rows, _ = view_terms[0].shape
    chunks = len(view_terms)
    own = pl.BlockSpec((rows, cols), lambda h, c: (h * chunks + c, 0))
    return pl.pallas_call(
        add_kernel,
        out_shape=jax.ShapeDtypeStruct((tok_rows, cols), jnp.bfloat16),
        grid=(n_head, chunks),
        in_specs=[own] + [pl.BlockSpec((1, rows, cols), lambda h, c: (h, 0, 0))] * chunks,
        out_specs=own,
        compiler_params=pltpu.CompilerParams(vmem_limit_bytes=SMALL_VMEM_BYTES),
        cost_estimate=pl.CostEstimate(
            flops=tok_rows * cols, bytes_accessed=8 * tok_rows * cols, transcendentals=0
        ),
        name="add",
    )(base, *view_terms)


def ring_chunks(own, n_tok):
    order = list(range(0, n_tok, 2)) + list(range(1, n_tok, 2))[::-1]
    upward = [(order[p], order[(p + 1) % n_tok]) for p in range(n_tok)]
    downward = [(order[p], order[p - 1]) for p in range(n_tok)]
    behind, ahead = [own], [own]
    for step in range(n_tok // 2):
        behind.append(lax.ppermute(behind[-1], "tok", upward))
        if step < (n_tok - 1) // 2:
            ahead.append(lax.ppermute(ahead[-1], "tok", downward))
    return ahead + behind[:0:-1]


def shards(
    n_head,
    n_tok,
    hires_tokens,
    lowres_tokens,
    norm_gain,
    w_cross_q,
    w_low_kv,
    w_view_qkv,
    w_out,
    block_lists,
    block_counts,
):
    tok_rows, width = hires_tokens.shape
    cols = w_cross_q.shape[1]
    quarter = tok_rows // n_head
    head_index = lax.axis_index("head")
    gain = norm_gain.reshape(1, width)

    w_view = lax.all_gather(w_view_qkv.transpose(1, 0, 2), "head", axis=0, tiled=False)
    low_kv = f32_dot(
        rms_rows(lowres_tokens, norm_gain), w_low_kv.reshape(width, 2 * cols)
    ).astype(jnp.bfloat16)
    kv_chunks = ring_chunks(low_kv, n_tok)
    kv_chunks, hires_tokens, w_out = lax.optimization_barrier((kv_chunks, hires_tokens, w_out))
    w_view_out = lax.all_gather(w_out[1], "head", axis=0, tiled=False)

    run = quarter // n_tok
    chunks = 2 if run % 32 == 0 else 1
    run = run // chunks
    arrived = []
    for c in range(chunks):
        start = head_index * quarter + c * n_tok * run
        rows = lax.dynamic_slice_in_dim(hires_tokens, start, n_tok * run, 0)
        arrived.append(
            lax.all_to_all(
                rows.reshape(n_tok, run, width), "tok", split_axis=0, concat_axis=0, tiled=True
            )
        )
    cross_out = cross_attention(
        hires_tokens, gain, w_cross_q, kv_chunks, block_lists, block_counts
    )
    cross_out, arrived, w_out = lax.optimization_barrier((cross_out, arrived, w_out))
    cross_all = lax.all_gather(cross_out, "head", axis=0, tiled=False)
    w_columns = lax.all_to_all(
        w_out[0].reshape(cols, n_head, width // n_head).transpose(1, 0, 2),
        "head", split_axis=0, concat_axis=0, tiled=True,
    )
    view_terms = []
    for tokens in arrived:
        term = view_attention(tokens, gain, w_view, w_view_out)
        term = lax.all_to_all(
            term.reshape(n_head * n_tok, run, cols),
            ("head", "tok"), split_axis=0, concat_axis=0, tiled=True,
        )
        view_terms.append(term.reshape(n_head, n_tok * run, cols))
    base = residual_and_cross(hires_tokens, cross_all, w_columns)
    return add_view(base, view_terms)


def solution(mesh):
    in_specs = (
        P("tok", None),
        P("tok", None),
        P(),
        P(None, "head"),
        P(None, None, "head"),
        P(None, None, "head"),
        P(None, "head", None),
        P("tok", None),
        P("tok"),
    )
    out_specs = P("tok", "head")
    body = functools.partial(shards, mesh.shape["head"], mesh.shape["tok"])
    return jax.shard_map(body, mesh=mesh, in_specs=in_specs, out_specs=out_specs, check_vma=False)
```

```python
import functools
import math

import jax
import jax.numpy as jnp
from jax import lax
from jax.experimental import pallas as pl
from jax.experimental.pallas import tpu as pltpu
from jax.sharding import PartitionSpec as P

HD = 128
VIEWS = 8
BLOCK = 128
LOG2_SCALE = math.log2(math.e) / math.sqrt(HD)
VMEM_BYTES = 60 * 1024 * 1024
CONTRACT_LAST = (((1,), (1,)), ((), ()))


def rms_rows(row_block, norm_gain):
    values = row_block.astype(jnp.float32)
    factor = lax.rsqrt(jnp.mean(values * values, axis=-1, keepdims=True) + 1e-06)
    return (values * factor * norm_gain).astype(jnp.bfloat16)


def f32_dot(left, right):
    return jnp.dot(left, right, preferred_element_type=jnp.float32)


def block_diagonal(tiles):
    rows = []
    for index, tile in enumerate(tiles):
        zero = jnp.zeros_like(tile)
        rows.append(
            jnp.concatenate([tile if k == index else zero for k in range(len(tiles))], axis=1)
        )
    return jnp.concatenate(rows, axis=0)


def ring_place(tok, n_tok):
    half = lax.div(tok, 2)
    return jnp.where(lax.rem(tok, 2) == 0, half, n_tok - 1 - half)


def cross_kernel(lists_ref, counts_ref, tok_ref, tokens_ref, gain_ref, wq_ref, *refs):
    kv_refs = refs[:-4]
    out_ref, k_ref, vt_ref, q_ref = refs[-4:]
    step = pl.program_id(0)
    rows, cols = out_ref.shape
    heads = cols // HD
    per_step = rows // BLOCK
    listed = lists_ref.shape[1]

    @pl.when(step == 0)
    def _():
        n_tok = len(kv_refs)
        for offset, kv_ref in enumerate(kv_refs):
            chunk = kv_ref.shape[0]
            place = lax.rem(ring_place(tok_ref[0], n_tok) + offset, n_tok)
            home = jnp.where(place < (n_tok + 1) // 2, 2 * place, 2 * (n_tok - 1 - place) + 1)
            start = pl.multiple_of(home * chunk, BLOCK)
            k_ref[pl.ds(start, chunk), :] = kv_ref[:, :cols]
            vt_ref[:, pl.ds(start, chunk)] = kv_ref[:, cols:].T

    normed = rms_rows(tokens_ref[...], gain_ref[...])
    q_ref[...] = (f32_dot(normed, wq_ref[...]) * LOG2_SCALE).astype(jnp.bfloat16)

    def one_block(local, carry):
        block = step * per_step + local
        row_start = pl.multiple_of(local * BLOCK, BLOCK)
        count = counts_ref[block]
        first = lists_ref[block, 0]
        starts = [
            pl.multiple_of(jnp.where(j < count, lists_ref[block, j], first) * BLOCK, BLOCK)
            for j in range(listed)
        ]
        query = block_diagonal(
            [q_ref[pl.ds(row_start, BLOCK), h * HD : (h + 1) * HD] for h in range(heads)]
        )
        keys = jnp.concatenate([k_ref[pl.ds(s, BLOCK), :] for s in starts], axis=0)
        scores = lax.dot_general(keys, query, CONTRACT_LAST, preferred_element_type=jnp.float32)
        top = jnp.max(scores, axis=0, keepdims=True)
        weights = []
        total = jnp.zeros_like(top)
        for j in range(listed):
            shift = top + jnp.where(j < count, 0.0, 1e30)
            weight = jnp.exp2(scores[j * BLOCK : (j + 1) * BLOCK] - shift)
            total = total + jnp.sum(weight, axis=0, keepdims=True)
            weights.append(weight.astype(jnp.bfloat16))
        values_t = jnp.concatenate([vt_ref[:, pl.ds(s, BLOCK)] for s in starts], axis=1)
        mixed_t = f32_dot(values_t, jnp.concatenate(weights, axis=0)) / total
        for h in range(heads):
            part = slice(h * HD, (h + 1) * HD)
            out_ref[pl.ds(row_start, BLOCK), part] = mixed_t[part, part].T.astype(jnp.bfloat16)
        return carry

    lax.fori_loop(0, per_step, one_block, 0, unroll=True)


def cross_attention(hires_tokens, gain, w_cross_q, kv_chunks, block_lists, block_counts):
    tok_index = lax.axis_index("tok").reshape(1)
    tok_rows, width = hires_tokens.shape
    cols = w_cross_q.shape[1]
    chunk = kv_chunks[0].shape[0]
    low_rows = chunk * len(kv_chunks)
    rows = math.gcd(tok_rows, 4 * BLOCK)
    return pl.pallas_call(
        cross_kernel,
        out_shape=jax.ShapeDtypeStruct((tok_rows, cols), jnp.bfloat16),
        grid_spec=pltpu.PrefetchScalarGridSpec(
            num_scalar_prefetch=3,
            grid=(tok_rows // rows,),
            in_specs=[
                pl.BlockSpec((rows, width), lambda i, *_: (i, 0)),
                pl.BlockSpec((1, width), lambda i, *_: (0, 0)),
                pl.BlockSpec((width, cols), lambda i, *_: (0, 0)),
            ]
            + [pl.BlockSpec((chunk, 2 * cols), lambda i, *_: (0, 0)) for _ in kv_chunks],
            out_specs=pl.BlockSpec((rows, cols), lambda i, *_: (i, 0)),
            scratch_shapes=[
                pltpu.VMEM((low_rows, cols), jnp.bfloat16),
                pltpu.VMEM((cols, low_rows), jnp.bfloat16),
                pltpu.VMEM((rows, cols), jnp.bfloat16),
            ],
        ),
        compiler_params=pltpu.CompilerParams(vmem_limit_bytes=VMEM_BYTES),
        cost_estimate=pl.CostEstimate(
            flops=2 * tok_rows * cols * (width + 2 * block_lists.shape[1] * BLOCK * 2),
            bytes_accessed=2 * tok_rows * (width + cols),
            transcendentals=tok_rows * block_lists.shape[1] * BLOCK * (cols // HD),
        ),
        name="cross",
    )(block_lists, block_counts, tok_index, hires_tokens, gain, w_cross_q, *kv_chunks)


def view_kernel(tokens_ref, gain_ref, w_ref, wo_ref, out_ref, normed_ref, qkv_ref, mixed_ref):
    sources, run, width = tokens_ref.shape
    parts, cols, _ = wo_ref.shape
    part_index = pl.program_id(0)
    heads = cols // HD
    rows = sources * run
    pixels = rows // VIEWS
    group = math.gcd(pixels, 32)
    tile = math.gcd(rows, 256)

    @pl.when(pl.program_id(0) == 0)
    def _():
        gain = gain_ref[...]
        step = max(1, tile // run)
        for s in range(0, sources, step):
            tokens = tokens_ref[s : s + step].reshape(step * run, width)
            normed_ref[s * run : (s + step) * run] = rms_rows(tokens, gain)

    for start in range(0, rows, tile):
        stop = start + tile
        tokens = normed_ref[start:stop]
        for k in range(3):
            projected = f32_dot(tokens, w_ref[0, k])
            if k == 0:
                projected = projected * LOG2_SCALE
            qkv_ref[start:stop, k * cols : (k + 1) * cols] = projected.astype(jnp.bfloat16)
    size = VIEWS * group
    row_pixel = lax.broadcasted_iota(jnp.int32, (size, size), 0) % group
    col_pixel = lax.broadcasted_iota(jnp.int32, (size, size), 1) % group
    same = row_pixel == col_pixel

    def gathered(first, column):
        part = slice(column, column + HD)
        return jnp.concatenate(
            [qkv_ref[v * pixels + first : v * pixels + first + group, part] for v in range(VIEWS)],
            axis=0,
        )

    for first in range(0, pixels, group):
        for h in range(heads):
            query = gathered(first, h * HD)
            key = gathered(first, cols + h * HD)
            value = gathered(first, 2 * cols + h * HD)
            scores = lax.dot_general(query, key, CONTRACT_LAST, preferred_element_type=jnp.float32)
            scores = jnp.where(same, scores, -1e30)
            weight = jnp.exp2(scores - jnp.max(scores, axis=1, keepdims=True))
            total = jnp.sum(weight, axis=1, keepdims=True)
            mixed = (f32_dot(weight.astype(jnp.bfloat16), value) / total).astype(jnp.bfloat16)
            for v in range(VIEWS):
                rows_of = slice(v * pixels + first, v * pixels + first + group)
                mixed_ref[part_index, rows_of, h * HD : (h + 1) * HD] = (
                    mixed[v * group : (v + 1) * group]
                )

    @pl.when(part_index == parts - 1)
    def _():
        step = max(1, tile // run)
        for s in range(0, sources, step):
            rows_of = slice(s * run, (s + step) * run)
            term = f32_dot(mixed_ref[0, rows_of], wo_ref[0])
            for g in range(1, parts):
                term = term + f32_dot(mixed_ref[g, rows_of], wo_ref[g])
            term = term.astype(jnp.bfloat16)
            for g in range(parts):
                out_ref[g, s : s + step] = term[:, g * cols : (g + 1) * cols].reshape(
                    step, run, cols
                )


def view_attention(tokens, gain, w_view, w_out):
    sources, run, width = tokens.shape
    parts = w_view.shape[0]
    cols = w_view.shape[3]
    rows = sources * run
    return pl.pallas_call(
        view_kernel,
        out_shape=jax.ShapeDtypeStruct((parts, sources, run, cols), jnp.bfloat16),
        grid=(parts,),
        in_specs=[
            pl.BlockSpec((sources, run, width), lambda i: (0, 0, 0)),
            pl.BlockSpec((1, width), lambda i: (0, 0)),
            pl.BlockSpec((1, 3, width, cols), lambda i: (i, 0, 0, 0)),
            pl.BlockSpec((parts, cols, width), lambda i: (0, 0, 0)),
        ],
        out_specs=pl.BlockSpec((parts, sources, run, cols), lambda i: (0, 0, 0, 0)),
        scratch_shapes=[
            pltpu.VMEM((rows, width), jnp.bfloat16),
            pltpu.VMEM((rows, 3 * cols), jnp.bfloat16),
            pltpu.VMEM((parts, rows, cols), jnp.bfloat16),
        ],
        compiler_params=pltpu.CompilerParams(vmem_limit_bytes=VMEM_BYTES),
        cost_estimate=pl.CostEstimate(
            flops=2 * rows * (parts * cols * (3 * width + 512) + width * width),
            bytes_accessed=2 * (2 * rows * width + 4 * parts * width * cols),
            transcendentals=parts * rows * 512,
        ),
        name="view",
    )(tokens, gain, w_view, w_out)


def base_kernel(index_ref, tokens_ref, cross_ref, *refs):
    w_refs, out_ref = refs[:-1], refs[-1]
    parts = len(w_refs)
    total = tokens_ref[...].astype(jnp.float32)
    for k, w_ref in enumerate(w_refs):
        group = lax.rem(index_ref[0] + parts - k, parts)
        total = total + f32_dot(cross_ref[group], w_ref[...])
    out_ref[...] = total


def residual_and_cross(head_index, hires_tokens, cross_all, w_columns):
    parts, tok_rows, cols = cross_all.shape
    rows = math.gcd(tok_rows, 512)
    return pl.pallas_call(
        base_kernel,
        out_shape=jax.ShapeDtypeStruct((tok_rows, cols), jnp.float32),
        grid_spec=pltpu.PrefetchScalarGridSpec(
            num_scalar_prefetch=1,
            grid=(tok_rows // rows,),
            in_specs=[
                pl.BlockSpec((rows, cols), lambda i, index: (i, index[0])),
                pl.BlockSpec((parts, rows, cols), lambda i, index: (0, i, 0)),
            ]
            + [pl.BlockSpec((cols, cols), lambda i, index: (0, 0))] * parts,
            out_specs=pl.BlockSpec((rows, cols), lambda i, index: (i, 0)),
        ),
        compiler_params=pltpu.CompilerParams(vmem_limit_bytes=VMEM_BYTES),
        cost_estimate=pl.CostEstimate(
            flops=2 * parts * tok_rows * cols * cols,
            bytes_accessed=2 * tok_rows * cols * (parts + 3),
            transcendentals=0,
        ),
        name="base",
    )(head_index.reshape(1), hires_tokens, cross_all, *w_columns)


def add_kernel(base_ref, view_ref, *refs):
    refs[-1][...] = (base_ref[...] + view_ref[0].astype(jnp.float32)).astype(jnp.bfloat16)


def add_view(base, view_term, chunk, chunks, earlier):
    tok_rows, cols = base.shape
    n_head, rows, _ = view_term.shape
    own = pl.BlockSpec((rows, cols), lambda h: (h * chunks + chunk, 0))
    in_specs = [own, pl.BlockSpec((1, rows, cols), lambda h: (h, 0, 0))]
    operands = [base, view_term]
    if earlier is not None:
        in_specs.append(pl.BlockSpec(memory_space=pl.ANY))
        operands.append(earlier)
    return pl.pallas_call(
        add_kernel,
        out_shape=jax.ShapeDtypeStruct((tok_rows, cols), jnp.bfloat16),
        grid=(n_head,),
        in_specs=in_specs,
        out_specs=own,
        input_output_aliases={} if earlier is None else {2: 0},
        compiler_params=pltpu.CompilerParams(vmem_limit_bytes=VMEM_BYTES),
        cost_estimate=pl.CostEstimate(
            flops=n_head * rows * cols, bytes_accessed=8 * n_head * rows * cols, transcendentals=0
        ),
        name="add",
    )(*operands)


def column_blocks(rows_of_w, head_index, n_head):
    cols = rows_of_w.shape[1] // n_head
    blocks = []
    for k in range(n_head):
        start = lax.rem(head_index + k, n_head) * cols
        block = lax.dynamic_slice_in_dim(rows_of_w, start, cols, 1)
        if k:
            pairs = [(h, (h + k) % n_head) for h in range(n_head)]
            block = lax.ppermute(block, "head", pairs)
        blocks.append(block)
    return blocks


def ring_chunks(own, n_tok):
    order = list(range(0, n_tok, 2)) + list(range(1, n_tok, 2))[::-1]
    upward = [(order[p], order[(p + 1) % n_tok]) for p in range(n_tok)]
    downward = [(order[p], order[p - 1]) for p in range(n_tok)]
    behind, ahead = [own], [own]
    for step in range(n_tok // 2):
        behind.append(lax.ppermute(behind[-1], "tok", upward))
        if step < (n_tok - 1) // 2:
            ahead.append(lax.ppermute(ahead[-1], "tok", downward))
    return ahead + behind[:0:-1]


def shards(
    n_head,
    n_tok,
    hires_tokens,
    lowres_tokens,
    norm_gain,
    w_cross_q,
    w_low_kv,
    w_view_qkv,
    w_out,
    block_lists,
    block_counts,
):
    tok_rows, width = hires_tokens.shape
    cols = w_cross_q.shape[1]
    quarter = tok_rows // n_head
    head_index = lax.axis_index("head")
    gain = norm_gain.reshape(1, width)

    w_view = lax.all_gather(w_view_qkv.transpose(1, 0, 2), "head", axis=0, tiled=False)
    low_kv = f32_dot(
        rms_rows(lowres_tokens, norm_gain), w_low_kv.reshape(width, 2 * cols)
    ).astype(jnp.bfloat16)
    kv_chunks = ring_chunks(low_kv, n_tok)
    w_view_out = lax.all_gather(w_out[1], "head", axis=0, tiled=False)
    kv_chunks, hires_tokens = lax.optimization_barrier((kv_chunks, hires_tokens))

    run = quarter // n_tok
    chunks = 2 if run % 32 == 0 else 1
    run = run // chunks

    def arrive(chunk, tokens):
        start = head_index * quarter + chunk * n_tok * run
        rows = lax.dynamic_slice_in_dim(tokens, start, n_tok * run, 0)
        return lax.all_to_all(
            rows.reshape(n_tok, run, width), "tok", split_axis=0, concat_axis=0, tiled=True
        )

    arrived = [arrive(0, hires_tokens)]
    cross_out = cross_attention(
        hires_tokens, gain, w_cross_q, kv_chunks, block_lists, block_counts
    )
    cross_out, arrived, w_out, hires_tokens = lax.optimization_barrier(
        (cross_out, arrived, w_out, hires_tokens)
    )
    cross_all = lax.all_gather(cross_out, "head", axis=0, tiled=False)
    for chunk in range(1, chunks):
        arrived.append(arrive(chunk, hires_tokens))
    w_columns = column_blocks(w_out[0], head_index, n_head)
    view_terms = []
    for tokens in arrived:
        term = view_attention(tokens, gain, w_view, w_view_out)
        term = lax.all_to_all(
            term.reshape(n_head * n_tok, run, cols),
            ("head", "tok"), split_axis=0, concat_axis=0, tiled=True,
        )
        view_terms.append(term.reshape(n_head, n_tok * run, cols))
    base = residual_and_cross(head_index, hires_tokens, cross_all, w_columns)
    layer_out = None
    for chunk, view_term in enumerate(view_terms):
        layer_out = add_view(base, view_term, chunk, chunks, layer_out)
    return layer_out


def solution(mesh):
    in_specs = (
        P("tok", None),
        P("tok", None),
        P(),
        P(None, "head"),
        P(None, None, "head"),
        P(None, None, "head"),
        P(None, "head", None),
        P("tok", None),
        P("tok"),
    )
    out_specs = P("tok", "head")
    body = functools.partial(shards, mesh.shape["head"], mesh.shape["tok"])
    return jax.shard_map(body, mesh=mesh, in_specs=in_specs, out_specs=out_specs, check_vma=False)
```

```python
import functools
import math

import jax
import jax.numpy as jnp
from jax import lax
from jax.experimental import pallas as pl
from jax.experimental.pallas import tpu as pltpu
from jax.sharding import PartitionSpec as P

HD = 128
VIEWS = 8
BLOCK = 128
LOG2_SCALE = math.log2(math.e) / math.sqrt(HD)
VMEM_BYTES = 60 * 1024 * 1024
CONTRACT_LAST = (((1,), (1,)), ((), ()))


def rms_rows(row_block, norm_gain):
    values = row_block.astype(jnp.float32)
    factor = lax.rsqrt(jnp.mean(values * values, axis=-1, keepdims=True) + 1e-06)
    return (values * factor * norm_gain).astype(jnp.bfloat16)


def f32_dot(left, right):
    return jnp.dot(left, right, preferred_element_type=jnp.float32)


def block_diagonal(tiles):
    rows = []
    for index, tile in enumerate(tiles):
        zero = jnp.zeros_like(tile)
        rows.append(
            jnp.concatenate([tile if k == index else zero for k in range(len(tiles))], axis=1)
        )
    return jnp.concatenate(rows, axis=0)


def ring_place(tok, n_tok):
    half = lax.div(tok, 2)
    return jnp.where(lax.rem(tok, 2) == 0, half, n_tok - 1 - half)


def cross_kernel(first_step, lists_ref, counts_ref, tok_ref, tokens_ref, gain_ref, wq_ref, *refs):
    kv_refs = refs[:-4]
    out_ref, k_ref, vt_ref, q_ref = refs[-4:]
    step = pl.program_id(0)
    rows, cols = out_ref.shape
    heads = cols // HD
    per_step = rows // BLOCK
    listed = lists_ref.shape[1]

    @pl.when(step == 0)
    def _():
        n_tok = len(kv_refs)
        for offset, kv_ref in enumerate(kv_refs):
            chunk = kv_ref.shape[0]
            place = lax.rem(ring_place(tok_ref[0], n_tok) + offset, n_tok)
            home = jnp.where(place < (n_tok + 1) // 2, 2 * place, 2 * (n_tok - 1 - place) + 1)
            start = pl.multiple_of(home * chunk, BLOCK)
            k_ref[pl.ds(start, chunk), :] = kv_ref[:, :cols]
            vt_ref[:, pl.ds(start, chunk)] = kv_ref[:, cols:].T

    normed = rms_rows(tokens_ref[...], gain_ref[...])
    q_ref[...] = (f32_dot(normed, wq_ref[...]) * LOG2_SCALE).astype(jnp.bfloat16)

    def one_block(local, carry):
        block = (first_step + step) * per_step + local
        row_start = pl.multiple_of(local * BLOCK, BLOCK)
        count = counts_ref[block]
        first = lists_ref[block, 0]
        starts = [
            pl.multiple_of(jnp.where(j < count, lists_ref[block, j], first) * BLOCK, BLOCK)
            for j in range(listed)
        ]
        query = block_diagonal(
            [q_ref[pl.ds(row_start, BLOCK), h * HD : (h + 1) * HD] for h in range(heads)]
        )
        keys = jnp.concatenate([k_ref[pl.ds(s, BLOCK), :] for s in starts], axis=0)
        scores = lax.dot_general(keys, query, CONTRACT_LAST, preferred_element_type=jnp.float32)
        top = jnp.max(scores, axis=0, keepdims=True)
        weights = []
        total = jnp.zeros_like(top)
        for j in range(listed):
            shift = top + jnp.where(j < count, 0.0, 1e30)
            weight = jnp.exp2(scores[j * BLOCK : (j + 1) * BLOCK] - shift)
            total = total + jnp.sum(weight, axis=0, keepdims=True)
            weights.append(weight.astype(jnp.bfloat16))
        values_t = jnp.concatenate([vt_ref[:, pl.ds(s, BLOCK)] for s in starts], axis=1)
        mixed_t = f32_dot(values_t, jnp.concatenate(weights, axis=0)) / total
        for h in range(heads):
            part = slice(h * HD, (h + 1) * HD)
            out_ref[pl.ds(row_start, BLOCK), part] = mixed_t[part, part].T.astype(jnp.bfloat16)
        return carry

    lax.fori_loop(0, per_step, one_block, 0, unroll=True)


def cross_attention(
    hires_tokens, gain, w_cross_q, kv_chunks, block_lists, block_counts, part, parts
):
    tok_index = lax.axis_index("tok").reshape(1)
    tok_rows, width = hires_tokens.shape
    cols = w_cross_q.shape[1]
    chunk = kv_chunks[0].shape[0]
    low_rows = chunk * len(kv_chunks)
    tok_rows = tok_rows // parts
    rows = math.gcd(tok_rows, 4 * BLOCK)
    first = part * tok_rows // rows
    return pl.pallas_call(
        functools.partial(cross_kernel, first),
        out_shape=jax.ShapeDtypeStruct((tok_rows, cols), jnp.bfloat16),
        grid_spec=pltpu.PrefetchScalarGridSpec(
            num_scalar_prefetch=3,
            grid=(tok_rows // rows,),
            in_specs=[
                pl.BlockSpec((rows, width), lambda i, *_: (first + i, 0)),
                pl.BlockSpec((1, width), lambda i, *_: (0, 0)),
                pl.BlockSpec((width, cols), lambda i, *_: (0, 0)),
            ]
            + [pl.BlockSpec((chunk, 2 * cols), lambda i, *_: (0, 0)) for _ in kv_chunks],
            out_specs=pl.BlockSpec((rows, cols), lambda i, *_: (i, 0)),
            scratch_shapes=[
                pltpu.VMEM((low_rows, cols), jnp.bfloat16),
                pltpu.VMEM((cols, low_rows), jnp.bfloat16),
                pltpu.VMEM((rows, cols), jnp.bfloat16),
            ],
        ),
        compiler_params=pltpu.CompilerParams(vmem_limit_bytes=VMEM_BYTES),
        cost_estimate=pl.CostEstimate(
            flops=2 * tok_rows * cols * (width + 2 * block_lists.shape[1] * BLOCK * 2),
            bytes_accessed=2 * tok_rows * (width + cols),
            transcendentals=tok_rows * block_lists.shape[1] * BLOCK * (cols // HD),
        ),
        name="cross",
    )(block_lists, block_counts, tok_index, hires_tokens, gain, w_cross_q, *kv_chunks)


def view_kernel(tok_ref, gain_ref, w_ref, wo_ref, *refs):
    token_refs = refs[:-4]
    out_ref, normed_ref, qkv_ref, mixed_ref = refs[-4:]
    parts, sources, run, cols = out_ref.shape
    part_index = pl.program_id(0)
    heads = cols // HD
    rows = sources * run
    pixels = rows // VIEWS
    group = math.gcd(pixels, 32)
    tile = math.gcd(rows, 256)

    @pl.when(pl.program_id(0) == 0)
    def _():
        gain = gain_ref[...]
        if len(token_refs) == 1:
            step = max(1, tile // run)
            for s in range(0, sources, step):
                tokens = token_refs[0][s : s + step].reshape(step * run, gain.shape[1])
                normed_ref[s * run : (s + step) * run] = rms_rows(tokens, gain)
        else:
            for k, token_ref in enumerate(token_refs):
                source = partner(tok_ref[0], k, sources, -1)
                start = pl.multiple_of(source * run, run)
                normed_ref[pl.ds(start, run), :] = rms_rows(token_ref[...], gain)

    for start in range(0, rows, tile):
        stop = start + tile
        tokens = normed_ref[start:stop]
        for k in range(3):
            projected = f32_dot(tokens, w_ref[0, k])
            if k == 0:
                projected = projected * LOG2_SCALE
            qkv_ref[start:stop, k * cols : (k + 1) * cols] = projected.astype(jnp.bfloat16)
    size = VIEWS * group
    row_pixel = lax.broadcasted_iota(jnp.int32, (size, size), 0) % group
    col_pixel = lax.broadcasted_iota(jnp.int32, (size, size), 1) % group
    same = row_pixel == col_pixel

    def gathered(first, column):
        part = slice(column, column + HD)
        return jnp.concatenate(
            [qkv_ref[v * pixels + first : v * pixels + first + group, part] for v in range(VIEWS)],
            axis=0,
        )

    for first in range(0, pixels, group):
        for h in range(heads):
            query = gathered(first, h * HD)
            key = gathered(first, cols + h * HD)
            value = gathered(first, 2 * cols + h * HD)
            scores = lax.dot_general(query, key, CONTRACT_LAST, preferred_element_type=jnp.float32)
            scores = jnp.where(same, scores, -1e30)
            weight = jnp.exp2(scores - jnp.max(scores, axis=1, keepdims=True))
            total = jnp.sum(weight, axis=1, keepdims=True)
            mixed = (f32_dot(weight.astype(jnp.bfloat16), value) / total).astype(jnp.bfloat16)
            for v in range(VIEWS):
                rows_of = slice(v * pixels + first, v * pixels + first + group)
                mixed_ref[part_index, rows_of, h * HD : (h + 1) * HD] = (
                    mixed[v * group : (v + 1) * group]
                )

    @pl.when(part_index == parts - 1)
    def _():
        step = max(1, tile // run)
        for s in range(0, sources, step):
            rows_of = slice(s * run, (s + step) * run)
            for column in range(parts):
                w_rows = slice(column * cols, (column + 1) * cols)
                term = f32_dot(mixed_ref[0, rows_of], wo_ref[0, 0, w_rows])
                for g in range(1, parts):
                    term = term + f32_dot(mixed_ref[g, rows_of], wo_ref[g, 0, w_rows])
                out_ref[column, s : s + step] = term.astype(jnp.bfloat16).reshape(step, run, cols)


def view_attention(tokens, gain, weights, n_tok):
    run, width = tokens[0].shape[-2:]
    parts, _, _, cols = weights.shape
    rows = n_tok * run
    token_specs = [
        pl.BlockSpec(block.shape, lambda i, tok, rank=block.ndim: (0,) * rank) for block in tokens
    ]
    tok_index = lax.axis_index("tok").reshape(1)
    return pl.pallas_call(
        view_kernel,
        out_shape=jax.ShapeDtypeStruct((parts, n_tok, run, cols), jnp.bfloat16),
        grid_spec=pltpu.PrefetchScalarGridSpec(
            num_scalar_prefetch=1,
            grid=(parts,),
            in_specs=[
                pl.BlockSpec((1, width), lambda i, tok: (0, 0)),
                pl.BlockSpec((1, 3, width, cols), lambda i, tok: (i, 0, 0, 0)),
                pl.BlockSpec((parts, 1, width, cols), lambda i, tok: (0, 3, 0, 0)),
            ]
            + token_specs,
            out_specs=pl.BlockSpec((parts, n_tok, run, cols), lambda i, tok: (0, 0, 0, 0)),
            scratch_shapes=[
                pltpu.VMEM((rows, width), jnp.bfloat16),
                pltpu.VMEM((rows, 3 * cols), jnp.bfloat16),
                pltpu.VMEM((parts, rows, cols), jnp.bfloat16),
            ],
        ),
        compiler_params=pltpu.CompilerParams(vmem_limit_bytes=VMEM_BYTES),
        cost_estimate=pl.CostEstimate(
            flops=2 * rows * (parts * cols * (3 * width + 512) + width * width),
            bytes_accessed=2 * (2 * rows * width + 4 * parts * width * cols),
            transcendentals=parts * rows * 512,
        ),
        name="view",
    )(tok_index, gain, weights, weights, *tokens)


def base_kernel(index_ref, tokens_ref, cross_ref, *refs):
    w_refs, out_ref = refs[:-1], refs[-1]
    parts = len(w_refs)
    total = tokens_ref[...].astype(jnp.float32)
    for k, w_ref in enumerate(w_refs):
        group = partner(index_ref[0], k, parts, -1)
        total = total + f32_dot(cross_ref[group], w_ref[...])
    out_ref[...] = total


def residual_and_cross(head_index, hires_tokens, cross_all, w_columns, part):
    parts, tok_rows, cols = cross_all.shape
    rows = math.gcd(tok_rows, 512)
    first = part * tok_rows // rows
    return pl.pallas_call(
        base_kernel,
        out_shape=jax.ShapeDtypeStruct((tok_rows, cols), jnp.float32),
        grid_spec=pltpu.PrefetchScalarGridSpec(
            num_scalar_prefetch=1,
            grid=(tok_rows // rows,),
            in_specs=[
                pl.BlockSpec((rows, cols), lambda i, index: (first + i, index[0])),
                pl.BlockSpec((parts, rows, cols), lambda i, index: (0, i, 0)),
            ]
            + [pl.BlockSpec((cols, cols), lambda i, index: (0, 0))] * parts,
            out_specs=pl.BlockSpec((rows, cols), lambda i, index: (i, 0)),
        ),
        compiler_params=pltpu.CompilerParams(vmem_limit_bytes=VMEM_BYTES),
        cost_estimate=pl.CostEstimate(
            flops=2 * parts * tok_rows * cols * cols,
            bytes_accessed=2 * tok_rows * cols * (parts + 3),
            transcendentals=0,
        ),
        name="base",
    )(head_index.reshape(1), hires_tokens, cross_all, *w_columns)


def add_kernel(steps, n_bases, *refs):
    view_ref, out_ref = refs[n_bases], refs[-1]
    for part in range(n_bases):
        @pl.when(lax.div(pl.program_id(0), steps) == part)
        def _():
            terms = refs[part][...] + view_ref[0].astype(jnp.float32)
            out_ref[...] = terms.astype(jnp.bfloat16)


def add_view(bases, view_term, chunk, chunks, earlier):
    cols = bases[0].shape[1]
    n_head, rows, _ = view_term.shape
    steps = n_head // len(bases)
    in_specs = [
        pl.BlockSpec(
            (rows, cols),
            lambda h, part=part: (jnp.clip(h - part * steps, 0, steps - 1) * chunks + chunk, 0),
        )
        for part in range(len(bases))
    ]
    in_specs.append(pl.BlockSpec((1, rows, cols), lambda h: (h, 0, 0)))
    operands = [*bases, view_term]
    if earlier is not None:
        in_specs.append(pl.BlockSpec(memory_space=pl.ANY))
        operands.append(earlier)
    return pl.pallas_call(
        functools.partial(add_kernel, steps, len(bases)),
        out_shape=jax.ShapeDtypeStruct((n_head * chunks * rows, cols), jnp.bfloat16),
        grid=(n_head,),
        in_specs=in_specs,
        out_specs=pl.BlockSpec((rows, cols), lambda h: (h * chunks + chunk, 0)),
        input_output_aliases={} if earlier is None else {len(operands) - 1: 0},
        compiler_params=pltpu.CompilerParams(vmem_limit_bytes=VMEM_BYTES),
        cost_estimate=pl.CostEstimate(
            flops=n_head * rows * cols, bytes_accessed=8 * n_head * rows * cols, transcendentals=0
        ),
        name="add",
    )(*operands)


def partner(index, k, n, sign):
    if n & (n - 1) == 0:
        return index ^ k
    return lax.rem(index + n + sign * k, n) if k else index


def exchange(block, axis, k, n):
    if k == 0:
        return block
    pairs = [(i, i ^ k if n & (n - 1) == 0 else (i + k) % n) for i in range(n)]
    return lax.ppermute(block, axis, pairs)


def ring_chunks(own, n_tok):
    order = list(range(0, n_tok, 2)) + list(range(1, n_tok, 2))[::-1]
    upward = [(order[p], order[(p + 1) % n_tok]) for p in range(n_tok)]
    downward = [(order[p], order[p - 1]) for p in range(n_tok)]
    behind, ahead = [own], [own]
    for step in range(n_tok // 2):
        behind.append(lax.ppermute(behind[-1], "tok", upward))
        if step < (n_tok - 1) // 2:
            ahead.append(lax.ppermute(ahead[-1], "tok", downward))
    return ahead + behind[:0:-1]


def shards(
    n_head,
    n_tok,
    hires_tokens,
    lowres_tokens,
    norm_gain,
    w_cross_q,
    w_low_kv,
    w_view_qkv,
    w_out,
    block_lists,
    block_counts,
):
    tok_rows, width = hires_tokens.shape
    cols = w_cross_q.shape[1]
    quarter = tok_rows // n_head
    head_index = lax.axis_index("head")
    tok_index = lax.axis_index("tok")
    gain = norm_gain.reshape(1, width)

    run = quarter // n_tok
    chunks = 2 if run % 32 == 0 else 1
    run = run // chunks
    parts = 2 if n_head % 2 == 0 else 1

    low_kv = f32_dot(
        rms_rows(lowres_tokens, norm_gain), w_low_kv.reshape(width, 2 * cols)
    ).astype(jnp.bfloat16)
    own_weights = jnp.concatenate(
        [
            w_view_qkv.transpose(1, 0, 2),
            w_out[1].reshape(cols, n_head, cols).transpose(1, 0, 2).reshape(1, width, cols),
        ],
        axis=0,
    )
    weights = lax.all_gather(own_weights, "head", axis=0, tiled=False)
    kv_chunks = ring_chunks(low_kv, n_tok)

    def rows_for(chunk, place, count):
        start = head_index * quarter + (chunk * n_tok + place) * run
        return lax.dynamic_slice_in_dim(hires_tokens, start, count * run, 0)

    first_rows = rows_for(0, 0, n_tok).reshape(n_tok, run, width)
    later_rows = [
        [rows_for(chunk, partner(tok_index, k, n_tok, 1), 1) for k in range(n_tok)]
        for chunk in range(1, chunks)
    ]
    w_columns = [
        lax.dynamic_slice_in_dim(w_out[0], partner(head_index, k, n_head, 1) * cols, cols, 1)
        for k in range(n_head)
    ]
    kv_chunks, first_rows, later_rows, w_columns = lax.optimization_barrier(
        (kv_chunks, first_rows, later_rows, w_columns)
    )

    arrived = [[lax.all_to_all(first_rows, "tok", split_axis=0, concat_axis=0, tiled=True)]]
    cross_parts = []
    for part in range(parts):
        out = cross_attention(
            hires_tokens, gain, w_cross_q, kv_chunks, block_lists, block_counts, part, parts
        )
        if part == 0:
            out, later_rows, w_columns, kv_chunks = lax.optimization_barrier(
                (out, later_rows, w_columns, kv_chunks)
            )
            for rows in later_rows:
                arrived.append([exchange(block, "tok", k, n_tok) for k, block in enumerate(rows)])
            w_columns = [exchange(block, "head", k, n_head) for k, block in enumerate(w_columns)]
        out, weights = lax.optimization_barrier((out, weights))
        cross_parts.append(lax.all_gather(out, "head", axis=0, tiled=False))
        if part == parts - 1:
            arrived[0], out = lax.optimization_barrier((arrived[0], out))
    view_terms = []
    for tokens in arrived:
        term = view_attention(tokens, gain, weights, n_tok)
        _, cross_parts = lax.optimization_barrier((term, cross_parts))
        term = lax.all_to_all(
            term.reshape(n_head * n_tok, run, cols),
            ("head", "tok"), split_axis=0, concat_axis=0, tiled=True,
        )
        view_terms.append(term.reshape(n_head, n_tok * run, cols))
    bases = [
        residual_and_cross(head_index, hires_tokens, cross_all, w_columns, part)
        for part, cross_all in enumerate(cross_parts)
    ]
    layer_out = None
    for chunk, view_term in enumerate(view_terms):
        layer_out = add_view(bases, view_term, chunk, chunks, layer_out)
    return layer_out


def solution(mesh):
    in_specs = (
        P("tok", None),
        P("tok", None),
        P(),
        P(None, "head"),
        P(None, None, "head"),
        P(None, None, "head"),
        P(None, "head", None),
        P("tok", None),
        P("tok"),
    )
    out_specs = P("tok", "head")
    body = functools.partial(shards, mesh.shape["head"], mesh.shape["tok"])
    return jax.shard_map(body, mesh=mesh, in_specs=in_specs, out_specs=out_specs, check_vma=False)
```

```python
import functools
import math

import jax
import jax.numpy as jnp
from jax import lax
from jax.experimental import pallas as pl
from jax.experimental.pallas import tpu as pltpu
from jax.sharding import PartitionSpec as P

HD = 128
VIEWS = 8
BLOCK = 128
LOG2_SCALE = math.log2(math.e) / math.sqrt(HD)
VMEM_BYTES = 60 * 1024 * 1024
CONTRACT_LAST = (((1,), (1,)), ((), ()))


def rms_rows(row_block, norm_gain):
    values = row_block.astype(jnp.float32)
    factor = lax.rsqrt(jnp.mean(values * values, axis=-1, keepdims=True) + 1e-06)
    return (values * factor * norm_gain).astype(jnp.bfloat16)


def f32_dot(left, right):
    return jnp.dot(left, right, preferred_element_type=jnp.float32)


def block_diagonal(tiles):
    rows = []
    for index, tile in enumerate(tiles):
        zero = jnp.zeros_like(tile)
        rows.append(
            jnp.concatenate([tile if k == index else zero for k in range(len(tiles))], axis=1)
        )
    return jnp.concatenate(rows, axis=0)


def ring_place(tok, n_tok):
    half = lax.div(tok, 2)
    return jnp.where(lax.rem(tok, 2) == 0, half, n_tok - 1 - half)


def cross_kernel(
    first_step, lists_ref, counts_ref, tok_ref, tokens_ref, gain_ref, wq_ref, wo_ref, *refs
):
    kv_refs = refs[:-5]
    out_ref, k_ref, vt_ref, q_ref, mixed_ref = refs[-5:]
    step = pl.program_id(0)
    rows, cols = mixed_ref.shape
    heads = cols // HD
    per_step = rows // BLOCK
    listed = lists_ref.shape[1]

    @pl.when(step == 0)
    def _():
        n_tok = len(kv_refs)
        for offset, kv_ref in enumerate(kv_refs):
            chunk = kv_ref.shape[0]
            place = lax.rem(ring_place(tok_ref[0], n_tok) + offset, n_tok)
            home = jnp.where(place < (n_tok + 1) // 2, 2 * place, 2 * (n_tok - 1 - place) + 1)
            start = pl.multiple_of(home * chunk, BLOCK)
            k_ref[pl.ds(start, chunk), :] = kv_ref[:, :cols]
            vt_ref[:, pl.ds(start, chunk)] = kv_ref[:, cols:].T

    normed = rms_rows(tokens_ref[...], gain_ref[...])
    q_ref[...] = (f32_dot(normed, wq_ref[...]) * LOG2_SCALE).astype(jnp.bfloat16)

    def one_block(local, carry):
        block = (first_step + step) * per_step + local
        row_start = pl.multiple_of(local * BLOCK, BLOCK)
        count = counts_ref[block]
        first = lists_ref[block, 0]
        starts = [
            pl.multiple_of(jnp.where(j < count, lists_ref[block, j], first) * BLOCK, BLOCK)
            for j in range(listed)
        ]
        query = block_diagonal(
            [q_ref[pl.ds(row_start, BLOCK), h * HD : (h + 1) * HD] for h in range(heads)]
        )
        keys = jnp.concatenate([k_ref[pl.ds(s, BLOCK), :] for s in starts], axis=0)
        scores = lax.dot_general(keys, query, CONTRACT_LAST, preferred_element_type=jnp.float32)
        top = jnp.max(scores, axis=0, keepdims=True)
        weights = []
        total = jnp.zeros_like(top)
        for j in range(listed):
            shift = top + jnp.where(j < count, 0.0, 1e30)
            weight = jnp.exp2(scores[j * BLOCK : (j + 1) * BLOCK] - shift)
            total = total + jnp.sum(weight, axis=0, keepdims=True)
            weights.append(weight.astype(jnp.bfloat16))
        values_t = jnp.concatenate([vt_ref[:, pl.ds(s, BLOCK)] for s in starts], axis=1)
        mixed_t = f32_dot(values_t, jnp.concatenate(weights, axis=0)) / total
        for h in range(heads):
            part = slice(h * HD, (h + 1) * HD)
            mixed_ref[pl.ds(row_start, BLOCK), part] = mixed_t[part, part].T.astype(jnp.bfloat16)
        return carry

    lax.fori_loop(0, per_step, one_block, 0, unroll=True)
    out_ref[...] = f32_dot(mixed_ref[...], wo_ref[0]).astype(jnp.bfloat16)


def cross_attention(
    hires_tokens, gain, w_cross_q, w_out, kv_chunks, block_lists, block_counts, part, parts
):
    tok_index = lax.axis_index("tok").reshape(1)
    tok_rows, width = hires_tokens.shape
    cols = w_cross_q.shape[1]
    chunk = kv_chunks[0].shape[0]
    low_rows = chunk * len(kv_chunks)
    tok_rows = tok_rows // parts
    rows = math.gcd(tok_rows, 4 * BLOCK)
    first = part * tok_rows // rows
    return pl.pallas_call(
        functools.partial(cross_kernel, first),
        out_shape=jax.ShapeDtypeStruct((tok_rows, width), jnp.bfloat16),
        grid_spec=pltpu.PrefetchScalarGridSpec(
            num_scalar_prefetch=3,
            grid=(tok_rows // rows,),
            in_specs=[
                pl.BlockSpec((rows, width), lambda i, *_: (first + i, 0)),
                pl.BlockSpec((1, width), lambda i, *_: (0, 0)),
                pl.BlockSpec((width, cols), lambda i, *_: (0, 0)),
                pl.BlockSpec((1, cols, width), lambda i, *_: (0, 0, 0)),
            ]
            + [pl.BlockSpec((chunk, 2 * cols), lambda i, *_: (0, 0)) for _ in kv_chunks],
            out_specs=pl.BlockSpec((rows, width), lambda i, *_: (i, 0)),
            scratch_shapes=[
                pltpu.VMEM((low_rows, cols), jnp.bfloat16),
                pltpu.VMEM((cols, low_rows), jnp.bfloat16),
                pltpu.VMEM((rows, cols), jnp.bfloat16),
                pltpu.VMEM((rows, cols), jnp.bfloat16),
            ],
        ),
        compiler_params=pltpu.CompilerParams(vmem_limit_bytes=VMEM_BYTES),
        cost_estimate=pl.CostEstimate(
            flops=2 * tok_rows * cols * (2 * width + 2 * block_lists.shape[1] * BLOCK * 2),
            bytes_accessed=4 * tok_rows * width,
            transcendentals=tok_rows * block_lists.shape[1] * BLOCK * (cols // HD),
        ),
        name="cross",
    )(block_lists, block_counts, tok_index, hires_tokens, gain, w_cross_q, w_out, *kv_chunks)


def view_kernel(
    tokens_ref, gain_ref, w_ref, wo_ref, out_ref, normed_ref, qkv_ref, mixed_ref
):
    parts, sources, run, cols = out_ref.shape
    part_index = pl.program_id(0)
    heads = cols // HD
    rows = sources * run
    pixels = rows // VIEWS
    group = math.gcd(pixels, 32)
    tile = math.gcd(rows, 256)

    @pl.when(pl.program_id(0) == 0)
    def _():
        gain = gain_ref[...]
        step = max(1, tile // run)
        for s in range(0, sources, step):
            tokens = tokens_ref[s : s + step].reshape(step * run, gain.shape[1])
            normed_ref[s * run : (s + step) * run] = rms_rows(tokens, gain)

    for start in range(0, rows, tile):
        stop = start + tile
        tokens = normed_ref[start:stop]
        for k in range(3):
            projected = f32_dot(tokens, w_ref[0, k])
            if k == 0:
                projected = projected * LOG2_SCALE
            qkv_ref[start:stop, k * cols : (k + 1) * cols] = projected.astype(jnp.bfloat16)
    size = VIEWS * group
    row_pixel = lax.broadcasted_iota(jnp.int32, (size, size), 0) % group
    col_pixel = lax.broadcasted_iota(jnp.int32, (size, size), 1) % group
    same = row_pixel == col_pixel

    def gathered(first, column):
        part = slice(column, column + HD)
        return jnp.concatenate(
            [qkv_ref[v * pixels + first : v * pixels + first + group, part] for v in range(VIEWS)],
            axis=0,
        )

    for first in range(0, pixels, group):
        for h in range(heads):
            query = gathered(first, h * HD)
            key = gathered(first, cols + h * HD)
            value = gathered(first, 2 * cols + h * HD)
            scores = lax.dot_general(query, key, CONTRACT_LAST, preferred_element_type=jnp.float32)
            scores = jnp.where(same, scores, -1e30)
            weight = jnp.exp2(scores - jnp.max(scores, axis=1, keepdims=True))
            total = jnp.sum(weight, axis=1, keepdims=True)
            mixed = (f32_dot(weight.astype(jnp.bfloat16), value) / total).astype(jnp.bfloat16)
            for v in range(VIEWS):
                rows_of = slice(v * pixels + first, v * pixels + first + group)
                mixed_ref[part_index, rows_of, h * HD : (h + 1) * HD] = (
                    mixed[v * group : (v + 1) * group]
                )

    @pl.when(part_index == parts - 1)
    def _():
        step = max(1, tile // run)
        for s in range(0, sources, step):
            rows_of = slice(s * run, (s + step) * run)
            for column in range(parts):
                w_rows = slice(column * cols, (column + 1) * cols)
                term = f32_dot(mixed_ref[0, rows_of], wo_ref[0, 0, w_rows])
                for g in range(1, parts):
                    term = term + f32_dot(mixed_ref[g, rows_of], wo_ref[g, 0, w_rows])
                out_ref[column, s : s + step] = term.astype(jnp.bfloat16).reshape(step, run, cols)


def view_attention(tokens, gain, weights):
    n_tok, run, width = tokens.shape
    parts, _, _, cols = weights.shape
    rows = n_tok * run
    return pl.pallas_call(
        view_kernel,
        out_shape=jax.ShapeDtypeStruct((parts, n_tok, run, cols), jnp.bfloat16),
        grid=(parts,),
        in_specs=[
            pl.BlockSpec((n_tok, run, width), lambda i: (0, 0, 0)),
            pl.BlockSpec((1, width), lambda i: (0, 0)),
            pl.BlockSpec((1, 3, width, cols), lambda i: (i, 0, 0, 0)),
            pl.BlockSpec((parts, 1, width, cols), lambda i: (0, 3, 0, 0)),
        ],
        out_specs=pl.BlockSpec((parts, n_tok, run, cols), lambda i: (0, 0, 0, 0)),
        scratch_shapes=[
            pltpu.VMEM((rows, width), jnp.bfloat16),
            pltpu.VMEM((rows, 3 * cols), jnp.bfloat16),
            pltpu.VMEM((parts, rows, cols), jnp.bfloat16),
        ],
        compiler_params=pltpu.CompilerParams(vmem_limit_bytes=VMEM_BYTES),
        cost_estimate=pl.CostEstimate(
            flops=2 * rows * (parts * cols * (3 * width + 512) + width * width),
            bytes_accessed=2 * (2 * rows * width + 4 * parts * width * cols),
            transcendentals=parts * rows * 512,
        ),
        name="view",
    )(tokens, gain, weights, weights)


def add_kernel(chunks, steps, n_parts, index_ref, tokens_ref, *refs):
    cross_refs, view_refs, out_ref = refs[:n_parts], refs[n_parts:-1], refs[-1]
    h, c = pl.program_id(0), pl.program_id(1)
    for part in range(n_parts):
        for chunk in range(chunks):
            @pl.when((lax.div(h, steps) == part) & (c == chunk))
            def _():
                terms = cross_refs[part][...].astype(jnp.float32)
                terms = terms + view_refs[chunk][0].astype(jnp.float32)
                out_ref[...] = (tokens_ref[...].astype(jnp.float32) + terms).astype(jnp.bfloat16)


def add_terms(head_index, hires_tokens, cross_terms, view_terms):
    cols = cross_terms[0].shape[1]
    n_head, rows, _ = view_terms[0].shape
    chunks, n_parts = len(view_terms), len(cross_terms)
    steps = n_head // n_parts
    cross_specs = [
        pl.BlockSpec(
            (rows, cols),
            lambda h, c, index, part=part: (
                jnp.clip(h * chunks + c - part * steps * chunks, 0, steps * chunks - 1), 0
            ),
        )
        for part in range(n_parts)
    ]
    view_spec = pl.BlockSpec((1, rows, cols), lambda h, c, index: (h, 0, 0))
    return pl.pallas_call(
        functools.partial(add_kernel, chunks, steps, n_parts),
        out_shape=jax.ShapeDtypeStruct((n_head * chunks * rows, cols), jnp.bfloat16),
        grid_spec=pltpu.PrefetchScalarGridSpec(
            num_scalar_prefetch=1,
            grid=(n_head, chunks),
            in_specs=[pl.BlockSpec((rows, cols), lambda h, c, index: (h * chunks + c, index[0]))]
            + cross_specs
            + [view_spec] * chunks,
            out_specs=pl.BlockSpec((rows, cols), lambda h, c, index: (h * chunks + c, 0)),
        ),
        compiler_params=pltpu.CompilerParams(vmem_limit_bytes=VMEM_BYTES),
        cost_estimate=pl.CostEstimate(
            flops=2 * n_head * chunks * rows * cols,
            bytes_accessed=8 * n_head * chunks * rows * cols,
            transcendentals=0,
        ),
        name="add",
    )(head_index.reshape(1), hires_tokens, *cross_terms, *view_terms)


def ring_chunks(own, n_tok):
    order = list(range(0, n_tok, 2)) + list(range(1, n_tok, 2))[::-1]
    upward = [(order[p], order[(p + 1) % n_tok]) for p in range(n_tok)]
    downward = [(order[p], order[p - 1]) for p in range(n_tok)]
    behind, ahead = [own], [own]
    for step in range(n_tok // 2):
        behind.append(lax.ppermute(behind[-1], "tok", upward))
        if step < (n_tok - 1) // 2:
            ahead.append(lax.ppermute(ahead[-1], "tok", downward))
    return ahead + behind[:0:-1]


def shards(
    n_head,
    n_tok,
    hires_tokens,
    lowres_tokens,
    norm_gain,
    w_cross_q,
    w_low_kv,
    w_view_qkv,
    w_out,
    block_lists,
    block_counts,
):
    tok_rows, width = hires_tokens.shape
    cols = w_cross_q.shape[1]
    quarter = tok_rows // n_head
    head_index = lax.axis_index("head")
    gain = norm_gain.reshape(1, width)

    run = quarter // n_tok
    chunks = 2 if run % 32 == 0 else 1
    run = run // chunks
    parts = 2 if n_head % 2 == 0 else 1

    low_kv = f32_dot(
        rms_rows(lowres_tokens, norm_gain), w_low_kv.reshape(width, 2 * cols)
    ).astype(jnp.bfloat16)
    own_weights = jnp.concatenate(
        [
            w_view_qkv.transpose(1, 0, 2),
            w_out[1].reshape(cols, n_head, cols).transpose(1, 0, 2).reshape(1, width, cols),
        ],
        axis=0,
    )
    weights = lax.all_gather(own_weights, "head", axis=0, tiled=False)
    kv_chunks = ring_chunks(low_kv, n_tok)

    rows_of_chunk = [
        lax.dynamic_slice_in_dim(
            hires_tokens, head_index * quarter + chunk * n_tok * run, n_tok * run, 0
        ).reshape(n_tok, run, width)
        for chunk in range(chunks)
    ]
    kv_chunks, rows_of_chunk = lax.optimization_barrier((kv_chunks, rows_of_chunk))

    def arrive(rows):
        return lax.all_to_all(rows, "tok", split_axis=0, concat_axis=0, tiled=True)

    arrived = [arrive(rows_of_chunk[0])]
    partials = []
    for part in range(parts):
        partials.append(
            cross_attention(
                hires_tokens, gain, w_cross_q, w_out, kv_chunks, block_lists, block_counts,
                part, parts,
            )
        )
    partials, arrived, rows_of_chunk = lax.optimization_barrier((partials, arrived, rows_of_chunk))
    arrived.extend(arrive(rows) for rows in rows_of_chunk[1:])
    partials, weights = lax.optimization_barrier((partials, weights))
    cross_terms = [
        lax.psum_scatter(partial, "head", scatter_dimension=1, tiled=True) for partial in partials
    ]
    view_terms = []
    for tokens in arrived:
        term = view_attention(tokens, gain, weights)
        term = lax.all_to_all(
            term.reshape(n_head * n_tok, run, cols),
            ("head", "tok"), split_axis=0, concat_axis=0, tiled=True,
        )
        view_terms.append(term.reshape(n_head, n_tok * run, cols))
    return add_terms(head_index, hires_tokens, cross_terms, view_terms)


def solution(mesh):
    in_specs = (
        P("tok", None),
        P("tok", None),
        P(),
        P(None, "head"),
        P(None, None, "head"),
        P(None, None, "head"),
        P(None, "head", None),
        P("tok", None),
        P("tok"),
    )
    out_specs = P("tok", "head")
    body = functools.partial(shards, mesh.shape["head"], mesh.shape["tok"])
    return jax.shard_map(body, mesh=mesh, in_specs=in_specs, out_specs=out_specs, check_vma=False)
```

```python
import functools
import math

import jax
import jax.numpy as jnp
from jax import lax
from jax.experimental import pallas as pl
from jax.experimental.pallas import tpu as pltpu
from jax.sharding import PartitionSpec as P

HD = 128
VIEWS = 8
BLOCK = 128
LOG2_SCALE = math.log2(math.e) / math.sqrt(HD)
VMEM_BYTES = 60 * 1024 * 1024
CONTRACT_LAST = (((1,), (1,)), ((), ()))


def rms_rows(row_block, norm_gain):
    values = row_block.astype(jnp.float32)
    factor = lax.rsqrt(jnp.mean(values * values, axis=-1, keepdims=True) + 1e-06)
    return (values * factor * norm_gain).astype(jnp.bfloat16)


def f32_dot(left, right):
    return jnp.dot(left, right, preferred_element_type=jnp.float32)


def block_diagonal(tiles):
    rows = []
    for index, tile in enumerate(tiles):
        zero = jnp.zeros_like(tile)
        rows.append(
            jnp.concatenate([tile if k == index else zero for k in range(len(tiles))], axis=1)
        )
    return jnp.concatenate(rows, axis=0)


def ring_place(tok, n_tok):
    half = lax.div(tok, 2)
    return jnp.where(lax.rem(tok, 2) == 0, half, n_tok - 1 - half)


def cross_kernel(lists_ref, counts_ref, tok_ref, tokens_ref, gain_ref, wq_ref, *refs):
    kv_refs = refs[:-4]
    out_ref, k_ref, vt_ref, q_ref = refs[-4:]
    step = pl.program_id(0)
    rows, cols = out_ref.shape
    heads = cols // HD
    per_step = rows // BLOCK
    listed = lists_ref.shape[1]

    @pl.when(step == 0)
    def _():
        n_tok = len(kv_refs)
        for offset, kv_ref in enumerate(kv_refs):
            chunk = kv_ref.shape[0]
            place = lax.rem(ring_place(tok_ref[0], n_tok) + offset, n_tok)
            home = jnp.where(place < (n_tok + 1) // 2, 2 * place, 2 * (n_tok - 1 - place) + 1)
            start = pl.multiple_of(home * chunk, BLOCK)
            k_ref[pl.ds(start, chunk), :] = kv_ref[:, :cols]
            vt_ref[:, pl.ds(start, chunk)] = kv_ref[:, cols:].T

    normed = rms_rows(tokens_ref[...], gain_ref[...])
    q_ref[...] = (f32_dot(normed, wq_ref[...]) * LOG2_SCALE).astype(jnp.bfloat16)

    def one_block(local, carry):
        block = step * per_step + local
        row_start = pl.multiple_of(local * BLOCK, BLOCK)
        count = counts_ref[block]
        first = lists_ref[block, 0]
        starts = [
            pl.multiple_of(jnp.where(j < count, lists_ref[block, j], first) * BLOCK, BLOCK)
            for j in range(listed)
        ]
        query = block_diagonal(
            [q_ref[pl.ds(row_start, BLOCK), h * HD : (h + 1) * HD] for h in range(heads)]
        )
        keys = jnp.concatenate([k_ref[pl.ds(s, BLOCK), :] for s in starts], axis=0)
        scores = lax.dot_general(keys, query, CONTRACT_LAST, preferred_element_type=jnp.float32)
        top = jnp.max(scores, axis=0, keepdims=True)
        weights = []
        total = jnp.zeros_like(top)
        for j in range(listed):
            shift = top + jnp.where(j < count, 0.0, 1e30)
            weight = jnp.exp2(scores[j * BLOCK : (j + 1) * BLOCK] - shift)
            total = total + jnp.sum(weight, axis=0, keepdims=True)
            weights.append(weight.astype(jnp.bfloat16))
        values_t = jnp.concatenate([vt_ref[:, pl.ds(s, BLOCK)] for s in starts], axis=1)
        mixed_t = f32_dot(values_t, jnp.concatenate(weights, axis=0)) / total
        for h in range(heads):
            part = slice(h * HD, (h + 1) * HD)
            out_ref[pl.ds(row_start, BLOCK), part] = mixed_t[part, part].T.astype(jnp.bfloat16)
        return carry

    lax.fori_loop(0, per_step, one_block, 0, unroll=True)


def cross_attention(hires_tokens, gain, w_cross_q, kv_chunks, block_lists, block_counts):
    tok_index = lax.axis_index("tok").reshape(1)
    tok_rows, width = hires_tokens.shape
    cols = w_cross_q.shape[1]
    chunk = kv_chunks[0].shape[0]
    low_rows = chunk * len(kv_chunks)
    rows = math.gcd(tok_rows, 4 * BLOCK)
    return pl.pallas_call(
        cross_kernel,
        out_shape=jax.ShapeDtypeStruct((tok_rows, cols), jnp.bfloat16),
        grid_spec=pltpu.PrefetchScalarGridSpec(
            num_scalar_prefetch=3,
            grid=(tok_rows // rows,),
            in_specs=[
                pl.BlockSpec((rows, width), lambda i, *_: (i, 0)),
                pl.BlockSpec((1, width), lambda i, *_: (0, 0)),
                pl.BlockSpec((width, cols), lambda i, *_: (0, 0)),
            ]
            + [pl.BlockSpec((chunk, 2 * cols), lambda i, *_: (0, 0)) for _ in kv_chunks],
            out_specs=pl.BlockSpec((rows, cols), lambda i, *_: (i, 0)),
            scratch_shapes=[
                pltpu.VMEM((low_rows, cols), jnp.bfloat16),
                pltpu.VMEM((cols, low_rows), jnp.bfloat16),
                pltpu.VMEM((rows, cols), jnp.bfloat16),
            ],
        ),
        compiler_params=pltpu.CompilerParams(vmem_limit_bytes=VMEM_BYTES),
        cost_estimate=pl.CostEstimate(
            flops=2 * tok_rows * cols * (width + 2 * block_lists.shape[1] * BLOCK * 2),
            bytes_accessed=2 * tok_rows * (width + cols),
            transcendentals=tok_rows * block_lists.shape[1] * BLOCK * (cols // HD),
        ),
        name="cross",
    )(block_lists, block_counts, tok_index, hires_tokens, gain, w_cross_q, *kv_chunks)


def view_kernel(
    tokens_ref, gain_ref, w_ref, wo_ref, out_ref, normed_ref, qkv_ref, mixed_ref
):
    parts, sources, run, cols = out_ref.shape
    part_index = pl.program_id(0)
    heads = cols // HD
    rows = sources * run
    pixels = rows // VIEWS
    group = math.gcd(pixels, 32)
    tile = math.gcd(rows, 256)

    @pl.when(pl.program_id(0) == 0)
    def _():
        gain = gain_ref[...]
        step = max(1, tile // run)
        for s in range(0, sources, step):
            tokens = tokens_ref[s : s + step].reshape(step * run, gain.shape[1])
            normed_ref[s * run : (s + step) * run] = rms_rows(tokens, gain)

    for start in range(0, rows, tile):
        stop = start + tile
        tokens = normed_ref[start:stop]
        for k in range(3):
            projected = f32_dot(tokens, w_ref[0, k])
            if k == 0:
                projected = projected * LOG2_SCALE
            qkv_ref[start:stop, k * cols : (k + 1) * cols] = projected.astype(jnp.bfloat16)
    size = VIEWS * group
    row_pixel = lax.broadcasted_iota(jnp.int32, (size, size), 0) % group
    col_pixel = lax.broadcasted_iota(jnp.int32, (size, size), 1) % group
    same = row_pixel == col_pixel

    def gathered(first, column):
        part = slice(column, column + HD)
        return jnp.concatenate(
            [qkv_ref[v * pixels + first : v * pixels + first + group, part] for v in range(VIEWS)],
            axis=0,
        )

    for first in range(0, pixels, group):
        for h in range(heads):
            query = gathered(first, h * HD)
            key = gathered(first, cols + h * HD)
            value = gathered(first, 2 * cols + h * HD)
            scores = lax.dot_general(query, key, CONTRACT_LAST, preferred_element_type=jnp.float32)
            scores = jnp.where(same, scores, -1e30)
            weight = jnp.exp2(scores - jnp.max(scores, axis=1, keepdims=True))
            total = jnp.sum(weight, axis=1, keepdims=True)
            mixed = (f32_dot(weight.astype(jnp.bfloat16), value) / total).astype(jnp.bfloat16)
            for v in range(VIEWS):
                rows_of = slice(v * pixels + first, v * pixels + first + group)
                mixed_ref[part_index, rows_of, h * HD : (h + 1) * HD] = (
                    mixed[v * group : (v + 1) * group]
                )

    @pl.when(part_index == parts - 1)
    def _():
        step = max(1, tile // run)
        for s in range(0, sources, step):
            rows_of = slice(s * run, (s + step) * run)
            for column in range(parts):
                w_rows = slice(column * cols, (column + 1) * cols)
                term = f32_dot(mixed_ref[0, rows_of], wo_ref[0, 0, w_rows])
                for g in range(1, parts):
                    term = term + f32_dot(mixed_ref[g, rows_of], wo_ref[g, 0, w_rows])
                out_ref[column, s : s + step] = term.astype(jnp.bfloat16).reshape(step, run, cols)


def view_attention(tokens, gain, weights):
    n_tok, run, width = tokens.shape
    parts, _, _, cols = weights.shape
    rows = n_tok * run
    return pl.pallas_call(
        view_kernel,
        out_shape=jax.ShapeDtypeStruct((parts, n_tok, run, cols), jnp.bfloat16),
        grid=(parts,),
        in_specs=[
            pl.BlockSpec((n_tok, run, width), lambda i: (0, 0, 0)),
            pl.BlockSpec((1, width), lambda i: (0, 0)),
            pl.BlockSpec((1, 3, width, cols), lambda i: (i, 0, 0, 0)),
            pl.BlockSpec((parts, 1, width, cols), lambda i: (0, 3, 0, 0)),
        ],
        out_specs=pl.BlockSpec((parts, n_tok, run, cols), lambda i: (0, 0, 0, 0)),
        scratch_shapes=[
            pltpu.VMEM((rows, width), jnp.bfloat16),
            pltpu.VMEM((rows, 3 * cols), jnp.bfloat16),
            pltpu.VMEM((parts, rows, cols), jnp.bfloat16),
        ],
        compiler_params=pltpu.CompilerParams(vmem_limit_bytes=VMEM_BYTES),
        cost_estimate=pl.CostEstimate(
            flops=2 * rows * (parts * cols * (3 * width + 512) + width * width),
            bytes_accessed=2 * (2 * rows * width + 4 * parts * width * cols),
            transcendentals=parts * rows * 512,
        ),
        name="view",
    )(tokens, gain, weights, weights)


def final_kernel(chunks, index_ref, tokens_ref, cross_ref, *refs):
    view_refs, w_refs, out_ref = refs[:chunks], refs[chunks:-1], refs[-1]
    parts = len(w_refs)
    total = tokens_ref[...].astype(jnp.float32)
    for k, w_ref in enumerate(w_refs):
        group = lax.rem(index_ref[0] + parts - k, parts)
        total = total + f32_dot(cross_ref[group], w_ref[...])
    for chunk, view_ref in enumerate(view_refs):
        @pl.when(pl.program_id(1) == chunk)
        def _():
            out_ref[...] = (total + view_ref[0].astype(jnp.float32)).astype(jnp.bfloat16)


def final_sum(head_index, hires_tokens, cross_all, view_terms, w_columns):
    parts, tok_rows, cols = cross_all.shape
    n_head, rows, _ = view_terms[0].shape
    chunks = len(view_terms)
    view_spec = pl.BlockSpec((1, rows, cols), lambda h, c, index: (h, 0, 0))
    w_spec = pl.BlockSpec((cols, cols), lambda h, c, index: (0, 0))
    return pl.pallas_call(
        functools.partial(final_kernel, chunks),
        out_shape=jax.ShapeDtypeStruct((tok_rows, cols), jnp.bfloat16),
        grid_spec=pltpu.PrefetchScalarGridSpec(
            num_scalar_prefetch=1,
            grid=(n_head, chunks),
            in_specs=[
                pl.BlockSpec((rows, cols), lambda h, c, index: (h * chunks + c, index[0])),
                pl.BlockSpec((parts, rows, cols), lambda h, c, index: (0, h * chunks + c, 0)),
            ]
            + [view_spec] * chunks
            + [w_spec] * parts,
            out_specs=pl.BlockSpec((rows, cols), lambda h, c, index: (h * chunks + c, 0)),
        ),
        compiler_params=pltpu.CompilerParams(vmem_limit_bytes=VMEM_BYTES),
        cost_estimate=pl.CostEstimate(
            flops=2 * parts * tok_rows * cols * cols,
            bytes_accessed=2 * tok_rows * cols * (parts + 3),
            transcendentals=0,
        ),
        name="final",
    )(head_index.reshape(1), hires_tokens, cross_all, *view_terms, *w_columns)


def column_blocks(rows_of_w, head_index, n_head):
    cols = rows_of_w.shape[1] // n_head
    blocks = []
    for k in range(n_head):
        start = lax.rem(head_index + k, n_head) * cols
        block = lax.dynamic_slice_in_dim(rows_of_w, start, cols, 1)
        if k:
            pairs = [(h, (h + k) % n_head) for h in range(n_head)]
            block = lax.ppermute(block, "head", pairs)
        blocks.append(block)
    return blocks


def ring_chunks(own, n_tok):
    order = list(range(0, n_tok, 2)) + list(range(1, n_tok, 2))[::-1]
    upward = [(order[p], order[(p + 1) % n_tok]) for p in range(n_tok)]
    downward = [(order[p], order[p - 1]) for p in range(n_tok)]
    behind, ahead = [own], [own]
    for step in range(n_tok // 2):
        behind.append(lax.ppermute(behind[-1], "tok", upward))
        if step < (n_tok - 1) // 2:
            ahead.append(lax.ppermute(ahead[-1], "tok", downward))
    return ahead + behind[:0:-1]


def shards(
    n_head,
    n_tok,
    hires_tokens,
    lowres_tokens,
    norm_gain,
    w_cross_q,
    w_low_kv,
    w_view_qkv,
    w_out,
    block_lists,
    block_counts,
):
    tok_rows, width = hires_tokens.shape
    cols = w_cross_q.shape[1]
    quarter = tok_rows // n_head
    head_index = lax.axis_index("head")
    gain = norm_gain.reshape(1, width)

    run = quarter // n_tok
    chunks = 2 if run % 32 == 0 else 1
    run = run // chunks

    own_weights = jnp.concatenate(
        [
            w_view_qkv.transpose(1, 0, 2),
            w_out[1].reshape(cols, n_head, cols).transpose(1, 0, 2).reshape(1, width, cols),
        ],
        axis=0,
    )
    weights = lax.all_gather(own_weights, "head", axis=0, tiled=False)
    low_kv = f32_dot(
        rms_rows(lowres_tokens, norm_gain), w_low_kv.reshape(width, 2 * cols)
    ).astype(jnp.bfloat16)
    kv_chunks = ring_chunks(low_kv, n_tok)
    w_columns = column_blocks(w_out[0], head_index, n_head)
    sent = [
        lax.dynamic_slice_in_dim(
            hires_tokens, head_index * quarter + chunk * n_tok * run, n_tok * run, 0
        ).reshape(n_tok, run, width)
        for chunk in range(chunks)
    ]
    kv_chunks, sent, w_columns = lax.optimization_barrier((kv_chunks, sent, w_columns))

    def arrive(rows):
        return lax.all_to_all(rows, "tok", split_axis=0, concat_axis=0, tiled=True)

    arrived = [arrive(sent[0])]
    cross_out = cross_attention(
        hires_tokens, gain, w_cross_q, kv_chunks, block_lists, block_counts
    )
    cross_out, arrived, sent = lax.optimization_barrier((cross_out, arrived, sent))
    cross_all = lax.all_gather(cross_out, "head", axis=0, tiled=False)
    arrived.extend(arrive(rows) for rows in sent[1:])
    view_terms = []
    for tokens in arrived:
        term = view_attention(tokens, gain, weights)
        term = lax.all_to_all(
            term.reshape(n_head * n_tok, run, cols),
            ("head", "tok"), split_axis=0, concat_axis=0, tiled=True,
        )
        view_terms.append(term.reshape(n_head, n_tok * run, cols))
    return final_sum(head_index, hires_tokens, cross_all, view_terms, w_columns)


def solution(mesh):
    in_specs = (
        P("tok", None),
        P("tok", None),
        P(),
        P(None, "head"),
        P(None, None, "head"),
        P(None, None, "head"),
        P(None, "head", None),
        P("tok", None),
        P("tok"),
    )
    out_specs = P("tok", "head")
    body = functools.partial(shards, mesh.shape["head"], mesh.shape["tok"])
    return jax.shard_map(body, mesh=mesh, in_specs=in_specs, out_specs=out_specs, check_vma=False)
```

```python
import functools
import math

import jax
import jax.numpy as jnp
from jax import lax
from jax.experimental import pallas as pl
from jax.experimental.pallas import tpu as pltpu
from jax.sharding import PartitionSpec as P

HD = 128
VIEWS = 8
BLOCK = 128
LOG2_SCALE = math.log2(math.e) / math.sqrt(HD)
VMEM_BYTES = 60 * 1024 * 1024
CONTRACT_LAST = (((1,), (1,)), ((), ()))


def rms_rows(row_block, norm_gain):
    values = row_block.astype(jnp.float32)
    factor = lax.rsqrt(jnp.mean(values * values, axis=-1, keepdims=True) + 1e-06)
    return (values * factor * norm_gain).astype(jnp.bfloat16)


def f32_dot(left, right):
    return jnp.dot(left, right, preferred_element_type=jnp.float32)


def block_diagonal(tiles):
    rows = []
    for index, tile in enumerate(tiles):
        zero = jnp.zeros_like(tile)
        rows.append(
            jnp.concatenate([tile if k == index else zero for k in range(len(tiles))], axis=1)
        )
    return jnp.concatenate(rows, axis=0)


def ring_place(tok, n_tok):
    half = lax.div(tok, 2)
    return jnp.where(lax.rem(tok, 2) == 0, half, n_tok - 1 - half)


def cross_kernel(halves, lists_ref, counts_ref, tok_ref, tokens_ref, gain_ref, wq_ref, *refs):
    kv_refs, out_refs = refs[: -4 - halves], refs[-4 - halves : -4]
    k_ref, vt_ref, q_ref, mixed_ref = refs[-4:]
    step = pl.program_id(0)
    rows, cols = mixed_ref.shape
    heads = cols // HD
    per_step = rows // BLOCK
    listed = lists_ref.shape[1]

    @pl.when(step == 0)
    def _():
        n_tok = len(kv_refs)
        for offset, kv_ref in enumerate(kv_refs):
            chunk = kv_ref.shape[0]
            place = lax.rem(ring_place(tok_ref[0], n_tok) + offset, n_tok)
            home = jnp.where(place < (n_tok + 1) // 2, 2 * place, 2 * (n_tok - 1 - place) + 1)
            start = pl.multiple_of(home * chunk, BLOCK)
            k_ref[pl.ds(start, chunk), :] = kv_ref[:, :cols]
            vt_ref[:, pl.ds(start, chunk)] = kv_ref[:, cols:].T

    normed = rms_rows(tokens_ref[...], gain_ref[...])
    q_ref[...] = (f32_dot(normed, wq_ref[...]) * LOG2_SCALE).astype(jnp.bfloat16)

    def one_block(local, carry):
        block = step * per_step + local
        row_start = pl.multiple_of(local * BLOCK, BLOCK)
        count = counts_ref[block]
        first = lists_ref[block, 0]
        starts = [
            pl.multiple_of(jnp.where(j < count, lists_ref[block, j], first) * BLOCK, BLOCK)
            for j in range(listed)
        ]
        query = block_diagonal(
            [q_ref[pl.ds(row_start, BLOCK), h * HD : (h + 1) * HD] for h in range(heads)]
        )
        keys = jnp.concatenate([k_ref[pl.ds(s, BLOCK), :] for s in starts], axis=0)
        scores = lax.dot_general(keys, query, CONTRACT_LAST, preferred_element_type=jnp.float32)
        top = jnp.max(scores, axis=0, keepdims=True)
        weights = []
        total = jnp.zeros_like(top)
        for j in range(listed):
            shift = top + jnp.where(j < count, 0.0, 1e30)
            weight = jnp.exp2(scores[j * BLOCK : (j + 1) * BLOCK] - shift)
            total = total + jnp.sum(weight, axis=0, keepdims=True)
            weights.append(weight.astype(jnp.bfloat16))
        values_t = jnp.concatenate([vt_ref[:, pl.ds(s, BLOCK)] for s in starts], axis=1)
        mixed_t = f32_dot(values_t, jnp.concatenate(weights, axis=0)) / total
        for h in range(heads):
            part = slice(h * HD, (h + 1) * HD)
            mixed_ref[pl.ds(row_start, BLOCK), part] = mixed_t[part, part].T.astype(jnp.bfloat16)
        return carry

    lax.fori_loop(0, per_step, one_block, 0, unroll=True)
    half_steps = pl.num_programs(0) // halves
    for half, out_ref in enumerate(out_refs):
        @pl.when(lax.div(step, half_steps) == half)
        def _():
            out_ref[...] = mixed_ref[...]


def cross_attention(hires_tokens, gain, w_cross_q, kv_chunks, block_lists, block_counts):
    tok_index = lax.axis_index("tok").reshape(1)
    tok_rows, width = hires_tokens.shape
    cols = w_cross_q.shape[1]
    chunk = kv_chunks[0].shape[0]
    low_rows = chunk * len(kv_chunks)
    halves = 2 if tok_rows % (2 * BLOCK) == 0 else 1
    rows = math.gcd(tok_rows // halves, 4 * BLOCK)
    half_steps = tok_rows // halves // rows
    return pl.pallas_call(
        functools.partial(cross_kernel, halves),
        out_shape=[jax.ShapeDtypeStruct((tok_rows // halves, cols), jnp.bfloat16)] * halves,
        grid_spec=pltpu.PrefetchScalarGridSpec(
            num_scalar_prefetch=3,
            grid=(tok_rows // rows,),
            in_specs=[
                pl.BlockSpec((rows, width), lambda i, *_: (i, 0)),
                pl.BlockSpec((1, width), lambda i, *_: (0, 0)),
                pl.BlockSpec((width, cols), lambda i, *_: (0, 0)),
            ]
            + [pl.BlockSpec((chunk, 2 * cols), lambda i, *_: (0, 0)) for _ in kv_chunks],
            out_specs=[
                pl.BlockSpec(
                    (rows, cols),
                    lambda i, *_, half=half: (jnp.clip(i - half * half_steps, 0, half_steps - 1), 0),
                )
                for half in range(halves)
            ],
            scratch_shapes=[
                pltpu.VMEM((low_rows, cols), jnp.bfloat16),
                pltpu.VMEM((cols, low_rows), jnp.bfloat16),
                pltpu.VMEM((rows, cols), jnp.bfloat16),
                pltpu.VMEM((rows, cols), jnp.bfloat16),
            ],
        ),
        compiler_params=pltpu.CompilerParams(vmem_limit_bytes=VMEM_BYTES),
        cost_estimate=pl.CostEstimate(
            flops=2 * tok_rows * cols * (width + 2 * block_lists.shape[1] * BLOCK * 2),
            bytes_accessed=2 * tok_rows * (width + cols),
            transcendentals=tok_rows * block_lists.shape[1] * BLOCK * (cols // HD),
        ),
        name="cross",
    )(block_lists, block_counts, tok_index, hires_tokens, gain, w_cross_q, *kv_chunks)


def view_kernel(
    first_row, tokens_ref, gain_ref, w_ref, wo_ref, out_ref, normed_ref, qkv_ref, mixed_ref
):
    parts, sources, run, cols = out_ref.shape
    part_index = pl.program_id(0)
    heads = cols // HD
    rows = sources * run
    pixels = rows // VIEWS
    group = math.gcd(pixels, 32)
    tile = math.gcd(rows, 256)

    @pl.when(pl.program_id(0) == 0)
    def _():
        gain = gain_ref[...]
        step = math.gcd(sources, max(1, tile // run))
        for s in range(0, sources, step):
            tokens = tokens_ref[s : s + step, first_row : first_row + run]
            tokens = tokens.reshape(step * run, gain.shape[1])
            normed_ref[s * run : (s + step) * run] = rms_rows(tokens, gain)

    for start in range(0, rows, tile):
        stop = start + tile
        tokens = normed_ref[start:stop]
        for k in range(3):
            projected = f32_dot(tokens, w_ref[0, k])
            if k == 0:
                projected = projected * LOG2_SCALE
            qkv_ref[start:stop, k * cols : (k + 1) * cols] = projected.astype(jnp.bfloat16)
    size = VIEWS * group
    row_pixel = lax.broadcasted_iota(jnp.int32, (size, size), 0) % group
    col_pixel = lax.broadcasted_iota(jnp.int32, (size, size), 1) % group
    same = row_pixel == col_pixel

    def gathered(first, column):
        part = slice(column, column + HD)
        return jnp.concatenate(
            [qkv_ref[v * pixels + first : v * pixels + first + group, part] for v in range(VIEWS)],
            axis=0,
        )

    for first in range(0, pixels, group):
        for h in range(heads):
            query = gathered(first, h * HD)
            key = gathered(first, cols + h * HD)
            value = gathered(first, 2 * cols + h * HD)
            scores = lax.dot_general(query, key, CONTRACT_LAST, preferred_element_type=jnp.float32)
            scores = jnp.where(same, scores, -1e30)
            weight = jnp.exp2(scores - jnp.max(scores, axis=1, keepdims=True))
            total = jnp.sum(weight, axis=1, keepdims=True)
            mixed = (f32_dot(weight.astype(jnp.bfloat16), value) / total).astype(jnp.bfloat16)
            for v in range(VIEWS):
                rows_of = slice(v * pixels + first, v * pixels + first + group)
                mixed_ref[part_index, rows_of, h * HD : (h + 1) * HD] = (
                    mixed[v * group : (v + 1) * group]
                )

    @pl.when(part_index == parts - 1)
    def _():
        step = math.gcd(sources, max(1, tile // run))
        for s in range(0, sources, step):
            rows_of = slice(s * run, (s + step) * run)
            for column in range(parts):
                w_rows = slice(column * cols, (column + 1) * cols)
                term = f32_dot(mixed_ref[0, rows_of], wo_ref[0, 0, w_rows])
                for g in range(1, parts):
                    term = term + f32_dot(mixed_ref[g, rows_of], wo_ref[g, 0, w_rows])
                out_ref[column, s : s + step] = term.astype(jnp.bfloat16).reshape(step, run, cols)


def view_attention(tokens, gain, weights, first_row, run):
    n_tok, whole_run, width = tokens.shape
    parts, _, _, cols = weights.shape
    rows = n_tok * run
    return pl.pallas_call(
        functools.partial(view_kernel, first_row),
        out_shape=jax.ShapeDtypeStruct((parts, n_tok, run, cols), jnp.bfloat16),
        grid=(parts,),
        in_specs=[
            pl.BlockSpec((n_tok, whole_run, width), lambda i: (0, 0, 0)),
            pl.BlockSpec((1, width), lambda i: (0, 0)),
            pl.BlockSpec((1, 3, width, cols), lambda i: (i, 0, 0, 0)),
            pl.BlockSpec((parts, 1, width, cols), lambda i: (0, 3, 0, 0)),
        ],
        out_specs=pl.BlockSpec((parts, n_tok, run, cols), lambda i: (0, 0, 0, 0)),
        scratch_shapes=[
            pltpu.VMEM((rows, width), jnp.bfloat16),
            pltpu.VMEM((rows, 3 * cols), jnp.bfloat16),
            pltpu.VMEM((parts, rows, cols), jnp.bfloat16),
        ],
        compiler_params=pltpu.CompilerParams(vmem_limit_bytes=VMEM_BYTES),
        cost_estimate=pl.CostEstimate(
            flops=2 * rows * (parts * cols * (3 * width + 512) + width * width),
            bytes_accessed=2 * (2 * rows * width + 4 * parts * width * cols),
            transcendentals=parts * rows * 512,
        ),
        name="view",
    )(tokens, gain, weights, weights)


def final_kernel(bounds, halves, index_ref, tokens_ref, *refs):
    chunks = len(bounds) - 1
    cross_refs, view_refs = refs[:halves], refs[halves : halves + chunks]
    w_refs, out_ref = refs[halves + chunks : -1], refs[-1]
    parts = len(w_refs)
    sources, run, cols = out_ref.shape
    half_steps = pl.num_programs(0) // halves
    for half, cross_ref in enumerate(cross_refs):
        @pl.when(lax.div(pl.program_id(0), half_steps) == half)
        def _():
            total = tokens_ref[...].reshape(sources * run, cols).astype(jnp.float32)
            for k, w_ref in enumerate(w_refs):
                group = lax.rem(index_ref[0] + parts - k, parts)
                total = total + f32_dot(cross_ref[group].reshape(sources * run, cols), w_ref[...])
            total = total.reshape(sources, run, cols)
            for view_ref, low, high in zip(view_refs, bounds, bounds[1:]):
                terms = total[:, low:high] + view_ref[...].astype(jnp.float32)
                out_ref[:, low:high] = terms.astype(jnp.bfloat16)


def final_sum(head_index, hires_tokens, cross_all, view_terms, w_columns, bounds):
    halves = len(cross_all)
    parts, half_rows, cols = cross_all[0].shape
    tok_rows = half_rows * halves
    width = hires_tokens.shape[1]
    places, run = view_terms[0].shape[0], bounds[-1]
    sources = math.gcd(places // halves, 4)
    half_steps = places // halves // sources
    w_spec = pl.BlockSpec((cols, cols), lambda i, index: (0, 0))
    out = pl.pallas_call(
        functools.partial(final_kernel, bounds, halves),
        out_shape=jax.ShapeDtypeStruct((places, run, cols), jnp.bfloat16),
        grid_spec=pltpu.PrefetchScalarGridSpec(
            num_scalar_prefetch=1,
            grid=(places // sources,),
            in_specs=[
                pl.BlockSpec((sources, run, cols), lambda i, index: (i, 0, index[0])),
            ]
            + [
                pl.BlockSpec(
                    (parts, sources, run, cols),
                    lambda i, index, half=half: (
                        0, jnp.clip(i - half * half_steps, 0, half_steps - 1), 0, 0
                    ),
                )
                for half in range(halves)
            ]
            + [
                pl.BlockSpec((sources, term.shape[1], cols), lambda i, index: (i, 0, 0))
                for term in view_terms
            ]
            + [w_spec] * parts,
            out_specs=pl.BlockSpec((sources, run, cols), lambda i, index: (i, 0, 0)),
        ),
        compiler_params=pltpu.CompilerParams(vmem_limit_bytes=VMEM_BYTES),
        cost_estimate=pl.CostEstimate(
            flops=2 * parts * tok_rows * cols * cols,
            bytes_accessed=2 * tok_rows * cols * (parts + 3),
            transcendentals=0,
        ),
        name="final",
    )(
        head_index.reshape(1),
        hires_tokens.reshape(places, run, width),
        *[half.reshape(parts, places // halves, run, cols) for half in cross_all],
        *view_terms,
        *w_columns,
    )
    return out.reshape(tok_rows, cols)


def column_blocks(rows_of_w, head_index, n_head):
    cols = rows_of_w.shape[1] // n_head
    return [
        lax.dynamic_slice_in_dim(rows_of_w, lax.rem(head_index + k, n_head) * cols, cols, 1)
        for k in range(n_head)
    ]


def send_blocks(blocks):
    n_head = len(blocks)
    return [
        lax.ppermute(block, "head", [(h, (h + k) % n_head) for h in range(n_head)]) if k else block
        for k, block in enumerate(blocks)
    ]


def ring_chunks(own, n_tok):
    order = list(range(0, n_tok, 2)) + list(range(1, n_tok, 2))[::-1]
    upward = [(order[p], order[(p + 1) % n_tok]) for p in range(n_tok)]
    downward = [(order[p], order[p - 1]) for p in range(n_tok)]
    behind, ahead = [own], [own]
    for step in range(n_tok // 2):
        behind.append(lax.ppermute(behind[-1], "tok", upward))
        if step < (n_tok - 1) // 2:
            ahead.append(lax.ppermute(ahead[-1], "tok", downward))
    return ahead + behind[:0:-1]


def shards(
    n_head,
    n_tok,
    hires_tokens,
    lowres_tokens,
    norm_gain,
    w_cross_q,
    w_low_kv,
    w_view_qkv,
    w_out,
    block_lists,
    block_counts,
):
    tok_rows, width = hires_tokens.shape
    cols = w_cross_q.shape[1]
    quarter = tok_rows // n_head
    head_index = lax.axis_index("head")
    gain = norm_gain.reshape(1, width)

    run = quarter // n_tok
    bounds = (0, run // 4, run) if run % 64 == 0 else (0, run)

    own_weights = jnp.concatenate(
        [
            w_view_qkv.transpose(1, 0, 2),
            w_out[1].reshape(cols, n_head, cols).transpose(1, 0, 2).reshape(1, width, cols),
        ],
        axis=0,
    )
    weights = lax.all_gather(own_weights, "head", axis=0, tiled=False)
    low_kv = f32_dot(
        rms_rows(lowres_tokens, norm_gain), w_low_kv.reshape(width, 2 * cols)
    ).astype(jnp.bfloat16)
    kv_chunks = ring_chunks(low_kv, n_tok)
    w_columns = column_blocks(w_out[0], head_index, n_head)
    sent = lax.dynamic_slice_in_dim(hires_tokens, head_index * quarter, quarter, 0)
    kv_chunks, sent, w_columns = lax.optimization_barrier((kv_chunks, sent, w_columns))

    arrived = lax.all_to_all(
        sent.reshape(n_tok, run, width), "tok", split_axis=0, concat_axis=0, tiled=True
    )
    cross_out = cross_attention(
        hires_tokens, gain, w_cross_q, kv_chunks, block_lists, block_counts
    )
    w_columns = send_blocks(w_columns)
    arrived, w_columns, last_half = lax.optimization_barrier((arrived, w_columns, cross_out[-1]))
    cross_all = [
        lax.all_gather(half, "head", axis=0, tiled=False) for half in [*cross_out[:-1], last_half]
    ]
    view_terms = []
    for low, high in zip(bounds, bounds[1:]):
        term = view_attention(arrived, gain, weights, low, high - low)
        view_terms.append(
            lax.all_to_all(
                term.reshape(n_head * n_tok, high - low, cols),
                ("head", "tok"), split_axis=0, concat_axis=0, tiled=True,
            )
        )
    return final_sum(head_index, hires_tokens, cross_all, view_terms, w_columns, bounds)


def solution(mesh):
    in_specs = (
        P("tok", None),
        P("tok", None),
        P(),
        P(None, "head"),
        P(None, None, "head"),
        P(None, None, "head"),
        P(None, "head", None),
        P("tok", None),
        P("tok"),
    )
    out_specs = P("tok", "head")
    body = functools.partial(shards, mesh.shape["head"], mesh.shape["tok"])
    return jax.shard_map(body, mesh=mesh, in_specs=in_specs, out_specs=out_specs, check_vma=False)
```

```python
import functools
import math

import jax
import jax.numpy as jnp
from jax import lax
from jax.experimental import pallas as pl
from jax.experimental.pallas import tpu as pltpu
from jax.sharding import PartitionSpec as P

HD = 128
VIEWS = 8
BLOCK = 128
LOG2_SCALE = math.log2(math.e) / math.sqrt(HD)
VMEM_BYTES = 60 * 1024 * 1024
CONTRACT_LAST = (((1,), (1,)), ((), ()))


def rms_rows(row_block, norm_gain):
    values = row_block.astype(jnp.float32)
    factor = lax.rsqrt(jnp.mean(values * values, axis=-1, keepdims=True) + 1e-06)
    return (values * factor * norm_gain).astype(jnp.bfloat16)


def f32_dot(left, right):
    return jnp.dot(left, right, preferred_element_type=jnp.float32)


def block_diagonal(tiles):
    rows = []
    for index, tile in enumerate(tiles):
        zero = jnp.zeros_like(tile)
        rows.append(
            jnp.concatenate([tile if k == index else zero for k in range(len(tiles))], axis=1)
        )
    return jnp.concatenate(rows, axis=0)


def ring_place(tok, n_tok):
    half = lax.div(tok, 2)
    return jnp.where(lax.rem(tok, 2) == 0, half, n_tok - 1 - half)


def cross_kernel(halves, lists_ref, counts_ref, tok_ref, tokens_ref, gain_ref, wq_ref, *refs):
    kv_refs, out_refs = refs[: -4 - halves], refs[-4 - halves : -4]
    k_ref, vt_ref, q_ref, mixed_ref = refs[-4:]
    step = pl.program_id(0)
    rows, cols = mixed_ref.shape
    heads = cols // HD
    per_step = rows // BLOCK
    listed = lists_ref.shape[1]

    @pl.when(step == 0)
    def _():
        n_tok = len(kv_refs)
        for offset, kv_ref in enumerate(kv_refs):
            chunk = kv_ref.shape[0]
            place = lax.rem(ring_place(tok_ref[0], n_tok) + offset, n_tok)
            home = jnp.where(place < (n_tok + 1) // 2, 2 * place, 2 * (n_tok - 1 - place) + 1)
            start = pl.multiple_of(home * chunk, BLOCK)
            k_ref[pl.ds(start, chunk), :] = kv_ref[:, :cols]
            vt_ref[:, pl.ds(start, chunk)] = kv_ref[:, cols:].T

    normed = rms_rows(tokens_ref[...], gain_ref[...])
    q_ref[...] = (f32_dot(normed, wq_ref[...]) * LOG2_SCALE).astype(jnp.bfloat16)

    def one_block(local, carry):
        block = step * per_step + local
        row_start = pl.multiple_of(local * BLOCK, BLOCK)
        count = counts_ref[block]
        first = lists_ref[block, 0]
        starts = [
            pl.multiple_of(jnp.where(j < count, lists_ref[block, j], first) * BLOCK, BLOCK)
            for j in range(listed)
        ]
        query = block_diagonal(
            [q_ref[pl.ds(row_start, BLOCK), h * HD : (h + 1) * HD] for h in range(heads)]
        )
        keys = jnp.concatenate([k_ref[pl.ds(s, BLOCK), :] for s in starts], axis=0)
        scores = lax.dot_general(keys, query, CONTRACT_LAST, preferred_element_type=jnp.float32)
        top = jnp.max(scores, axis=0, keepdims=True)
        weights = []
        total = jnp.zeros_like(top)
        for j in range(listed):
            shift = top + jnp.where(j < count, 0.0, 1e30)
            weight = jnp.exp2(scores[j * BLOCK : (j + 1) * BLOCK] - shift)
            total = total + jnp.sum(weight, axis=0, keepdims=True)
            weights.append(weight.astype(jnp.bfloat16))
        values_t = jnp.concatenate([vt_ref[:, pl.ds(s, BLOCK)] for s in starts], axis=1)
        mixed_t = f32_dot(values_t, jnp.concatenate(weights, axis=0)) / total
        for h in range(heads):
            part = slice(h * HD, (h + 1) * HD)
            mixed_ref[pl.ds(row_start, BLOCK), part] = mixed_t[part, part].T.astype(jnp.bfloat16)
        return carry

    lax.fori_loop(0, per_step, one_block, 0, unroll=True)
    half_steps = pl.num_programs(0) // halves
    for half, out_ref in enumerate(out_refs):
        @pl.when(lax.div(step, half_steps) == half)
        def _():
            out_ref[...] = mixed_ref[...]


def cross_attention(hires_tokens, gain, w_cross_q, kv_chunks, block_lists, block_counts):
    tok_index = lax.axis_index("tok").reshape(1)
    tok_rows, width = hires_tokens.shape
    cols = w_cross_q.shape[1]
    chunk = kv_chunks[0].shape[0]
    low_rows = chunk * len(kv_chunks)
    halves = 2 if tok_rows % (2 * BLOCK) == 0 else 1
    rows = math.gcd(tok_rows // halves, 4 * BLOCK)
    half_steps = tok_rows // halves // rows
    return pl.pallas_call(
        functools.partial(cross_kernel, halves),
        out_shape=[jax.ShapeDtypeStruct((tok_rows // halves, cols), jnp.bfloat16)] * halves,
        grid_spec=pltpu.PrefetchScalarGridSpec(
            num_scalar_prefetch=3,
            grid=(tok_rows // rows,),
            in_specs=[
                pl.BlockSpec((rows, width), lambda i, *_: (i, 0)),
                pl.BlockSpec((1, width), lambda i, *_: (0, 0)),
                pl.BlockSpec((width, cols), lambda i, *_: (0, 0)),
            ]
            + [pl.BlockSpec((chunk, 2 * cols), lambda i, *_: (0, 0)) for _ in kv_chunks],
            out_specs=[
                pl.BlockSpec(
                    (rows, cols),
                    lambda i, *_, half=half: (jnp.clip(i - half * half_steps, 0, half_steps - 1), 0),
                )
                for half in range(halves)
            ],
            scratch_shapes=[
                pltpu.VMEM((low_rows, cols), jnp.bfloat16),
                pltpu.VMEM((cols, low_rows), jnp.bfloat16),
                pltpu.VMEM((rows, cols), jnp.bfloat16),
                pltpu.VMEM((rows, cols), jnp.bfloat16),
            ],
        ),
        compiler_params=pltpu.CompilerParams(vmem_limit_bytes=VMEM_BYTES),
        cost_estimate=pl.CostEstimate(
            flops=2 * tok_rows * cols * (width + 2 * block_lists.shape[1] * BLOCK * 2),
            bytes_accessed=2 * tok_rows * (width + cols),
            transcendentals=tok_rows * block_lists.shape[1] * BLOCK * (cols // HD),
        ),
        name="cross",
    )(block_lists, block_counts, tok_index, hires_tokens, gain, w_cross_q, *kv_chunks)


def view_kernel(tokens_ref, gain_ref, w_ref, wo_ref, out_ref, normed_ref, qkv_ref, mixed_ref):
    parts, sources, run, cols = out_ref.shape
    part_index = pl.program_id(0)
    heads = cols // HD
    rows = sources * run
    pixels = rows // VIEWS
    group = math.gcd(pixels, 32)
    tile = math.gcd(rows, 512)

    @pl.when(pl.program_id(0) == 0)
    def _():
        gain = gain_ref[...]
        step = math.gcd(sources, max(1, tile // run))
        for s in range(0, sources, step):
            tokens = tokens_ref[s : s + step].reshape(step * run, gain.shape[1])
            normed_ref[s * run : (s + step) * run] = rms_rows(tokens, gain)

    for start in range(0, rows, tile):
        stop = start + tile
        tokens = normed_ref[start:stop]
        for k in range(3):
            projected = f32_dot(tokens, w_ref[0, k])
            if k == 0:
                projected = projected * LOG2_SCALE
            qkv_ref[start:stop, k * cols : (k + 1) * cols] = projected.astype(jnp.bfloat16)
    size = VIEWS * group
    row_pixel = lax.broadcasted_iota(jnp.int32, (size, size), 0) % group
    col_pixel = lax.broadcasted_iota(jnp.int32, (size, size), 1) % group
    same = row_pixel == col_pixel

    def gathered(first, column):
        part = slice(column, column + HD)
        return jnp.concatenate(
            [qkv_ref[v * pixels + first : v * pixels + first + group, part] for v in range(VIEWS)],
            axis=0,
        )

    for first in range(0, pixels, group):
        for h in range(heads):
            query = gathered(first, h * HD)
            key = gathered(first, cols + h * HD)
            value = gathered(first, 2 * cols + h * HD)
            scores = lax.dot_general(query, key, CONTRACT_LAST, preferred_element_type=jnp.float32)
            scores = jnp.where(same, scores, -1e30)
            weight = jnp.exp2(scores - jnp.max(scores, axis=1, keepdims=True))
            value_and_one = jnp.concatenate([value, jnp.ones_like(value)], axis=1)
            mixed_and_total = f32_dot(weight.astype(jnp.bfloat16), value_and_one)
            mixed = (mixed_and_total[:, :HD] / mixed_and_total[:, HD:]).astype(jnp.bfloat16)
            for v in range(VIEWS):
                rows_of = slice(v * pixels + first, v * pixels + first + group)
                mixed_ref[part_index, rows_of, h * HD : (h + 1) * HD] = (
                    mixed[v * group : (v + 1) * group]
                )

    @pl.when(part_index == parts - 1)
    def _():
        step = math.gcd(sources, max(1, tile // run))
        for s in range(0, sources, step):
            rows_of = slice(s * run, (s + step) * run)
            for column in range(parts):
                w_rows = slice(column * cols, (column + 1) * cols)
                term = f32_dot(mixed_ref[0, rows_of], wo_ref[0, 0, w_rows])
                for g in range(1, parts):
                    term = term + f32_dot(mixed_ref[g, rows_of], wo_ref[g, 0, w_rows])
                out_ref[column, s : s + step] = term.astype(jnp.bfloat16).reshape(step, run, cols)


def view_attention(tokens, gain, weights):
    n_tok, run, width = tokens.shape
    parts, _, _, cols = weights.shape
    rows = n_tok * run
    return pl.pallas_call(
        view_kernel,
        out_shape=jax.ShapeDtypeStruct((parts, n_tok, run, cols), jnp.bfloat16),
        grid=(parts,),
        in_specs=[
            pl.BlockSpec((n_tok, run, width), lambda i: (0, 0, 0)),
            pl.BlockSpec((1, width), lambda i: (0, 0)),
            pl.BlockSpec((1, 3, width, cols), lambda i: (i, 0, 0, 0)),
            pl.BlockSpec((parts, 1, width, cols), lambda i: (0, 3, 0, 0)),
        ],
        out_specs=pl.BlockSpec((parts, n_tok, run, cols), lambda i: (0, 0, 0, 0)),
        scratch_shapes=[
            pltpu.VMEM((rows, width), jnp.bfloat16),
            pltpu.VMEM((rows, 3 * cols), jnp.bfloat16),
            pltpu.VMEM((parts, rows, cols), jnp.bfloat16),
        ],
        compiler_params=pltpu.CompilerParams(vmem_limit_bytes=VMEM_BYTES),
        cost_estimate=pl.CostEstimate(
            flops=2 * rows * (parts * cols * (3 * width + 512) + width * width),
            bytes_accessed=2 * (2 * rows * width + 4 * parts * width * cols),
            transcendentals=parts * rows * 512,
        ),
        name="view",
    )(tokens, gain, weights, weights)


def base_kernel(halves, index_ref, tokens_ref, *refs):
    cross_refs, w_refs, out_ref = refs[:halves], refs[halves:-1], refs[-1]
    parts = len(w_refs)
    half_steps = pl.num_programs(0) // halves
    for half, cross_ref in enumerate(cross_refs):
        @pl.when(lax.div(pl.program_id(0), half_steps) == half)
        def _():
            total = tokens_ref[...].astype(jnp.float32)
            for k, w_ref in enumerate(w_refs):
                group = lax.rem(index_ref[0] + parts - k, parts)
                total = total + f32_dot(cross_ref[group], w_ref[...])
            out_ref[...] = total


def residual_and_cross(head_index, hires_tokens, cross_all, w_columns):
    halves = len(cross_all)
    parts, half_rows, cols = cross_all[0].shape
    tok_rows = half_rows * halves
    rows = math.gcd(half_rows, 512)
    half_steps = half_rows // rows
    cross_specs = [
        pl.BlockSpec(
            (parts, rows, cols),
            lambda i, index, half=half: (0, jnp.clip(i - half * half_steps, 0, half_steps - 1), 0),
        )
        for half in range(halves)
    ]
    return pl.pallas_call(
        functools.partial(base_kernel, halves),
        out_shape=jax.ShapeDtypeStruct((tok_rows, cols), jnp.float32),
        grid_spec=pltpu.PrefetchScalarGridSpec(
            num_scalar_prefetch=1,
            grid=(tok_rows // rows,),
            in_specs=[pl.BlockSpec((rows, cols), lambda i, index: (i, index[0]))]
            + cross_specs
            + [pl.BlockSpec((cols, cols), lambda i, index: (0, 0))] * parts,
            out_specs=pl.BlockSpec((rows, cols), lambda i, index: (i, 0)),
        ),
        compiler_params=pltpu.CompilerParams(vmem_limit_bytes=VMEM_BYTES),
        cost_estimate=pl.CostEstimate(
            flops=2 * parts * tok_rows * cols * cols,
            bytes_accessed=2 * tok_rows * cols * (parts + 3),
            transcendentals=0,
        ),
        name="base",
    )(head_index.reshape(1), hires_tokens, *cross_all, *w_columns)


def column_blocks(rows_of_w, head_index, n_head):
    cols = rows_of_w.shape[1] // n_head
    return [
        lax.dynamic_slice_in_dim(rows_of_w, lax.rem(head_index + k, n_head) * cols, cols, 1)
        for k in range(n_head)
    ]


def send_blocks(blocks):
    n_head = len(blocks)
    return [
        lax.ppermute(block, "head", [(h, (h + k) % n_head) for h in range(n_head)]) if k else block
        for k, block in enumerate(blocks)
    ]


def ring_chunks(own, n_tok):
    order = list(range(0, n_tok, 2)) + list(range(1, n_tok, 2))[::-1]
    upward = [(order[p], order[(p + 1) % n_tok]) for p in range(n_tok)]
    downward = [(order[p], order[p - 1]) for p in range(n_tok)]
    behind, ahead = [own], [own]
    for step in range(n_tok // 2):
        behind.append(lax.ppermute(behind[-1], "tok", upward))
        if step < (n_tok - 1) // 2:
            ahead.append(lax.ppermute(ahead[-1], "tok", downward))
    return ahead + behind[:0:-1]


def shards(
    n_head,
    n_tok,
    hires_tokens,
    lowres_tokens,
    norm_gain,
    w_cross_q,
    w_low_kv,
    w_view_qkv,
    w_out,
    block_lists,
    block_counts,
):
    tok_rows, width = hires_tokens.shape
    cols = w_cross_q.shape[1]
    quarter = tok_rows // n_head
    head_index = lax.axis_index("head")
    gain = norm_gain.reshape(1, width)

    run = quarter // n_tok

    own_weights = jnp.concatenate(
        [
            w_view_qkv.transpose(1, 0, 2),
            w_out[1].reshape(cols, n_head, cols).transpose(1, 0, 2).reshape(1, width, cols),
        ],
        axis=0,
    )
    weights = lax.all_gather(own_weights, "head", axis=0, tiled=False)
    low_kv = f32_dot(
        rms_rows(lowres_tokens, norm_gain), w_low_kv.reshape(width, 2 * cols)
    ).astype(jnp.bfloat16)
    kv_chunks = ring_chunks(low_kv, n_tok)
    sent = lax.dynamic_slice_in_dim(hires_tokens, head_index * quarter, quarter, 0)
    kv_chunks, sent = lax.optimization_barrier((kv_chunks, sent))

    arrived = lax.all_to_all(
        sent.reshape(n_tok, run, width), "tok", split_axis=0, concat_axis=0, tiled=True
    )
    cross_out = cross_attention(
        hires_tokens, gain, w_cross_q, kv_chunks, block_lists, block_counts
    )
    arrived, w_out, last_half = lax.optimization_barrier((arrived, w_out, cross_out[-1]))
    cross_all = [
        lax.all_gather(half, "head", axis=0, tiled=False) for half in [*cross_out[:-1], last_half]
    ]
    w_columns = send_blocks(column_blocks(w_out[0], head_index, n_head))
    term = view_attention(arrived, gain, weights)
    _, w_columns, cross_all = lax.optimization_barrier((term, w_columns, cross_all))
    view_term = lax.all_to_all(
        term.reshape(n_head * n_tok, run, cols),
        ("head", "tok"), split_axis=0, concat_axis=0, tiled=True,
    )
    base = residual_and_cross(head_index, hires_tokens, cross_all, w_columns)
    return (base + view_term.reshape(tok_rows, cols).astype(jnp.float32)).astype(jnp.bfloat16)


def solution(mesh):
    in_specs = (
        P("tok", None),
        P("tok", None),
        P(),
        P(None, "head"),
        P(None, None, "head"),
        P(None, None, "head"),
        P(None, "head", None),
        P("tok", None),
        P("tok"),
    )
    out_specs = P("tok", "head")
    body = functools.partial(shards, mesh.shape["head"], mesh.shape["tok"])
    return jax.shard_map(body, mesh=mesh, in_specs=in_specs, out_specs=out_specs, check_vma=False)
```

```python
import functools
import math

import jax
import jax.numpy as jnp
from jax import lax
from jax.experimental import pallas as pl
from jax.experimental.pallas import tpu as pltpu
from jax.sharding import PartitionSpec as P

HD = 128
VIEWS = 8
BLOCK = 128
LOG2_SCALE = math.log2(math.e) / math.sqrt(HD)
VMEM_BYTES = 60 * 1024 * 1024
CONTRACT_LAST = (((1,), (1,)), ((), ()))


def rms_rows(row_block, norm_gain):
    values = row_block.astype(jnp.float32)
    factor = lax.rsqrt(jnp.mean(values * values, axis=-1, keepdims=True) + 1e-06)
    return (values * factor * norm_gain).astype(jnp.bfloat16)


def f32_dot(left, right):
    return jnp.dot(left, right, preferred_element_type=jnp.float32)


def block_diagonal(tiles):
    rows = []
    for index, tile in enumerate(tiles):
        zero = jnp.zeros_like(tile)
        rows.append(
            jnp.concatenate([tile if k == index else zero for k in range(len(tiles))], axis=1)
        )
    return jnp.concatenate(rows, axis=0)


def ring_place(tok, n_tok):
    half = lax.div(tok, 2)
    return jnp.where(lax.rem(tok, 2) == 0, half, n_tok - 1 - half)


def cross_kernel(halves, lists_ref, counts_ref, tok_ref, tokens_ref, gain_ref, wq_ref, *refs):
    kv_refs, out_refs = refs[: -4 - halves], refs[-4 - halves : -4]
    k_ref, vt_ref, q_ref, mixed_ref = refs[-4:]
    step = pl.program_id(0)
    rows, cols = mixed_ref.shape
    heads = cols // HD
    per_step = rows // BLOCK
    listed = lists_ref.shape[1]

    @pl.when(step == 0)
    def _():
        n_tok = len(kv_refs)
        for offset, kv_ref in enumerate(kv_refs):
            chunk = kv_ref.shape[0]
            place = lax.rem(ring_place(tok_ref[0], n_tok) + offset, n_tok)
            home = jnp.where(place < (n_tok + 1) // 2, 2 * place, 2 * (n_tok - 1 - place) + 1)
            start = pl.multiple_of(home * chunk, BLOCK)
            k_ref[pl.ds(start, chunk), :] = kv_ref[:, :cols]
            vt_ref[:, pl.ds(start, chunk)] = kv_ref[:, cols:].T

    normed = rms_rows(tokens_ref[...], gain_ref[...])
    q_ref[...] = (f32_dot(normed, wq_ref[...]) * LOG2_SCALE).astype(jnp.bfloat16)

    def one_block(local, carry):
        block = step * per_step + local
        row_start = pl.multiple_of(local * BLOCK, BLOCK)
        count = counts_ref[block]
        first = lists_ref[block, 0]
        starts = [
            pl.multiple_of(jnp.where(j < count, lists_ref[block, j], first) * BLOCK, BLOCK)
            for j in range(listed)
        ]
        query = block_diagonal(
            [q_ref[pl.ds(row_start, BLOCK), h * HD : (h + 1) * HD] for h in range(heads)]
        )
        keys = jnp.concatenate([k_ref[pl.ds(s, BLOCK), :] for s in starts], axis=0)
        scores = lax.dot_general(keys, query, CONTRACT_LAST, preferred_element_type=jnp.float32)
        top = jnp.max(scores, axis=0, keepdims=True)
        weights = []
        total = jnp.zeros_like(top)
        for j in range(listed):
            shift = top + jnp.where(j < count, 0.0, 1e30)
            weight = jnp.exp2(scores[j * BLOCK : (j + 1) * BLOCK] - shift)
            total = total + jnp.sum(weight, axis=0, keepdims=True)
            weights.append(weight.astype(jnp.bfloat16))
        values_t = jnp.concatenate([vt_ref[:, pl.ds(s, BLOCK)] for s in starts], axis=1)
        mixed_t = f32_dot(values_t, jnp.concatenate(weights, axis=0)) / total
        for h in range(heads):
            part = slice(h * HD, (h + 1) * HD)
            mixed_ref[pl.ds(row_start, BLOCK), part] = mixed_t[part, part].T.astype(jnp.bfloat16)
        return carry

    lax.fori_loop(0, per_step, one_block, 0, unroll=True)
    half_steps = pl.num_programs(0) // halves
    for half, out_ref in enumerate(out_refs):
        @pl.when(lax.div(step, half_steps) == half)
        def _():
            out_ref[...] = mixed_ref[...]


def cross_attention(hires_tokens, gain, w_cross_q, kv_chunks, block_lists, block_counts):
    tok_index = lax.axis_index("tok").reshape(1)
    tok_rows, width = hires_tokens.shape
    cols = w_cross_q.shape[1]
    chunk = kv_chunks[0].shape[0]
    low_rows = chunk * len(kv_chunks)
    halves = 2 if tok_rows % (2 * BLOCK) == 0 else 1
    rows = math.gcd(tok_rows // halves, 4 * BLOCK)
    half_steps = tok_rows // halves // rows
    return pl.pallas_call(
        functools.partial(cross_kernel, halves),
        out_shape=[jax.ShapeDtypeStruct((tok_rows // halves, cols), jnp.bfloat16)] * halves,
        grid_spec=pltpu.PrefetchScalarGridSpec(
            num_scalar_prefetch=3,
            grid=(tok_rows // rows,),
            in_specs=[
                pl.BlockSpec((rows, width), lambda i, *_: (i, 0)),
                pl.BlockSpec((1, width), lambda i, *_: (0, 0)),
                pl.BlockSpec((width, cols), lambda i, *_: (0, 0)),
            ]
            + [pl.BlockSpec((chunk, 2 * cols), lambda i, *_: (0, 0)) for _ in kv_chunks],
            out_specs=[
                pl.BlockSpec(
                    (rows, cols),
                    lambda i, *_, half=half: (jnp.clip(i - half * half_steps, 0, half_steps - 1), 0),
                )
                for half in range(halves)
            ],
            scratch_shapes=[
                pltpu.VMEM((low_rows, cols), jnp.bfloat16),
                pltpu.VMEM((cols, low_rows), jnp.bfloat16),
                pltpu.VMEM((rows, cols), jnp.bfloat16),
                pltpu.VMEM((rows, cols), jnp.bfloat16),
            ],
        ),
        compiler_params=pltpu.CompilerParams(vmem_limit_bytes=VMEM_BYTES),
        cost_estimate=pl.CostEstimate(
            flops=2 * tok_rows * cols * (width + 2 * block_lists.shape[1] * BLOCK * 2),
            bytes_accessed=2 * tok_rows * (width + cols),
            transcendentals=tok_rows * block_lists.shape[1] * BLOCK * (cols // HD),
        ),
        name="cross",
    )(block_lists, block_counts, tok_index, hires_tokens, gain, w_cross_q, *kv_chunks)


def view_kernel(tokens_ref, gain_ref, w_ref, wo_ref, out_ref, normed_ref, qkv_ref, mixed_ref):
    parts, sources, run, cols = out_ref.shape
    part_index = pl.program_id(0)
    heads = cols // HD
    rows = sources * run
    pixels = rows // VIEWS
    group = math.gcd(pixels, 32)
    tile = math.gcd(rows, 512)

    @pl.when(pl.program_id(0) == 0)
    def _():
        gain = gain_ref[...]
        step = math.gcd(sources, max(1, tile // run))
        for s in range(0, sources, step):
            tokens = tokens_ref[s : s + step].reshape(step * run, gain.shape[1])
            normed_ref[s * run : (s + step) * run] = rms_rows(tokens, gain)

    for start in range(0, rows, tile):
        stop = start + tile
        tokens = normed_ref[start:stop]
        for k in range(3):
            projected = f32_dot(tokens, w_ref[0, k])
            if k == 0:
                projected = projected * LOG2_SCALE
            qkv_ref[start:stop, k * cols : (k + 1) * cols] = projected.astype(jnp.bfloat16)
    size = VIEWS * group
    row_pixel = lax.broadcasted_iota(jnp.int32, (size, size), 0) % group
    col_pixel = lax.broadcasted_iota(jnp.int32, (size, size), 1) % group
    same = row_pixel == col_pixel

    def gathered(first, column):
        part = slice(column, column + HD)
        return jnp.concatenate(
            [qkv_ref[v * pixels + first : v * pixels + first + group, part] for v in range(VIEWS)],
            axis=0,
        )

    for first in range(0, pixels, group):
        for h in range(heads):
            query = gathered(first, h * HD)
            key = gathered(first, cols + h * HD)
            value = gathered(first, 2 * cols + h * HD)
            scores = lax.dot_general(query, key, CONTRACT_LAST, preferred_element_type=jnp.float32)
            scores = jnp.where(same, scores, -1e30)
            weight = jnp.exp2(scores - jnp.max(scores, axis=1, keepdims=True))
            value_and_one = jnp.concatenate([value, jnp.ones_like(value)], axis=1)
            mixed_and_total = f32_dot(weight.astype(jnp.bfloat16), value_and_one)
            mixed = (mixed_and_total[:, :HD] / mixed_and_total[:, HD:]).astype(jnp.bfloat16)
            for v in range(VIEWS):
                rows_of = slice(v * pixels + first, v * pixels + first + group)
                mixed_ref[part_index, rows_of, h * HD : (h + 1) * HD] = (
                    mixed[v * group : (v + 1) * group]
                )

    @pl.when(part_index == parts - 1)
    def _():
        step = math.gcd(sources, max(1, tile // run))
        for s in range(0, sources, step):
            rows_of = slice(s * run, (s + step) * run)
            for column in range(parts):
                w_rows = slice(column * cols, (column + 1) * cols)
                term = f32_dot(mixed_ref[0, rows_of], wo_ref[0, 0, w_rows])
                for g in range(1, parts):
                    term = term + f32_dot(mixed_ref[g, rows_of], wo_ref[g, 0, w_rows])
                out_ref[column, s : s + step] = term.astype(jnp.bfloat16).reshape(step, run, cols)


def view_attention(tokens, gain, weights):
    n_tok, run, width = tokens.shape
    parts, _, _, cols = weights.shape
    rows = n_tok * run
    return pl.pallas_call(
        view_kernel,
        out_shape=jax.ShapeDtypeStruct((parts, n_tok, run, cols), jnp.bfloat16),
        grid=(parts,),
        in_specs=[
            pl.BlockSpec((n_tok, run, width), lambda i: (0, 0, 0)),
            pl.BlockSpec((1, width), lambda i: (0, 0)),
            pl.BlockSpec((1, 3, width, cols), lambda i: (i, 0, 0, 0)),
            pl.BlockSpec((parts, 1, width, cols), lambda i: (0, 3, 0, 0)),
        ],
        out_specs=pl.BlockSpec((parts, n_tok, run, cols), lambda i: (0, 0, 0, 0)),
        scratch_shapes=[
            pltpu.VMEM((rows, width), jnp.bfloat16),
            pltpu.VMEM((rows, 3 * cols), jnp.bfloat16),
            pltpu.VMEM((parts, rows, cols), jnp.bfloat16),
        ],
        compiler_params=pltpu.CompilerParams(vmem_limit_bytes=VMEM_BYTES),
        cost_estimate=pl.CostEstimate(
            flops=32 * rows * (parts * cols * (3 * width + 512) + width * width),
            bytes_accessed=2 * (2 * rows * width + 4 * parts * width * cols),
            transcendentals=parts * rows * 512,
        ),
        name="view",
    )(tokens, gain, weights, weights)


def base_kernel(halves, index_ref, tokens_ref, *refs):
    cross_refs, w_refs, out_ref = refs[:halves], refs[halves:-1], refs[-1]
    parts = len(w_refs)
    half_steps = pl.num_programs(0) // halves
    for half, cross_ref in enumerate(cross_refs):
        @pl.when(lax.div(pl.program_id(0), half_steps) == half)
        def _():
            total = tokens_ref[...].astype(jnp.float32)
            for k, w_ref in enumerate(w_refs):
                group = lax.rem(index_ref[0] + parts - k, parts)
                total = total + f32_dot(cross_ref[group], w_ref[...])
            out_ref[...] = total


def residual_and_cross(head_index, hires_tokens, cross_all, w_columns):
    halves = len(cross_all)
    parts, half_rows, cols = cross_all[0].shape
    tok_rows = half_rows * halves
    rows = math.gcd(half_rows, 512)
    half_steps = half_rows // rows
    cross_specs = [
        pl.BlockSpec(
            (parts, rows, cols),
            lambda i, index, half=half: (0, jnp.clip(i - half * half_steps, 0, half_steps - 1), 0),
        )
        for half in range(halves)
    ]
    return pl.pallas_call(
        functools.partial(base_kernel, halves),
        out_shape=jax.ShapeDtypeStruct((tok_rows, cols), jnp.float32),
        grid_spec=pltpu.PrefetchScalarGridSpec(
            num_scalar_prefetch=1,
            grid=(tok_rows // rows,),
            in_specs=[pl.BlockSpec((rows, cols), lambda i, index: (i, index[0]))]
            + cross_specs
            + [pl.BlockSpec((cols, cols), lambda i, index: (0, 0))] * parts,
            out_specs=pl.BlockSpec((rows, cols), lambda i, index: (i, 0)),
        ),
        compiler_params=pltpu.CompilerParams(vmem_limit_bytes=VMEM_BYTES),
        cost_estimate=pl.CostEstimate(
            flops=2 * parts * tok_rows * cols * cols,
            bytes_accessed=2 * tok_rows * cols * (parts + 3),
            transcendentals=0,
        ),
        name="base",
    )(head_index.reshape(1), hires_tokens, *cross_all, *w_columns)


def column_blocks(rows_of_w, head_index, n_head):
    cols = rows_of_w.shape[1] // n_head
    return [
        lax.dynamic_slice_in_dim(rows_of_w, lax.rem(head_index + k, n_head) * cols, cols, 1)
        for k in range(n_head)
    ]


def send_block(block, k, n_head):
    return lax.ppermute(block, "head", [(h, (h + k) % n_head) for h in range(n_head)])


def ring_chunks(own, n_tok, blocks):
    order = list(range(0, n_tok, 2)) + list(range(1, n_tok, 2))[::-1]
    upward = [(order[p], order[(p + 1) % n_tok]) for p in range(n_tok)]
    downward = [(order[p], order[p - 1]) for p in range(n_tok)]
    behind, ahead = [own], [own]
    sent = [blocks[0]]
    for step in range(n_tok // 2):
        behind.append(lax.ppermute(behind[-1], "tok", upward))
        if step < (n_tok - 1) // 2:
            ahead.append(lax.ppermute(ahead[-1], "tok", downward))
        if len(sent) < len(blocks):
            block = send_block(blocks[len(sent)], len(sent), len(blocks))
            behind[-1], ahead[-1], block = lax.optimization_barrier((behind[-1], ahead[-1], block))
            sent.append(block)
    for k in range(len(sent), len(blocks)):
        sent.append(send_block(blocks[k], k, len(blocks)))
    return ahead + behind[:0:-1], sent


def shards(
    n_head,
    n_tok,
    hires_tokens,
    lowres_tokens,
    norm_gain,
    w_cross_q,
    w_low_kv,
    w_view_qkv,
    w_out,
    block_lists,
    block_counts,
):
    tok_rows, width = hires_tokens.shape
    cols = w_cross_q.shape[1]
    quarter = tok_rows // n_head
    head_index = lax.axis_index("head")
    gain = norm_gain.reshape(1, width)

    run = quarter // n_tok

    own_weights = jnp.concatenate(
        [
            w_view_qkv.transpose(1, 0, 2),
            w_out[1].reshape(cols, n_head, cols).transpose(1, 0, 2).reshape(1, width, cols),
        ],
        axis=0,
    )
    weights = lax.all_gather(own_weights, "head", axis=0, tiled=False)
    low_kv = f32_dot(
        rms_rows(lowres_tokens, norm_gain), w_low_kv.reshape(width, 2 * cols)
    ).astype(jnp.bfloat16)
    kv_chunks, w_columns = ring_chunks(
        low_kv, n_tok, column_blocks(w_out[0], head_index, n_head)
    )
    sent = lax.dynamic_slice_in_dim(hires_tokens, head_index * quarter, quarter, 0)
    kv_chunks, sent = lax.optimization_barrier((kv_chunks, sent))

    arrived = lax.all_to_all(
        sent.reshape(n_tok, run, width), "tok", split_axis=0, concat_axis=0, tiled=True
    )
    cross_out = cross_attention(
        hires_tokens, gain, w_cross_q, kv_chunks, block_lists, block_counts
    )
    arrived, last_half = lax.optimization_barrier((arrived, cross_out[-1]))
    cross_all = [
        lax.all_gather(half, "head", axis=0, tiled=False) for half in [*cross_out[:-1], last_half]
    ]
    term = view_attention(arrived, gain, weights)
    _, cross_all = lax.optimization_barrier((term, cross_all))
    view_term = lax.all_to_all(
        term.reshape(n_head * n_tok, run, cols),
        ("head", "tok"), split_axis=0, concat_axis=0, tiled=True,
    )
    base = residual_and_cross(head_index, hires_tokens, cross_all, w_columns)
    return (base + view_term.reshape(tok_rows, cols).astype(jnp.float32)).astype(jnp.bfloat16)


def solution(mesh):
    in_specs = (
        P("tok", None),
        P("tok", None),
        P(),
        P(None, "head"),
        P(None, None, "head"),
        P(None, None, "head"),
        P(None, "head", None),
        P("tok", None),
        P("tok"),
    )
    out_specs = P("tok", "head")
    body = functools.partial(shards, mesh.shape["head"], mesh.shape["tok"])
    return jax.shard_map(body, mesh=mesh, in_specs=in_specs, out_specs=out_specs, check_vma=False)
```

```python
import functools
import math

import jax
import jax.numpy as jnp
from jax import lax
from jax.experimental import pallas as pl
from jax.experimental.pallas import tpu as pltpu
from jax.sharding import PartitionSpec as P

HD = 128
VIEWS = 8
BLOCK = 128
LOG2_SCALE = math.log2(math.e) / math.sqrt(HD)
VMEM_BYTES = 60 * 1024 * 1024
CONTRACT_LAST = (((1,), (1,)), ((), ()))


def rms_rows(row_block, norm_gain):
    values = row_block.astype(jnp.float32)
    factor = lax.rsqrt(jnp.mean(values * values, axis=-1, keepdims=True) + 1e-06)
    return (values * factor * norm_gain).astype(jnp.bfloat16)


def f32_dot(left, right):
    return jnp.dot(left, right, preferred_element_type=jnp.float32)


def block_diagonal(tiles):
    rows = []
    for index, tile in enumerate(tiles):
        zero = jnp.zeros_like(tile)
        rows.append(
            jnp.concatenate([tile if k == index else zero for k in range(len(tiles))], axis=1)
        )
    return jnp.concatenate(rows, axis=0)


def ring_place(tok, n_tok):
    half = lax.div(tok, 2)
    return jnp.where(lax.rem(tok, 2) == 0, half, n_tok - 1 - half)


def cross_kernel(halves, lists_ref, counts_ref, tok_ref, tokens_ref, gain_ref, wq_ref, *refs):
    kv_refs, out_refs = refs[: -4 - halves], refs[-4 - halves : -4]
    k_ref, vt_ref, q_ref, mixed_ref = refs[-4:]
    step = pl.program_id(0)
    rows, cols = mixed_ref.shape
    heads = cols // HD
    per_step = rows // BLOCK
    listed = lists_ref.shape[1]

    @pl.when(step == 0)
    def _():
        n_tok = len(kv_refs)
        for offset, kv_ref in enumerate(kv_refs):
            chunk = kv_ref.shape[0]
            place = lax.rem(ring_place(tok_ref[0], n_tok) + offset, n_tok)
            home = jnp.where(place < (n_tok + 1) // 2, 2 * place, 2 * (n_tok - 1 - place) + 1)
            start = pl.multiple_of(home * chunk, BLOCK)
            k_ref[pl.ds(start, chunk), :] = kv_ref[:, :cols]
            vt_ref[:, pl.ds(start, chunk)] = kv_ref[:, cols:].T

    normed = rms_rows(tokens_ref[...], gain_ref[...])
    q_ref[...] = (f32_dot(normed, wq_ref[...]) * LOG2_SCALE).astype(jnp.bfloat16)

    def one_block(local, carry):
        block = step * per_step + local
        row_start = pl.multiple_of(local * BLOCK, BLOCK)
        count = counts_ref[block]
        first = lists_ref[block, 0]
        starts = [
            pl.multiple_of(jnp.where(j < count, lists_ref[block, j], first) * BLOCK, BLOCK)
            for j in range(listed)
        ]
        query = block_diagonal(
            [q_ref[pl.ds(row_start, BLOCK), h * HD : (h + 1) * HD] for h in range(heads)]
        )
        keys = jnp.concatenate([k_ref[pl.ds(s, BLOCK), :] for s in starts], axis=0)
        scores = lax.dot_general(keys, query, CONTRACT_LAST, preferred_element_type=jnp.float32)
        top = jnp.max(scores, axis=0, keepdims=True)
        weights = []
        total = jnp.zeros_like(top)
        for j in range(listed):
            shift = top + jnp.where(j < count, 0.0, 1e30)
            weight = jnp.exp2(scores[j * BLOCK : (j + 1) * BLOCK] - shift)
            total = total + jnp.sum(weight, axis=0, keepdims=True)
            weights.append(weight.astype(jnp.bfloat16))
        values_t = jnp.concatenate([vt_ref[:, pl.ds(s, BLOCK)] for s in starts], axis=1)
        mixed_t = f32_dot(values_t, jnp.concatenate(weights, axis=0)) / total
        for h in range(heads):
            part = slice(h * HD, (h + 1) * HD)
            mixed_ref[pl.ds(row_start, BLOCK), part] = mixed_t[part, part].T.astype(jnp.bfloat16)
        return carry

    lax.fori_loop(0, per_step, one_block, 0, unroll=True)
    half_steps = pl.num_programs(0) // halves
    for half, out_ref in enumerate(out_refs):
        @pl.when(lax.div(step, half_steps) == half)
        def _():
            out_ref[...] = mixed_ref[...]


def cross_attention(hires_tokens, gain, w_cross_q, kv_chunks, block_lists, block_counts):
    tok_index = lax.axis_index("tok").reshape(1)
    tok_rows, width = hires_tokens.shape
    cols = w_cross_q.shape[1]
    chunk = kv_chunks[0].shape[0]
    low_rows = chunk * len(kv_chunks)
    halves = 1
    rows = math.gcd(tok_rows // halves, 4 * BLOCK)
    half_steps = tok_rows // halves // rows
    return pl.pallas_call(
        functools.partial(cross_kernel, halves),
        out_shape=[jax.ShapeDtypeStruct((tok_rows // halves, cols), jnp.bfloat16)] * halves,
        grid_spec=pltpu.PrefetchScalarGridSpec(
            num_scalar_prefetch=3,
            grid=(tok_rows // rows,),
            in_specs=[
                pl.BlockSpec((rows, width), lambda i, *_: (i, 0)),
                pl.BlockSpec((1, width), lambda i, *_: (0, 0)),
                pl.BlockSpec((width, cols), lambda i, *_: (0, 0)),
            ]
            + [pl.BlockSpec((chunk, 2 * cols), lambda i, *_: (0, 0)) for _ in kv_chunks],
            out_specs=[
                pl.BlockSpec(
                    (rows, cols),
                    lambda i, *_, half=half: (jnp.clip(i - half * half_steps, 0, half_steps - 1), 0),
                )
                for half in range(halves)
            ],
            scratch_shapes=[
                pltpu.VMEM((low_rows, cols), jnp.bfloat16),
                pltpu.VMEM((cols, low_rows), jnp.bfloat16),
                pltpu.VMEM((rows, cols), jnp.bfloat16),
                pltpu.VMEM((rows, cols), jnp.bfloat16),
            ],
        ),
        compiler_params=pltpu.CompilerParams(vmem_limit_bytes=VMEM_BYTES),
        cost_estimate=pl.CostEstimate(
            flops=2 * tok_rows * cols * (width + 2 * block_lists.shape[1] * BLOCK * 2),
            bytes_accessed=2 * tok_rows * (width + cols),
            transcendentals=tok_rows * block_lists.shape[1] * BLOCK * (cols // HD),
        ),
        name="cross",
    )(block_lists, block_counts, tok_index, hires_tokens, gain, w_cross_q, *kv_chunks)


def view_kernel(tokens_ref, gain_ref, w_ref, wo_ref, out_ref, normed_ref, qkv_ref, mixed_ref):
    parts, sources, run, cols = out_ref.shape
    part_index = pl.program_id(0)
    heads = cols // HD
    rows = sources * run
    pixels = rows // VIEWS
    group = math.gcd(pixels, 32)
    tile = math.gcd(rows, 512)

    @pl.when(pl.program_id(0) == 0)
    def _():
        gain = gain_ref[...]
        step = math.gcd(sources, max(1, tile // run))
        for s in range(0, sources, step):
            tokens = tokens_ref[s : s + step].reshape(step * run, gain.shape[1])
            normed_ref[s * run : (s + step) * run] = rms_rows(tokens, gain)

    for start in range(0, rows, tile):
        stop = start + tile
        tokens = normed_ref[start:stop]
        for k in range(3):
            projected = f32_dot(tokens, w_ref[0, k])
            if k == 0:
                projected = projected * LOG2_SCALE
            qkv_ref[start:stop, k * cols : (k + 1) * cols] = projected.astype(jnp.bfloat16)
    size = VIEWS * group
    row_pixel = lax.broadcasted_iota(jnp.int32, (size, size), 0) % group
    col_pixel = lax.broadcasted_iota(jnp.int32, (size, size), 1) % group
    same = row_pixel == col_pixel

    def gathered(first, column):
        part = slice(column, column + HD)
        return jnp.concatenate(
            [qkv_ref[v * pixels + first : v * pixels + first + group, part] for v in range(VIEWS)],
            axis=0,
        )

    for first in range(0, pixels, group):
        for h in range(heads):
            query = gathered(first, h * HD)
            key = gathered(first, cols + h * HD)
            value = gathered(first, 2 * cols + h * HD)
            scores = lax.dot_general(query, key, CONTRACT_LAST, preferred_element_type=jnp.float32)
            scores = jnp.where(same, scores, -1e30)
            weight = jnp.exp2(scores - jnp.max(scores, axis=1, keepdims=True))
            value_and_one = jnp.concatenate([value, jnp.ones_like(value)], axis=1)
            mixed_and_total = f32_dot(weight.astype(jnp.bfloat16), value_and_one)
            mixed = (mixed_and_total[:, :HD] / mixed_and_total[:, HD:]).astype(jnp.bfloat16)
            for v in range(VIEWS):
                rows_of = slice(v * pixels + first, v * pixels + first + group)
                mixed_ref[part_index, rows_of, h * HD : (h + 1) * HD] = (
                    mixed[v * group : (v + 1) * group]
                )

    @pl.when(part_index == parts - 1)
    def _():
        step = math.gcd(sources, max(1, tile // run))
        for s in range(0, sources, step):
            rows_of = slice(s * run, (s + step) * run)
            for column in range(parts):
                w_rows = slice(column * cols, (column + 1) * cols)
                term = f32_dot(mixed_ref[0, rows_of], wo_ref[0, 0, w_rows])
                for g in range(1, parts):
                    term = term + f32_dot(mixed_ref[g, rows_of], wo_ref[g, 0, w_rows])
                out_ref[column, s : s + step] = term.astype(jnp.bfloat16).reshape(step, run, cols)


def view_attention(tokens, gain, weights):
    n_tok, run, width = tokens.shape
    parts, _, _, cols = weights.shape
    rows = n_tok * run
    return pl.pallas_call(
        view_kernel,
        out_shape=jax.ShapeDtypeStruct((parts, n_tok, run, cols), jnp.bfloat16),
        grid=(parts,),
        in_specs=[
            pl.BlockSpec((n_tok, run, width), lambda i: (0, 0, 0)),
            pl.BlockSpec((1, width), lambda i: (0, 0)),
            pl.BlockSpec((1, 3, width, cols), lambda i: (i, 0, 0, 0)),
            pl.BlockSpec((parts, 1, width, cols), lambda i: (0, 4, 0, 0)),
        ],
        out_specs=pl.BlockSpec((parts, n_tok, run, cols), lambda i: (0, 0, 0, 0)),
        scratch_shapes=[
            pltpu.VMEM((rows, width), jnp.bfloat16),
            pltpu.VMEM((rows, 3 * cols), jnp.bfloat16),
            pltpu.VMEM((parts, rows, cols), jnp.bfloat16),
        ],
        compiler_params=pltpu.CompilerParams(vmem_limit_bytes=VMEM_BYTES),
        cost_estimate=pl.CostEstimate(
            flops=2 * rows * (parts * cols * (3 * width + 512) + width * width),
            bytes_accessed=2 * (2 * rows * width + 4 * parts * width * cols),
            transcendentals=parts * rows * 512,
        ),
        name="view",
    )(tokens, gain, weights, weights)


def final_kernel(index_ref, tokens_ref, cross_ref, view_ref, w_ref, out_ref):
    total = tokens_ref[...].astype(jnp.float32) + view_ref[...].astype(jnp.float32)
    for g in range(cross_ref.shape[0]):
        total = total + f32_dot(cross_ref[g], w_ref[g, 0])
    out_ref[...] = total.astype(jnp.bfloat16)


def final_sum(head_index, hires_tokens, cross_all, view_term, weights):
    parts, tok_rows, cols = cross_all.shape
    rows = math.gcd(tok_rows, 512)
    own = pl.BlockSpec((rows, cols), lambda i, index: (i, 0))
    return pl.pallas_call(
        final_kernel,
        out_shape=jax.ShapeDtypeStruct((tok_rows, cols), jnp.bfloat16),
        grid_spec=pltpu.PrefetchScalarGridSpec(
            num_scalar_prefetch=1,
            grid=(tok_rows // rows,),
            in_specs=[
                pl.BlockSpec((rows, cols), lambda i, index: (i, index[0])),
                pl.BlockSpec((parts, rows, cols), lambda i, index: (0, i, 0)),
                own,
                pl.BlockSpec((parts, 1, cols, cols), lambda i, index: (0, 3, index[0], 0)),
            ],
            out_specs=own,
        ),
        compiler_params=pltpu.CompilerParams(vmem_limit_bytes=VMEM_BYTES),
        cost_estimate=pl.CostEstimate(
            flops=2 * parts * tok_rows * cols * cols,
            bytes_accessed=2 * tok_rows * cols * (parts + 3),
            transcendentals=0,
        ),
        name="final",
    )(head_index.reshape(1), hires_tokens, cross_all, view_term, weights)


def ring_chunks(own, n_tok):
    order = list(range(0, n_tok, 2)) + list(range(1, n_tok, 2))[::-1]
    upward = [(order[p], order[(p + 1) % n_tok]) for p in range(n_tok)]
    downward = [(order[p], order[p - 1]) for p in range(n_tok)]
    behind, ahead = [own], [own]
    for step in range(n_tok // 2):
        behind.append(lax.ppermute(behind[-1], "tok", upward))
        if step < (n_tok - 1) // 2:
            ahead.append(lax.ppermute(ahead[-1], "tok", downward))
    return ahead + behind[:0:-1]


def shards(
    n_head,
    n_tok,
    hires_tokens,
    lowres_tokens,
    norm_gain,
    w_cross_q,
    w_low_kv,
    w_view_qkv,
    w_out,
    block_lists,
    block_counts,
):
    tok_rows, width = hires_tokens.shape
    cols = w_cross_q.shape[1]
    quarter = tok_rows // n_head
    head_index = lax.axis_index("head")
    gain = norm_gain.reshape(1, width)

    run = quarter // n_tok

    own_weights = jnp.concatenate(
        [
            w_view_qkv.transpose(1, 0, 2),
            w_out.reshape(2, cols, n_head, cols).transpose(0, 2, 1, 3).reshape(2, width, cols),
        ],
        axis=0,
    )
    weights = lax.all_gather(own_weights, "head", axis=0, tiled=False)
    low_kv = f32_dot(
        rms_rows(lowres_tokens, norm_gain), w_low_kv.reshape(width, 2 * cols)
    ).astype(jnp.bfloat16)
    kv_chunks = ring_chunks(low_kv, n_tok)
    sent = lax.dynamic_slice_in_dim(hires_tokens, head_index * quarter, quarter, 0)
    kv_chunks, sent = lax.optimization_barrier((kv_chunks, sent))

    arrived = lax.all_to_all(
        sent.reshape(n_tok, run, width), "tok", split_axis=0, concat_axis=0, tiled=True
    )
    (cross_out,) = cross_attention(
        hires_tokens, gain, w_cross_q, kv_chunks, block_lists, block_counts
    )
    cross_out, arrived = lax.optimization_barrier((cross_out, arrived))
    cross_all = lax.all_gather(cross_out, "head", axis=0, tiled=False)
    view_term = lax.all_to_all(
        view_attention(arrived, gain, weights).reshape(n_head * n_tok, run, cols),
        ("head", "tok"), split_axis=0, concat_axis=0, tiled=True,
    )
    return final_sum(
        head_index, hires_tokens, cross_all, view_term.reshape(tok_rows, cols), weights
    )


def solution(mesh):
    in_specs = (
        P("tok", None),
        P("tok", None),
        P(),
        P(None, "head"),
        P(None, None, "head"),
        P(None, None, "head"),
        P(None, "head", None),
        P("tok", None),
        P("tok"),
    )
    out_specs = P("tok", "head")
    body = functools.partial(shards, mesh.shape["head"], mesh.shape["tok"])
    return jax.shard_map(body, mesh=mesh, in_specs=in_specs, out_specs=out_specs, check_vma=False)
```

```python
import functools
import math

import jax
import jax.numpy as jnp
from jax import lax
from jax.experimental import pallas as pl
from jax.experimental.pallas import tpu as pltpu
from jax.sharding import PartitionSpec as P

HD = 128
VIEWS = 8
BLOCK = 128
LOG2_SCALE = math.log2(math.e) / math.sqrt(HD)
VMEM_BYTES = 60 * 1024 * 1024
CONTRACT_LAST = (((1,), (1,)), ((), ()))


def rms_rows(row_block, norm_gain):
    values = row_block.astype(jnp.float32)
    factor = lax.rsqrt(jnp.mean(values * values, axis=-1, keepdims=True) + 1e-06)
    return (values * factor * norm_gain).astype(jnp.bfloat16)


def f32_dot(left, right):
    return jnp.dot(left, right, preferred_element_type=jnp.float32)


def block_diagonal(tiles):
    rows = []
    for index, tile in enumerate(tiles):
        zero = jnp.zeros_like(tile)
        rows.append(
            jnp.concatenate([tile if k == index else zero for k in range(len(tiles))], axis=1)
        )
    return jnp.concatenate(rows, axis=0)


def ring_place(tok, n_tok):
    half = lax.div(tok, 2)
    return jnp.where(lax.rem(tok, 2) == 0, half, n_tok - 1 - half)


def cross_kernel(halves, lists_ref, counts_ref, tok_ref, tokens_ref, gain_ref, wq_ref, *refs):
    kv_refs, out_refs = refs[: -4 - halves], refs[-4 - halves : -4]
    k_ref, vt_ref, q_ref, mixed_ref = refs[-4:]
    step = pl.program_id(0)
    rows, cols = mixed_ref.shape
    heads = cols // HD
    per_step = rows // BLOCK
    listed = lists_ref.shape[1]

    @pl.when(step == 0)
    def _():
        n_tok = len(kv_refs)
        for offset, kv_ref in enumerate(kv_refs):
            chunk = kv_ref.shape[0]
            place = lax.rem(ring_place(tok_ref[0], n_tok) + offset, n_tok)
            home = jnp.where(place < (n_tok + 1) // 2, 2 * place, 2 * (n_tok - 1 - place) + 1)
            start = pl.multiple_of(home * chunk, BLOCK)
            k_ref[pl.ds(start, chunk), :] = kv_ref[:, :cols]
            vt_ref[:, pl.ds(start, chunk)] = kv_ref[:, cols:].T

    normed = rms_rows(tokens_ref[...], gain_ref[...])
    q_ref[...] = (f32_dot(normed, wq_ref[...]) * LOG2_SCALE).astype(jnp.bfloat16)

    def one_block(local, carry):
        block = step * per_step + local
        row_start = pl.multiple_of(local * BLOCK, BLOCK)
        count = counts_ref[block]
        first = lists_ref[block, 0]
        starts = [
            pl.multiple_of(jnp.where(j < count, lists_ref[block, j], first) * BLOCK, BLOCK)
            for j in range(listed)
        ]
        query = block_diagonal(
            [q_ref[pl.ds(row_start, BLOCK), h * HD : (h + 1) * HD] for h in range(heads)]
        )
        keys = jnp.concatenate([k_ref[pl.ds(s, BLOCK), :] for s in starts], axis=0)
        scores = lax.dot_general(keys, query, CONTRACT_LAST, preferred_element_type=jnp.float32)
        top = jnp.max(scores, axis=0, keepdims=True)
        weights = []
        total = jnp.zeros_like(top)
        for j in range(listed):
            shift = top + jnp.where(j < count, 0.0, 1e30)
            weight = jnp.exp2(scores[j * BLOCK : (j + 1) * BLOCK] - shift)
            total = total + jnp.sum(weight, axis=0, keepdims=True)
            weights.append(weight.astype(jnp.bfloat16))
        values_t = jnp.concatenate([vt_ref[:, pl.ds(s, BLOCK)] for s in starts], axis=1)
        mixed_t = f32_dot(values_t, jnp.concatenate(weights, axis=0)) / total
        for h in range(heads):
            part = slice(h * HD, (h + 1) * HD)
            mixed_ref[pl.ds(row_start, BLOCK), part] = mixed_t[part, part].T.astype(jnp.bfloat16)
        return carry

    lax.fori_loop(0, per_step, one_block, 0, unroll=True)
    half_steps = pl.num_programs(0) // halves
    for half, out_ref in enumerate(out_refs):
        @pl.when(lax.div(step, half_steps) == half)
        def _():
            out_ref[...] = mixed_ref[...]


def cross_attention(hires_tokens, gain, w_cross_q, kv_chunks, block_lists, block_counts):
    tok_index = lax.axis_index("tok").reshape(1)
    tok_rows, width = hires_tokens.shape
    cols = w_cross_q.shape[1]
    chunk = kv_chunks[0].shape[0]
    low_rows = chunk * len(kv_chunks)
    halves = 1
    rows = math.gcd(tok_rows // halves, 4 * BLOCK)
    half_steps = tok_rows // halves // rows
    return pl.pallas_call(
        functools.partial(cross_kernel, halves),
        out_shape=[jax.ShapeDtypeStruct((tok_rows // halves, cols), jnp.bfloat16)] * halves,
        grid_spec=pltpu.PrefetchScalarGridSpec(
            num_scalar_prefetch=3,
            grid=(tok_rows // rows,),
            in_specs=[
                pl.BlockSpec((rows, width), lambda i, *_: (i, 0)),
                pl.BlockSpec((1, width), lambda i, *_: (0, 0)),
                pl.BlockSpec((width, cols), lambda i, *_: (0, 0)),
            ]
            + [pl.BlockSpec((chunk, 2 * cols), lambda i, *_: (0, 0)) for _ in kv_chunks],
            out_specs=[
                pl.BlockSpec(
                    (rows, cols),
                    lambda i, *_, half=half: (jnp.clip(i - half * half_steps, 0, half_steps - 1), 0),
                )
                for half in range(halves)
            ],
            scratch_shapes=[
                pltpu.VMEM((low_rows, cols), jnp.bfloat16),
                pltpu.VMEM((cols, low_rows), jnp.bfloat16),
                pltpu.VMEM((rows, cols), jnp.bfloat16),
                pltpu.VMEM((rows, cols), jnp.bfloat16),
            ],
        ),
        compiler_params=pltpu.CompilerParams(vmem_limit_bytes=VMEM_BYTES),
        cost_estimate=pl.CostEstimate(
            flops=2 * tok_rows * cols * (width + 2 * block_lists.shape[1] * BLOCK * 2),
            bytes_accessed=2 * tok_rows * (width + cols),
            transcendentals=tok_rows * block_lists.shape[1] * BLOCK * (cols // HD),
        ),
        name="cross",
    )(block_lists, block_counts, tok_index, hires_tokens, gain, w_cross_q, *kv_chunks)


def view_kernel(tokens_ref, gain_ref, w_ref, wo_ref, out_ref, normed_ref, qkv_ref, mixed_ref):
    parts, sources, run, cols = out_ref.shape
    part_index = pl.program_id(0)
    heads = cols // HD
    rows = sources * run
    pixels = rows // VIEWS
    group = math.gcd(pixels, 32)
    tile = math.gcd(rows, 512)

    @pl.when(pl.program_id(0) == 0)
    def _():
        gain = gain_ref[...]
        step = math.gcd(sources, max(1, tile // run))
        for s in range(0, sources, step):
            tokens = tokens_ref[s : s + step].reshape(step * run, gain.shape[1])
            normed_ref[s * run : (s + step) * run] = rms_rows(tokens, gain)

    for start in range(0, rows, tile):
        stop = start + tile
        tokens = normed_ref[start:stop]
        for k in range(3):
            projected = f32_dot(tokens, w_ref[0, k])
            if k == 0:
                projected = projected * LOG2_SCALE
            qkv_ref[start:stop, k * cols : (k + 1) * cols] = projected.astype(jnp.bfloat16)
    size = VIEWS * group
    row_pixel = lax.broadcasted_iota(jnp.int32, (size, size), 0) % group
    col_pixel = lax.broadcasted_iota(jnp.int32, (size, size), 1) % group
    same = row_pixel == col_pixel

    def gathered(first, column):
        part = slice(column, column + HD)
        return jnp.concatenate(
            [qkv_ref[v * pixels + first : v * pixels + first + group, part] for v in range(VIEWS)],
            axis=0,
        )

    for first in range(0, pixels, group):
        for h in range(heads):
            query = gathered(first, h * HD)
            key = gathered(first, cols + h * HD)
            value = gathered(first, 2 * cols + h * HD)
            scores = lax.dot_general(query, key, CONTRACT_LAST, preferred_element_type=jnp.float32)
            scores = jnp.where(same, scores, -1e30)
            weight = jnp.exp2(scores - jnp.max(scores, axis=1, keepdims=True))
            value_and_one = jnp.concatenate([value, jnp.ones_like(value)], axis=1)
            mixed_and_total = f32_dot(weight.astype(jnp.bfloat16), value_and_one)
            mixed = (mixed_and_total[:, :HD] / mixed_and_total[:, HD:]).astype(jnp.bfloat16)
            for v in range(VIEWS):
                rows_of = slice(v * pixels + first, v * pixels + first + group)
                mixed_ref[part_index, rows_of, h * HD : (h + 1) * HD] = (
                    mixed[v * group : (v + 1) * group]
                )

    @pl.when(part_index == parts - 1)
    def _():
        step = math.gcd(sources, max(1, tile // run))
        for s in range(0, sources, step):
            rows_of = slice(s * run, (s + step) * run)
            for column in range(parts):
                w_rows = slice(column * cols, (column + 1) * cols)
                term = f32_dot(mixed_ref[0, rows_of], wo_ref[0, 0, w_rows])
                for g in range(1, parts):
                    term = term + f32_dot(mixed_ref[g, rows_of], wo_ref[g, 0, w_rows])
                out_ref[column, s : s + step] = term.astype(jnp.bfloat16).reshape(step, run, cols)


def view_attention(tokens, gain, weights):
    n_tok, run, width = tokens.shape
    parts, _, _, cols = weights.shape
    rows = n_tok * run
    return pl.pallas_call(
        view_kernel,
        out_shape=jax.ShapeDtypeStruct((parts, n_tok, run, cols), jnp.bfloat16),
        grid=(parts,),
        in_specs=[
            pl.BlockSpec((n_tok, run, width), lambda i: (0, 0, 0)),
            pl.BlockSpec((1, width), lambda i: (0, 0)),
            pl.BlockSpec((1, 3, width, cols), lambda i: (i, 0, 0, 0)),
            pl.BlockSpec((parts, 1, width, cols), lambda i: (0, 4, 0, 0)),
        ],
        out_specs=pl.BlockSpec((parts, n_tok, run, cols), lambda i: (0, 0, 0, 0)),
        scratch_shapes=[
            pltpu.VMEM((rows, width), jnp.bfloat16),
            pltpu.VMEM((rows, 3 * cols), jnp.bfloat16),
            pltpu.VMEM((parts, rows, cols), jnp.bfloat16),
        ],
        compiler_params=pltpu.CompilerParams(vmem_limit_bytes=VMEM_BYTES),
        cost_estimate=pl.CostEstimate(
            flops=2 * rows * (parts * cols * (3 * width + 512) + width * width),
            bytes_accessed=2 * (2 * rows * width + 4 * parts * width * cols),
            transcendentals=parts * rows * 512,
        ),
        name="view",
    )(tokens, gain, weights, weights)


def final_kernel(index_ref, tokens_ref, cross_ref, view_ref, w_ref, out_ref):
    total = tokens_ref[...].astype(jnp.float32) + view_ref[...].astype(jnp.float32)
    for g in range(cross_ref.shape[0]):
        total = total + f32_dot(cross_ref[g], w_ref[g, 0])
    out_ref[...] = total.astype(jnp.bfloat16)


def final_sum(head_index, hires_tokens, cross_all, view_term, weights):
    parts, tok_rows, cols = cross_all.shape
    rows = math.gcd(tok_rows, 512)
    own = pl.BlockSpec((rows, cols), lambda i, index: (i, 0))
    return pl.pallas_call(
        final_kernel,
        out_shape=jax.ShapeDtypeStruct((tok_rows, cols), jnp.bfloat16),
        grid_spec=pltpu.PrefetchScalarGridSpec(
            num_scalar_prefetch=1,
            grid=(tok_rows // rows,),
            in_specs=[
                pl.BlockSpec((rows, cols), lambda i, index: (i, index[0])),
                pl.BlockSpec((parts, rows, cols), lambda i, index: (0, i, 0)),
                own,
                pl.BlockSpec((parts, 1, cols, cols), lambda i, index: (0, 3, index[0], 0)),
            ],
            out_specs=own,
        ),
        compiler_params=pltpu.CompilerParams(vmem_limit_bytes=VMEM_BYTES),
        cost_estimate=pl.CostEstimate(
            flops=2 * parts * tok_rows * cols * cols,
            bytes_accessed=2 * tok_rows * cols * (parts + 3),
            transcendentals=0,
        ),
        name="final",
    )(head_index.reshape(1), hires_tokens, cross_all, view_term, weights)


def ring_chunks(own, n_tok):
    order = list(range(0, n_tok, 2)) + list(range(1, n_tok, 2))[::-1]
    upward = [(order[p], order[(p + 1) % n_tok]) for p in range(n_tok)]
    downward = [(order[p], order[p - 1]) for p in range(n_tok)]
    behind, ahead = [own], [own]
    for step in range(n_tok // 2):
        behind.append(lax.ppermute(behind[-1], "tok", upward))
        if step < (n_tok - 1) // 2:
            ahead.append(lax.ppermute(ahead[-1], "tok", downward))
    return ahead + behind[:0:-1]


def shards(
    n_head,
    n_tok,
    hires_tokens,
    lowres_tokens,
    norm_gain,
    w_cross_q,
    w_low_kv,
    w_view_qkv,
    w_out,
    block_lists,
    block_counts,
):
    tok_rows, width = hires_tokens.shape
    cols = w_cross_q.shape[1]
    quarter = tok_rows // n_head
    head_index = lax.axis_index("head")
    gain = norm_gain.reshape(1, width)

    run = quarter // n_tok

    low_kv = f32_dot(
        rms_rows(lowres_tokens, norm_gain), w_low_kv.reshape(width, 2 * cols)
    ).astype(jnp.bfloat16)
    low_kv, w_view_qkv, w_out = lax.optimization_barrier((low_kv, w_view_qkv, w_out))
    own_weights = jnp.concatenate(
        [
            w_view_qkv.transpose(1, 0, 2),
            w_out.reshape(2, cols, n_head, cols).transpose(0, 2, 1, 3).reshape(2, width, cols),
        ],
        axis=0,
    )
    weights = lax.all_gather(own_weights, "head", axis=0, tiled=False)
    kv_chunks = ring_chunks(low_kv, n_tok)
    sent = lax.dynamic_slice_in_dim(hires_tokens, head_index * quarter, quarter, 0)
    kv_chunks, sent = lax.optimization_barrier((kv_chunks, sent))

    arrived = lax.all_to_all(
        sent.reshape(n_tok, run, width), "tok", split_axis=0, concat_axis=0, tiled=True
    )
    (cross_out,) = cross_attention(
        hires_tokens, gain, w_cross_q, kv_chunks, block_lists, block_counts
    )
    cross_out, arrived = lax.optimization_barrier((cross_out, arrived))
    cross_all = lax.all_gather(cross_out, "head", axis=0, tiled=False)
    view_term = lax.all_to_all(
        view_attention(arrived, gain, weights).reshape(n_head * n_tok, run, cols),
        ("head", "tok"), split_axis=0, concat_axis=0, tiled=True,
    )
    return final_sum(
        head_index, hires_tokens, cross_all, view_term.reshape(tok_rows, cols), weights
    )


def solution(mesh):
    in_specs = (
        P("tok", None),
        P("tok", None),
        P(),
        P(None, "head"),
        P(None, None, "head"),
        P(None, None, "head"),
        P(None, "head", None),
        P("tok", None),
        P("tok"),
    )
    out_specs = P("tok", "head")
    body = functools.partial(shards, mesh.shape["head"], mesh.shape["tok"])
    return jax.shard_map(body, mesh=mesh, in_specs=in_specs, out_specs=out_specs, check_vma=False)
```

```python
import functools
import math

import jax
import jax.numpy as jnp
from jax import lax
from jax.experimental import pallas as pl
from jax.experimental.pallas import tpu as pltpu
from jax.sharding import PartitionSpec as P

HD = 128
VIEWS = 8
BLOCK = 128
LOG2_SCALE = math.log2(math.e) / math.sqrt(HD)
VMEM_BYTES = 60 * 1024 * 1024
CONTRACT_LAST = (((1,), (1,)), ((), ()))


def rms_rows(row_block, norm_gain):
    values = row_block.astype(jnp.float32)
    factor = lax.rsqrt(jnp.mean(values * values, axis=-1, keepdims=True) + 1e-06)
    return (values * factor * norm_gain).astype(jnp.bfloat16)


def f32_dot(left, right):
    return jnp.dot(left, right, preferred_element_type=jnp.float32)


def block_diagonal(tiles):
    rows = []
    for index, tile in enumerate(tiles):
        zero = jnp.zeros_like(tile)
        rows.append(
            jnp.concatenate([tile if k == index else zero for k in range(len(tiles))], axis=1)
        )
    return jnp.concatenate(rows, axis=0)


def ring_place(tok, n_tok):
    half = lax.div(tok, 2)
    return jnp.where(lax.rem(tok, 2) == 0, half, n_tok - 1 - half)


def cross_kernel(halves, lists_ref, counts_ref, tok_ref, tokens_ref, gain_ref, wq_ref, *refs):
    kv_refs, out_refs = refs[: -4 - halves], refs[-4 - halves : -4]
    k_ref, vt_ref, q_ref, mixed_ref = refs[-4:]
    step = pl.program_id(0)
    rows, cols = mixed_ref.shape
    heads = cols // HD
    per_step = rows // BLOCK
    listed = lists_ref.shape[1]

    @pl.when(step == 0)
    def _():
        n_tok = len(kv_refs)
        for offset, kv_ref in enumerate(kv_refs):
            chunk = kv_ref.shape[0]
            place = lax.rem(ring_place(tok_ref[0], n_tok) + offset, n_tok)
            home = jnp.where(place < (n_tok + 1) // 2, 2 * place, 2 * (n_tok - 1 - place) + 1)
            start = pl.multiple_of(home * chunk, BLOCK)
            k_ref[pl.ds(start, chunk), :] = kv_ref[:, :cols]
            vt_ref[:, pl.ds(start, chunk)] = kv_ref[:, cols:].T

    normed = rms_rows(tokens_ref[...], gain_ref[...])
    q_ref[...] = (f32_dot(normed, wq_ref[...]) * LOG2_SCALE).astype(jnp.bfloat16)

    def one_block(local, carry):
        block = step * per_step + local
        row_start = pl.multiple_of(local * BLOCK, BLOCK)
        count = counts_ref[block]
        first = lists_ref[block, 0]
        starts = [
            pl.multiple_of(jnp.where(j < count, lists_ref[block, j], first) * BLOCK, BLOCK)
            for j in range(listed)
        ]
        query = block_diagonal(
            [q_ref[pl.ds(row_start, BLOCK), h * HD : (h + 1) * HD] for h in range(heads)]
        )
        keys = jnp.concatenate([k_ref[pl.ds(s, BLOCK), :] for s in starts], axis=0)
        scores = lax.dot_general(keys, query, CONTRACT_LAST, preferred_element_type=jnp.float32)
        top = jnp.max(scores, axis=0, keepdims=True)
        weights = []
        total = jnp.zeros_like(top)
        for j in range(listed):
            shift = top + jnp.where(j < count, 0.0, 1e30)
            weight = jnp.exp2(scores[j * BLOCK : (j + 1) * BLOCK] - shift)
            total = total + jnp.sum(weight, axis=0, keepdims=True)
            weights.append(weight.astype(jnp.bfloat16))
        values_t = jnp.concatenate([vt_ref[:, pl.ds(s, BLOCK)] for s in starts], axis=1)
        mixed_t = f32_dot(values_t, jnp.concatenate(weights, axis=0)) / total
        for h in range(heads):
            part = slice(h * HD, (h + 1) * HD)
            mixed_ref[pl.ds(row_start, BLOCK), part] = mixed_t[part, part].T.astype(jnp.bfloat16)
        return carry

    lax.fori_loop(0, per_step, one_block, 0, unroll=True)
    half_steps = pl.num_programs(0) // halves
    for half, out_ref in enumerate(out_refs):
        @pl.when(lax.div(step, half_steps) == half)
        def _():
            out_ref[...] = mixed_ref[...]


def cross_attention(hires_tokens, gain, w_cross_q, kv_chunks, block_lists, block_counts):
    tok_index = lax.axis_index("tok").reshape(1)
    tok_rows, width = hires_tokens.shape
    cols = w_cross_q.shape[1]
    chunk = kv_chunks[0].shape[0]
    low_rows = chunk * len(kv_chunks)
    halves = 1
    rows = math.gcd(tok_rows // halves, 4 * BLOCK)
    half_steps = tok_rows // halves // rows
    return pl.pallas_call(
        functools.partial(cross_kernel, halves),
        out_shape=[jax.ShapeDtypeStruct((tok_rows // halves, cols), jnp.bfloat16)] * halves,
        grid_spec=pltpu.PrefetchScalarGridSpec(
            num_scalar_prefetch=3,
            grid=(tok_rows // rows,),
            in_specs=[
                pl.BlockSpec((rows, width), lambda i, *_: (i, 0)),
                pl.BlockSpec((1, width), lambda i, *_: (0, 0)),
                pl.BlockSpec((width, cols), lambda i, *_: (0, 0)),
            ]
            + [pl.BlockSpec((chunk, 2 * cols), lambda i, *_: (0, 0)) for _ in kv_chunks],
            out_specs=[
                pl.BlockSpec(
                    (rows, cols),
                    lambda i, *_, half=half: (jnp.clip(i - half * half_steps, 0, half_steps - 1), 0),
                )
                for half in range(halves)
            ],
            scratch_shapes=[
                pltpu.VMEM((low_rows, cols), jnp.bfloat16),
                pltpu.VMEM((cols, low_rows), jnp.bfloat16),
                pltpu.VMEM((rows, cols), jnp.bfloat16),
                pltpu.VMEM((rows, cols), jnp.bfloat16),
            ],
        ),
        compiler_params=pltpu.CompilerParams(vmem_limit_bytes=VMEM_BYTES),
        cost_estimate=pl.CostEstimate(
            flops=2 * tok_rows * cols * (width + 2 * block_lists.shape[1] * BLOCK * 2),
            bytes_accessed=2 * tok_rows * (width + cols),
            transcendentals=tok_rows * block_lists.shape[1] * BLOCK * (cols // HD),
        ),
        name="cross",
    )(block_lists, block_counts, tok_index, hires_tokens, gain, w_cross_q, *kv_chunks)


def view_kernel(tokens_ref, gain_ref, w_ref, wo_ref, out_ref, normed_ref, qkv_ref, mixed_ref):
    parts, sources, run, cols = out_ref.shape
    part_index = pl.program_id(0)
    heads = cols // HD
    rows = sources * run
    pixels = rows // VIEWS
    group = math.gcd(pixels, 32)
    tile = math.gcd(rows, 512)

    @pl.when(pl.program_id(0) == 0)
    def _():
        gain = gain_ref[...]
        step = math.gcd(sources, max(1, tile // run))
        for s in range(0, sources, step):
            tokens = tokens_ref[s : s + step].reshape(step * run, gain.shape[1])
            normed_ref[s * run : (s + step) * run] = rms_rows(tokens, gain)

    for start in range(0, rows, tile):
        stop = start + tile
        tokens = normed_ref[start:stop]
        for k in range(3):
            projected = f32_dot(tokens, w_ref[0, k])
            if k == 0:
                projected = projected * LOG2_SCALE
            qkv_ref[start:stop, k * cols : (k + 1) * cols] = projected.astype(jnp.bfloat16)
    size = VIEWS * group
    row_pixel = lax.broadcasted_iota(jnp.int32, (size, size), 0) % group
    col_pixel = lax.broadcasted_iota(jnp.int32, (size, size), 1) % group
    same = row_pixel == col_pixel

    def gathered(first, column):
        part = slice(column, column + HD)
        return jnp.concatenate(
            [qkv_ref[v * pixels + first : v * pixels + first + group, part] for v in range(VIEWS)],
            axis=0,
        )

    for first in range(0, pixels, group):
        for h in range(heads):
            query = gathered(first, h * HD)
            key = gathered(first, cols + h * HD)
            value = gathered(first, 2 * cols + h * HD)
            scores = lax.dot_general(query, key, CONTRACT_LAST, preferred_element_type=jnp.float32)
            scores = jnp.where(same, scores, -1e30)
            weight = jnp.exp2(scores - jnp.max(scores, axis=1, keepdims=True))
            value_and_one = jnp.concatenate([value, jnp.ones_like(value)], axis=1)
            mixed_and_total = f32_dot(weight.astype(jnp.bfloat16), value_and_one)
            mixed = (mixed_and_total[:, :HD] / mixed_and_total[:, HD:]).astype(jnp.bfloat16)
            for v in range(VIEWS):
                rows_of = slice(v * pixels + first, v * pixels + first + group)
                mixed_ref[part_index, rows_of, h * HD : (h + 1) * HD] = (
                    mixed[v * group : (v + 1) * group]
                )

    @pl.when(part_index == parts - 1)
    def _():
        step = math.gcd(sources, max(1, tile // run))
        for s in range(0, sources, step):
            rows_of = slice(s * run, (s + step) * run)
            for column in range(parts):
                w_rows = slice(column * cols, (column + 1) * cols)
                term = f32_dot(mixed_ref[0, rows_of], wo_ref[0, 0, w_rows])
                for g in range(1, parts):
                    term = term + f32_dot(mixed_ref[g, rows_of], wo_ref[g, 0, w_rows])
                out_ref[column, s : s + step] = term.astype(jnp.bfloat16).reshape(step, run, cols)


def view_attention(tokens, gain, weights):
    n_tok, run, width = tokens.shape
    parts, _, _, cols = weights.shape
    rows = n_tok * run
    return pl.pallas_call(
        view_kernel,
        out_shape=jax.ShapeDtypeStruct((parts, n_tok, run, cols), jnp.bfloat16),
        grid=(parts,),
        in_specs=[
            pl.BlockSpec((n_tok, run, width), lambda i: (0, 0, 0)),
            pl.BlockSpec((1, width), lambda i: (0, 0)),
            pl.BlockSpec((1, 3, width, cols), lambda i: (i, 0, 0, 0)),
            pl.BlockSpec((parts, 1, width, cols), lambda i: (0, 4, 0, 0)),
        ],
        out_specs=pl.BlockSpec((parts, n_tok, run, cols), lambda i: (0, 0, 0, 0)),
        scratch_shapes=[
            pltpu.VMEM((rows, width), jnp.bfloat16),
            pltpu.VMEM((rows, 3 * cols), jnp.bfloat16),
            pltpu.VMEM((parts, rows, cols), jnp.bfloat16),
        ],
        compiler_params=pltpu.CompilerParams(vmem_limit_bytes=VMEM_BYTES),
        cost_estimate=pl.CostEstimate(
            flops=2 * rows * (parts * cols * (3 * width + 512) + width * width),
            bytes_accessed=2 * (2 * rows * width + 4 * parts * width * cols),
            transcendentals=parts * rows * 512,
        ),
        name="view",
    )(tokens, gain, weights, weights)


def final_kernel(index_ref, tokens_ref, near_ref, far_ref, view_ref, w_ref, out_ref):
    total = tokens_ref[...].astype(jnp.float32) + view_ref[...].astype(jnp.float32)
    parity = lax.rem(index_ref[0], 2)
    for k in range(near_ref.shape[0]):
        total = total + f32_dot(near_ref[k], w_ref[2 * k + parity, 0])
        total = total + f32_dot(far_ref[k], w_ref[2 * k + 1 - parity, 0])
    out_ref[...] = total.astype(jnp.bfloat16)


def final_sum(head_index, hires_tokens, near, far, view_term, weights):
    half, tok_rows, cols = near.shape
    parts = weights.shape[0]
    rows = math.gcd(tok_rows, 512)
    own = pl.BlockSpec((rows, cols), lambda i, index: (i, 0))
    return pl.pallas_call(
        final_kernel,
        out_shape=jax.ShapeDtypeStruct((tok_rows, cols), jnp.bfloat16),
        grid_spec=pltpu.PrefetchScalarGridSpec(
            num_scalar_prefetch=1,
            grid=(tok_rows // rows,),
            in_specs=[
                pl.BlockSpec((rows, cols), lambda i, index: (i, index[0])),
                pl.BlockSpec((half, rows, cols), lambda i, index: (0, i, 0)),
                pl.BlockSpec((half, rows, cols), lambda i, index: (0, i, 0)),
                own,
                pl.BlockSpec((parts, 1, cols, cols), lambda i, index: (0, 3, index[0], 0)),
            ],
            out_specs=own,
        ),
        compiler_params=pltpu.CompilerParams(vmem_limit_bytes=VMEM_BYTES),
        cost_estimate=pl.CostEstimate(
            flops=2 * parts * tok_rows * cols * cols,
            bytes_accessed=2 * tok_rows * cols * (parts + 3),
            transcendentals=0,
        ),
        name="final",
    )(head_index.reshape(1), hires_tokens, near, far, view_term, weights)


def ring_chunks(own, n_tok):
    order = list(range(0, n_tok, 2)) + list(range(1, n_tok, 2))[::-1]
    upward = [(order[p], order[(p + 1) % n_tok]) for p in range(n_tok)]
    downward = [(order[p], order[p - 1]) for p in range(n_tok)]
    behind, ahead = [own], [own]
    for step in range(n_tok // 2):
        behind.append(lax.ppermute(behind[-1], "tok", upward))
        if step < (n_tok - 1) // 2:
            ahead.append(lax.ppermute(ahead[-1], "tok", downward))
    return ahead + behind[:0:-1]


def shards(
    n_head,
    n_tok,
    hires_tokens,
    lowres_tokens,
    norm_gain,
    w_cross_q,
    w_low_kv,
    w_view_qkv,
    w_out,
    block_lists,
    block_counts,
):
    tok_rows, width = hires_tokens.shape
    cols = w_cross_q.shape[1]
    quarter = tok_rows // n_head
    head_index = lax.axis_index("head")
    gain = norm_gain.reshape(1, width)

    run = quarter // n_tok

    own_weights = jnp.concatenate(
        [
            w_view_qkv.transpose(1, 0, 2),
            w_out.reshape(2, cols, n_head, cols).transpose(0, 2, 1, 3).reshape(2, width, cols),
        ],
        axis=0,
    )
    weights = lax.all_gather(own_weights, "head", axis=0, tiled=False)
    low_kv = f32_dot(
        rms_rows(lowres_tokens, norm_gain), w_low_kv.reshape(width, 2 * cols)
    ).astype(jnp.bfloat16)
    kv_chunks = ring_chunks(low_kv, n_tok)
    sent = lax.dynamic_slice_in_dim(hires_tokens, head_index * quarter, quarter, 0)
    kv_chunks, sent = lax.optimization_barrier((kv_chunks, sent))

    arrived = lax.all_to_all(
        sent.reshape(n_tok, run, width), "tok", split_axis=0, concat_axis=0, tiled=True
    )
    (cross_out,) = cross_attention(
        hires_tokens, gain, w_cross_q, kv_chunks, block_lists, block_counts
    )
    cross_out, arrived = lax.optimization_barrier((cross_out, arrived))
    same_parity = [list(range(p, n_head, 2)) for p in range(2)]
    near = lax.all_gather(
        cross_out, "head", axis=0, tiled=False, axis_index_groups=same_parity
    )
    term = view_attention(arrived, gain, weights)
    _, near = lax.optimization_barrier((term, near))
    far = lax.ppermute(near, "head", [(h, h ^ 1) for h in range(n_head)])
    view_term = lax.all_to_all(
        term.reshape(n_head * n_tok, run, cols),
        ("head", "tok"), split_axis=0, concat_axis=0, tiled=True,
    )
    return final_sum(
        head_index, hires_tokens, near, far, view_term.reshape(tok_rows, cols), weights
    )


def solution(mesh):
    in_specs = (
        P("tok", None),
        P("tok", None),
        P(),
        P(None, "head"),
        P(None, None, "head"),
        P(None, None, "head"),
        P(None, "head", None),
        P("tok", None),
        P("tok"),
    )
    out_specs = P("tok", "head")
    body = functools.partial(shards, mesh.shape["head"], mesh.shape["tok"])
    return jax.shard_map(body, mesh=mesh, in_specs=in_specs, out_specs=out_specs, check_vma=False)
```

```python
import functools
import math

import jax
import jax.numpy as jnp
from jax import lax
from jax.experimental import pallas as pl
from jax.experimental.pallas import tpu as pltpu
from jax.sharding import PartitionSpec as P

HD = 128
VIEWS = 8
BLOCK = 128
LOG2_SCALE = math.log2(math.e) / math.sqrt(HD)
VMEM_BYTES = 60 * 1024 * 1024
ROOM_VMEM_BYTES = 57 * 1024 * 1024
CONTRACT_LAST = (((1,), (1,)), ((), ()))


def rms_rows(row_block, norm_gain):
    values = row_block.astype(jnp.float32)
    factor = lax.rsqrt(jnp.mean(values * values, axis=-1, keepdims=True) + 1e-06)
    return (values * factor * norm_gain).astype(jnp.bfloat16)


def f32_dot(left, right):
    return jnp.dot(left, right, preferred_element_type=jnp.float32)


def block_diagonal(tiles):
    rows = []
    for index, tile in enumerate(tiles):
        zero = jnp.zeros_like(tile)
        rows.append(
            jnp.concatenate([tile if k == index else zero for k in range(len(tiles))], axis=1)
        )
    return jnp.concatenate(rows, axis=0)


def ring_place(tok, n_tok):
    half = lax.div(tok, 2)
    return jnp.where(lax.rem(tok, 2) == 0, half, n_tok - 1 - half)


def cross_kernel(halves, lists_ref, counts_ref, tok_ref, tokens_ref, gain_ref, wq_ref, *refs):
    kv_refs, out_refs = refs[: -4 - halves], refs[-4 - halves : -4]
    k_ref, vt_ref, q_ref, mixed_ref = refs[-4:]
    step = pl.program_id(0)
    rows, cols = mixed_ref.shape
    heads = cols // HD
    per_step = rows // BLOCK
    listed = lists_ref.shape[1]

    @pl.when(step == 0)
    def _():
        n_tok = len(kv_refs)
        for offset, kv_ref in enumerate(kv_refs):
            chunk = kv_ref.shape[0]
            place = lax.rem(ring_place(tok_ref[0], n_tok) + offset, n_tok)
            home = jnp.where(place < (n_tok + 1) // 2, 2 * place, 2 * (n_tok - 1 - place) + 1)
            start = pl.multiple_of(home * chunk, BLOCK)
            k_ref[pl.ds(start, chunk), :] = kv_ref[:, :cols]
            vt_ref[:, pl.ds(start, chunk)] = kv_ref[:, cols:].T

    normed = rms_rows(tokens_ref[...], gain_ref[...])
    q_ref[...] = (f32_dot(normed, wq_ref[...]) * LOG2_SCALE).astype(jnp.bfloat16)

    def one_block(local, carry):
        block = step * per_step + local
        row_start = pl.multiple_of(local * BLOCK, BLOCK)
        count = counts_ref[block]
        first = lists_ref[block, 0]
        starts = [
            pl.multiple_of(jnp.where(j < count, lists_ref[block, j], first) * BLOCK, BLOCK)
            for j in range(listed)
        ]
        query = block_diagonal(
            [q_ref[pl.ds(row_start, BLOCK), h * HD : (h + 1) * HD] for h in range(heads)]
        )
        keys = jnp.concatenate([k_ref[pl.ds(s, BLOCK), :] for s in starts], axis=0)
        scores = lax.dot_general(keys, query, CONTRACT_LAST, preferred_element_type=jnp.float32)
        top = jnp.max(scores, axis=0, keepdims=True)
        weights = []
        total = jnp.zeros_like(top)
        for j in range(listed):
            shift = top + jnp.where(j < count, 0.0, 1e30)
            weight = jnp.exp2(scores[j * BLOCK : (j + 1) * BLOCK] - shift)
            total = total + jnp.sum(weight, axis=0, keepdims=True)
            weights.append(weight.astype(jnp.bfloat16))
        values_t = jnp.concatenate([vt_ref[:, pl.ds(s, BLOCK)] for s in starts], axis=1)
        mixed_t = f32_dot(values_t, jnp.concatenate(weights, axis=0)) / total
        for h in range(heads):
            part = slice(h * HD, (h + 1) * HD)
            mixed_ref[pl.ds(row_start, BLOCK), part] = mixed_t[part, part].T.astype(jnp.bfloat16)
        return carry

    lax.fori_loop(0, per_step, one_block, 0, unroll=True)
    half_steps = pl.num_programs(0) // halves
    for half, out_ref in enumerate(out_refs):
        @pl.when(lax.div(step, half_steps) == half)
        def _():
            out_ref[...] = mixed_ref[...]


def cross_attention(hires_tokens, gain, w_cross_q, kv_chunks, block_lists, block_counts):
    tok_index = lax.axis_index("tok").reshape(1)
    tok_rows, width = hires_tokens.shape
    cols = w_cross_q.shape[1]
    chunk = kv_chunks[0].shape[0]
    low_rows = chunk * len(kv_chunks)
    halves = 1
    rows = math.gcd(tok_rows // halves, 4 * BLOCK)
    half_steps = tok_rows // halves // rows
    return pl.pallas_call(
        functools.partial(cross_kernel, halves),
        out_shape=[jax.ShapeDtypeStruct((tok_rows // halves, cols), jnp.bfloat16)] * halves,
        grid_spec=pltpu.PrefetchScalarGridSpec(
            num_scalar_prefetch=3,
            grid=(tok_rows // rows,),
            in_specs=[
                pl.BlockSpec((rows, width), lambda i, *_: (i, 0)),
                pl.BlockSpec((1, width), lambda i, *_: (0, 0)),
                pl.BlockSpec((width, cols), lambda i, *_: (0, 0)),
            ]
            + [pl.BlockSpec((chunk, 2 * cols), lambda i, *_: (0, 0)) for _ in kv_chunks],
            out_specs=[
                pl.BlockSpec(
                    (rows, cols),
                    lambda i, *_, half=half: (jnp.clip(i - half * half_steps, 0, half_steps - 1), 0),
                )
                for half in range(halves)
            ],
            scratch_shapes=[
                pltpu.VMEM((low_rows, cols), jnp.bfloat16),
                pltpu.VMEM((cols, low_rows), jnp.bfloat16),
                pltpu.VMEM((rows, cols), jnp.bfloat16),
                pltpu.VMEM((rows, cols), jnp.bfloat16),
            ],
        ),
        compiler_params=pltpu.CompilerParams(vmem_limit_bytes=VMEM_BYTES),
        cost_estimate=pl.CostEstimate(
            flops=2 * tok_rows * cols * (width + 2 * block_lists.shape[1] * BLOCK * 2),
            bytes_accessed=2 * tok_rows * (width + cols),
            transcendentals=tok_rows * block_lists.shape[1] * BLOCK * (cols // HD),
        ),
        name="cross",
    )(block_lists, block_counts, tok_index, hires_tokens, gain, w_cross_q, *kv_chunks)


def view_kernel(tokens_ref, gain_ref, w_ref, wo_ref, out_ref, normed_ref, qkv_ref, mixed_ref):
    parts, sources, run, cols = out_ref.shape
    part_index = pl.program_id(0)
    heads = cols // HD
    rows = sources * run
    pixels = rows // VIEWS
    group = math.gcd(pixels, 32)
    tile = math.gcd(rows, 512)

    @pl.when(pl.program_id(0) == 0)
    def _():
        gain = gain_ref[...]
        step = math.gcd(sources, max(1, tile // run))
        for s in range(0, sources, step):
            tokens = tokens_ref[s : s + step].reshape(step * run, gain.shape[1])
            normed_ref[s * run : (s + step) * run] = rms_rows(tokens, gain)

    for start in range(0, rows, tile):
        stop = start + tile
        tokens = normed_ref[start:stop]
        for k in range(3):
            projected = f32_dot(tokens, w_ref[0, k])
            if k == 0:
                projected = projected * LOG2_SCALE
            qkv_ref[start:stop, k * cols : (k + 1) * cols] = projected.astype(jnp.bfloat16)
    size = VIEWS * group
    row_pixel = lax.broadcasted_iota(jnp.int32, (size, size), 0) % group
    col_pixel = lax.broadcasted_iota(jnp.int32, (size, size), 1) % group
    same = row_pixel == col_pixel

    def gathered(first, column):
        part = slice(column, column + HD)
        return jnp.concatenate(
            [qkv_ref[v * pixels + first : v * pixels + first + group, part] for v in range(VIEWS)],
            axis=0,
        )

    for first in range(0, pixels, group):
        for h in range(heads):
            query = gathered(first, h * HD)
            key = gathered(first, cols + h * HD)
            value = gathered(first, 2 * cols + h * HD)
            scores = lax.dot_general(query, key, CONTRACT_LAST, preferred_element_type=jnp.float32)
            scores = jnp.where(same, scores, -1e30)
            weight = jnp.exp2(scores - jnp.max(scores, axis=1, keepdims=True))
            value_and_one = jnp.concatenate([value, jnp.ones_like(value)], axis=1)
            mixed_and_total = f32_dot(weight.astype(jnp.bfloat16), value_and_one)
            mixed = (mixed_and_total[:, :HD] / mixed_and_total[:, HD:]).astype(jnp.bfloat16)
            for v in range(VIEWS):
                rows_of = slice(v * pixels + first, v * pixels + first + group)
                mixed_ref[part_index, rows_of, h * HD : (h + 1) * HD] = (
                    mixed[v * group : (v + 1) * group]
                )

    @pl.when(part_index == parts - 1)
    def _():
        step = math.gcd(sources, max(1, tile // run))
        for s in range(0, sources, step):
            rows_of = slice(s * run, (s + step) * run)
            for column in range(parts):
                w_rows = slice(column * cols, (column + 1) * cols)
                term = f32_dot(mixed_ref[0, rows_of], wo_ref[0, 0, w_rows])
                for g in range(1, parts):
                    term = term + f32_dot(mixed_ref[g, rows_of], wo_ref[g, 0, w_rows])
                out_ref[column, s : s + step] = term.astype(jnp.bfloat16).reshape(step, run, cols)


def view_attention(tokens, gain, weights):
    n_tok, run, width = tokens.shape
    parts, _, _, cols = weights.shape
    rows = n_tok * run
    return pl.pallas_call(
        view_kernel,
        out_shape=jax.ShapeDtypeStruct((parts, n_tok, run, cols), jnp.bfloat16),
        grid=(parts,),
        in_specs=[
            pl.BlockSpec((n_tok, run, width), lambda i: (0, 0, 0)),
            pl.BlockSpec((1, width), lambda i: (0, 0)),
            pl.BlockSpec((1, 3, width, cols), lambda i: (i, 0, 0, 0)),
            pl.BlockSpec((parts, 1, width, cols), lambda i: (0, 4, 0, 0)),
        ],
        out_specs=pl.BlockSpec((parts, n_tok, run, cols), lambda i: (0, 0, 0, 0)),
        scratch_shapes=[
            pltpu.VMEM((rows, width), jnp.bfloat16),
            pltpu.VMEM((rows, 3 * cols), jnp.bfloat16),
            pltpu.VMEM((parts, rows, cols), jnp.bfloat16),
        ],
        compiler_params=pltpu.CompilerParams(vmem_limit_bytes=ROOM_VMEM_BYTES),
        cost_estimate=pl.CostEstimate(
            flops=2 * rows * (parts * cols * (3 * width + 512) + width * width),
            bytes_accessed=2 * (2 * rows * width + 4 * parts * width * cols),
            transcendentals=parts * rows * 512,
        ),
        name="view",
    )(tokens, gain, weights, weights)


def final_kernel(index_ref, tokens_ref, cross_ref, view_ref, w_ref, out_ref):
    total = tokens_ref[...].astype(jnp.float32) + view_ref[...].astype(jnp.float32)
    for g in range(cross_ref.shape[0]):
        total = total + f32_dot(cross_ref[g], w_ref[g, 0])
    out_ref[...] = total.astype(jnp.bfloat16)


def final_sum(head_index, hires_tokens, cross_all, view_term, weights):
    parts, tok_rows, cols = cross_all.shape
    rows = math.gcd(tok_rows, 512)
    own = pl.BlockSpec((rows, cols), lambda i, index: (i, 0))
    return pl.pallas_call(
        final_kernel,
        out_shape=jax.ShapeDtypeStruct((tok_rows, cols), jnp.bfloat16),
        grid_spec=pltpu.PrefetchScalarGridSpec(
            num_scalar_prefetch=1,
            grid=(tok_rows // rows,),
            in_specs=[
                pl.BlockSpec((rows, cols), lambda i, index: (i, index[0])),
                pl.BlockSpec((parts, rows, cols), lambda i, index: (0, i, 0)),
                own,
                pl.BlockSpec((parts, 1, cols, cols), lambda i, index: (0, 3, index[0], 0)),
            ],
            out_specs=own,
        ),
        compiler_params=pltpu.CompilerParams(vmem_limit_bytes=ROOM_VMEM_BYTES),
        cost_estimate=pl.CostEstimate(
            flops=2 * parts * tok_rows * cols * cols,
            bytes_accessed=2 * tok_rows * cols * (parts + 3),
            transcendentals=0,
        ),
        name="final",
    )(head_index.reshape(1), hires_tokens, cross_all, view_term, weights)


def ring_chunks(own, n_tok):
    order = list(range(0, n_tok, 2)) + list(range(1, n_tok, 2))[::-1]
    upward = [(order[p], order[(p + 1) % n_tok]) for p in range(n_tok)]
    downward = [(order[p], order[p - 1]) for p in range(n_tok)]
    behind, ahead = [own], [own]
    for step in range(n_tok // 2):
        behind.append(lax.ppermute(behind[-1], "tok", upward))
        if step < (n_tok - 1) // 2:
            ahead.append(lax.ppermute(ahead[-1], "tok", downward))
    return ahead + behind[:0:-1]


def shards(
    n_head,
    n_tok,
    hires_tokens,
    lowres_tokens,
    norm_gain,
    w_cross_q,
    w_low_kv,
    w_view_qkv,
    w_out,
    block_lists,
    block_counts,
):
    tok_rows, width = hires_tokens.shape
    cols = w_cross_q.shape[1]
    quarter = tok_rows // n_head
    head_index = lax.axis_index("head")
    gain = norm_gain.reshape(1, width)

    run = quarter // n_tok

    low_kv = f32_dot(
        rms_rows(lowres_tokens, norm_gain), w_low_kv.reshape(width, 2 * cols)
    ).astype(jnp.bfloat16)
    low_kv, w_view_qkv, w_out = lax.optimization_barrier((low_kv, w_view_qkv, w_out))
    own_weights = jnp.concatenate(
        [
            w_view_qkv.transpose(1, 0, 2),
            w_out.reshape(2, cols, n_head, cols).transpose(0, 2, 1, 3).reshape(2, width, cols),
        ],
        axis=0,
    )
    weights = lax.all_gather(own_weights, "head", axis=0, tiled=False)
    kv_chunks = ring_chunks(low_kv, n_tok)
    sent = lax.dynamic_slice_in_dim(hires_tokens, head_index * quarter, quarter, 0)
    kv_chunks, sent = lax.optimization_barrier((kv_chunks, sent))

    arrived = lax.all_to_all(
        sent.reshape(n_tok, run, width), "tok", split_axis=0, concat_axis=0, tiled=True
    )
    (cross_out,) = cross_attention(
        hires_tokens, gain, w_cross_q, kv_chunks, block_lists, block_counts
    )
    cross_out, arrived = lax.optimization_barrier((cross_out, arrived))
    cross_all = lax.all_gather(cross_out, "head", axis=0, tiled=False)
    view_term = lax.all_to_all(
        view_attention(arrived, gain, weights).reshape(n_head * n_tok, run, cols),
        ("head", "tok"), split_axis=0, concat_axis=0, tiled=True,
    )
    return final_sum(
        head_index, hires_tokens, cross_all, view_term.reshape(tok_rows, cols), weights
    )


def solution(mesh):
    in_specs = (
        P("tok", None),
        P("tok", None),
        P(),
        P(None, "head"),
        P(None, None, "head"),
        P(None, None, "head"),
        P(None, "head", None),
        P("tok", None),
        P("tok"),
    )
    out_specs = P("tok", "head")
    body = functools.partial(shards, mesh.shape["head"], mesh.shape["tok"])
    return jax.shard_map(body, mesh=mesh, in_specs=in_specs, out_specs=out_specs, check_vma=False)
```
